32 devices in a mesh: groups: 2 (over x), row: 16 (over z, y, core).
Axes of the slice: x: 2, y: 2, z: 4, core: 2. Of those that a mesh axis runs over, the one named last changes fastest.
Arguments:
- weight: bfloat16 [106496, 8192], P(('groups', 'row')), parts along dimension 0, may hold values from -18 to 18
- test_matrix: bfloat16 [53248, 240], P('row'), may hold values from -6 to 6
- rank_mask: int32 [480], P('groups'), parts along dimension 0, may hold values from 0 to 1, as said below
Outputs:
- left_factor: float32 [16384, 224], P(('groups', 'row')), parts along dimension 0
- right_factor: bfloat16 [106496, 224], P(('groups', 'row')), parts along dimension 0
- spread: float32 [2], P('groups'), parts along dimension 0
The draws below stay inside these ranges and needn't reach their ends.
There are 2 independent parts, one for each index of `groups`. The reference program is written for one: setup_inputs(seed, part) draws one part's arguments, and reference() takes and returns one part's arrays. A program takes and returns all parts, laid end to end along the dimension named above; an argument that names none is the same for every part. Nothing has to cross between parts.
Inputs may be any that keep to these rules, and one draw needn't show every extreme that they name: `rank_mask`: exactly 224 entries are 1, the others 0.
All inputs are finite; a program needn't handle non-finite values.
Results may differ from the reference program's by a relative error of at most 0.0055.
Values may be sent and summed in bfloat16 or wider, within the bound.
No kernel may reach another device: no remote copies, remote signals or barrier semaphores. Data moves between devices by JAX's collectives and lax.ppermute only.
A program may use at most 192 MiB of HBM per device.

```python
import math
import jax
import jax.numpy as jnp
from jax import lax

D = 8192
FF = 53248
SKETCH = 240
RANK = 224


def draw_weight(key, part):
    key = jax.random.fold_in(key, 11)
    value_key, scale_key = jax.random.split(key)
    place = jnp.arange(FF, dtype=jnp.float32)[:, None] / FF
    jitter = jax.random.uniform(scale_key, (FF, 1), jnp.float32)
    values = jnp.clip(jax.random.normal(value_key, (FF, D), jnp.float32), -6.0, 6.0)
    row_scale = 0.1 * jnp.exp(math.log(3.0) * place + math.log(10.0) * jitter)
    return (values * row_scale).astype(jnp.bfloat16)


def draw_rank_mask(key, part):
    key = jax.random.fold_in(key, 5)
    ordering = jax.random.permutation(key, SKETCH)
    return (ordering < RANK).astype(jnp.int32)


def levels(key, extent, pieces, least, high):
    factor_of, own = 1.0, jax.random.fold_in(key, 6)
    for dim, blocks in pieces:
        heights = jnp.exp(jax.random.uniform(jax.random.fold_in(own, dim), (blocks,), jnp.float32, least / len(pieces), high / len(pieces)))
        factor_of = factor_of * jnp.repeat(heights, extent[dim] // blocks).reshape([-1 if axis == dim else 1 for axis in range(len(extent))])
    return factor_of


def bell_draw(stream_key, extent, width, most, cuts=(), kind=jnp.bfloat16):
    level = levels(stream_key, extent, cuts, -0.22, 0.18) if cuts else 1.0
    entries = jax.random.normal(stream_key, extent, jnp.float32) * width * level
    return jnp.minimum(jnp.maximum(entries, -most), most).astype(kind)


def setup_inputs(seed: int = 0, part: int = 0) -> dict:
    key_list = jax.random.split(jax.random.key(seed), 4)
    own_keys = jax.random.split(jax.random.fold_in(key_list[3], part), 4)
    return {
        "weight": draw_weight(jax.random.fold_in(jax.random.fold_in(key_list[3], part), 71), part),
        "test_matrix": bell_draw(key_list[1], (FF, SKETCH), 1.0, 6.0, ((0, 16),)),
        "rank_mask": draw_rank_mask(jax.random.fold_in(jax.random.fold_in(key_list[3], part), 71), part),
    }


def selector(rank_mask, kept):
    positions = (jnp.cumsum(rank_mask) - 1).astype(jnp.int32)
    targets = lax.iota(jnp.int32, kept)
    matches = (rank_mask[:, None] == 1) & (positions[:, None] == targets[None, :])
    return matches.astype(jnp.float32)

def reference(weight, test_matrix, rank_mask):
    across = (((0,), (0,)), ((), ()))
    sketch = lax.dot_general(weight.astype(jnp.float32), test_matrix.astype(jnp.float32), across, preferred_element_type=jnp.float32).astype(jnp.bfloat16)
    mixed = jnp.dot(weight.astype(jnp.float32), sketch.astype(jnp.float32), preferred_element_type=jnp.float32).astype(jnp.bfloat16)
    powered = lax.dot_general(weight.astype(jnp.float32), mixed.astype(jnp.float32), across, preferred_element_type=jnp.float32)
    gram_matrix = lax.dot_general(powered, powered, across, precision=lax.Precision.HIGHEST)
    cholesky_factor = jnp.linalg.cholesky(gram_matrix)
    ortho_basis = lax.linalg.triangular_solve(cholesky_factor, powered, left_side=False, lower=True, transpose_a=True)
    chosen = jnp.dot(ortho_basis, selector(rank_mask, RANK), precision=lax.Precision.HIGHEST)
    left_factor = chosen * math.sqrt(D)
    chosen_b = chosen.astype(jnp.bfloat16)
    projected = jnp.dot(weight.astype(jnp.float32), chosen_b.astype(jnp.float32), preferred_element_type=jnp.float32)
    energy = jnp.sum(projected * projected)
    spread = jnp.sqrt(energy / (FF * RANK) + 1e-06)
    right_factor = (projected / spread).astype(jnp.bfloat16)
    return (left_factor, right_factor, spread.reshape(1))
```

```python
import functools
import math

import jax
import jax.numpy as jnp
import numpy as np
from jax import lax
from jax.experimental import pallas as pl
from jax.experimental.pallas import tpu as pltpu
from jax.sharding import PartitionSpec as P

RANK = 224
MIB = 1024 * 1024


def selector(rank_mask, kept):
    positions = jnp.cumsum(rank_mask) - 1
    targets = lax.iota(jnp.int32, kept)
    matches = (rank_mask[:, None] == 1) & (positions[:, None] == targets[None, :])
    return matches.astype(jnp.float32)


def plain_body(weight, test_matrix, rank_mask):
    across = (((0,), (0,)), ((), ()))
    members = lax.axis_size("row")
    picker = selector(rank_mask, RANK)
    sketch_part = lax.psum_scatter(
        lax.dot_general(weight, test_matrix, across, preferred_element_type=jnp.float32),
        "row",
        scatter_dimension=0,
        tiled=True,
    ).astype(jnp.bfloat16)

    def add_rows(piece_rows):
        return jnp.dot(weight, piece_rows, preferred_element_type=jnp.float32)

    mixed = add_rows(lax.all_gather(sketch_part, "row", axis=0, tiled=True)).astype(jnp.bfloat16)
    powered = lax.psum_scatter(
        lax.dot_general(weight, mixed, across, preferred_element_type=jnp.float32),
        "row",
        scatter_dimension=0,
        tiled=True,
    )
    local_gram = lax.dot_general(powered, powered, across, precision=lax.Precision.HIGHEST)
    gram_matrix = lax.psum(local_gram, "row")
    cholesky_factor = jnp.linalg.cholesky(gram_matrix)
    ortho_basis = lax.linalg.triangular_solve(
        cholesky_factor, powered, left_side=False, lower=True, transpose_a=True
    )
    own_chosen = jnp.dot(ortho_basis, picker, precision=lax.Precision.HIGHEST)
    projected = add_rows(lax.all_gather(own_chosen.astype(jnp.bfloat16), "row", axis=0, tiled=True))
    left_factor = own_chosen * math.sqrt(weight.shape[1])
    energy = lax.psum(jnp.sum(projected * projected), "row")
    spread = jnp.sqrt(energy / (weight.shape[0] * members * RANK) + 1e-06)
    right_factor = (projected / spread).astype(jnp.bfloat16)
    return (left_factor, right_factor, spread.reshape(1))


class Ring:
    def __init__(self, members):
        chips = members // 2
        order = list(range(0, chips, 2)) + list(range(chips - 1, 0, -2))
        place = {chip: at for at, chip in enumerate(order)}
        self.chips, self.far = chips, chips // 2
        self.pair = [(device, device ^ 1) for device in range(members)]
        self.ahead = []
        for at, chip in enumerate(order):
            self.ahead.append((2 * chip, 2 * order[(at + 1) % chips]))
            self.ahead.append((2 * chip + 1, 2 * order[at - 1] + 1))

        def halves(device, steps, core):
            at = place[device // 2] + (steps if device % 2 == 0 else -steps)
            chip = order[at % chips]
            return [2 * chip + core, 2 * chip + 1 - core]

        self.width, self.table = {}, []
        for device in range(members):
            core, row = device % 2, []

            def put(name, values):
                self.width[name] = (len(row), len(values))
                row.extend(values)

            for k in range(self.far + 1):
                one = k == self.far
                mine, other = halves(device, k, core), halves(device, -k, 1 - core)
                put(("sum", k), mine if k == 0 else (mine[:1] + other[:1] if one else mine + other))
                mine, other = halves(device, -k, core), halves(device, k, 1 - core)
                put(("use", k), mine if k == 0 else (mine[:1] + other[:1] if one else mine + other))
            arrival = [device // 2]
            for k in range(1, self.far):
                arrival += [halves(device, -k, core)[0] // 2, halves(device, k, core)[0] // 2]
            arrival.append(halves(device, self.far, core)[0] // 2)
            put("arrival", [arrival.index(chip) for chip in range(chips)])
            self.table.append(row)

    def row(self):
        table = jnp.asarray(np.array(self.table, np.int32))
        row = lax.dynamic_index_in_dim(table, lax.axis_index("row"), 0, keepdims=False)
        return {name: row[at : at + size] for name, (at, size) in self.width.items()}


def columns_kernel(kept, ids_ref, left_ref, weight_ref, keep_ref, *give):
    step = pl.program_id(0)
    part = jnp.dot(left_ref[...], weight_ref[...], preferred_element_type=jnp.float32)
    if not give:
        keep_ref[...] = part
        return

    @pl.when(step < kept)
    def _():
        keep_ref[...] = part

    @pl.when(step >= kept)
    def _():
        give[0][...] = part.astype(jnp.bfloat16)


def column_sums(left, weight, halves, half, split):
    rows, wide = left.shape[1], left.shape[0]
    block = min(256, half)
    per = half // block
    ids = (halves[:, None] * per + jnp.arange(per, dtype=jnp.int32)[None, :]).reshape(-1)
    steps = ids.shape[0]
    kept = steps // 2 if split else steps
    out_shape = [jax.ShapeDtypeStruct((wide, kept * block), jnp.float32)]
    out_specs = [pl.BlockSpec((wide, block), lambda j, ids: (0, jnp.minimum(j, kept - 1)))]
    if split:
        out_shape.append(jax.ShapeDtypeStruct((wide, kept * block), jnp.bfloat16))
        out_specs.append(pl.BlockSpec((wide, block), lambda j, ids: (0, jnp.maximum(j - kept, 0))))
    return pl.pallas_call(
        functools.partial(columns_kernel, kept),
        out_shape=out_shape,
        grid_spec=pltpu.PrefetchScalarGridSpec(
            num_scalar_prefetch=1,
            grid=(steps,),
            in_specs=[
                pl.BlockSpec((wide, rows), lambda j, ids: (0, 0)),
                pl.BlockSpec((rows, block), lambda j, ids: (0, ids[j])),
            ],
            out_specs=out_specs,
        ),
        compiler_params=pltpu.CompilerParams(
            dimension_semantics=("arbitrary",), vmem_limit_bytes=32 * MIB
        ),
        cost_estimate=pl.CostEstimate(
            flops=2 * wide * rows * steps * block,
            bytes_accessed=2 * rows * steps * block + 2 * rows * wide,
            transcendentals=0,
        ),
    )(ids, left, weight)


def rows_kernel(pieces, halves, chained, turned, with_gram, *refs):
    refs = list(refs[1:])
    weight_ref = refs.pop(0)
    piece_refs = [refs.pop(0) for _ in range(pieces)]
    before_ref = refs.pop(0) if chained else None
    out_ref = refs.pop(0)
    gram_ref = refs.pop(0) if with_gram else None
    total_ref = refs.pop(0) if turned else out_ref
    block, step = pl.program_id(0), pl.program_id(1)
    steps = pieces * halves
    piece = piece_refs[0][...]
    if pieces == 2:
        piece = jnp.where(step < halves, piece, piece_refs[1][...])
    onto = (((1,), (1,)), ((), ()))
    part = lax.dot_general(weight_ref[...], piece, onto, preferred_element_type=jnp.float32)

    @pl.when(step == 0)
    def _():
        total_ref[...] = before_ref[...] + part if chained else part

    @pl.when(step > 0)
    def _():
        total_ref[...] += part

    if turned:

        @pl.when(step == steps - 1)
        def _():
            out_ref[...] = total_ref[...].T.astype(jnp.bfloat16)

    if with_gram:
        slots = gram_ref.shape[0]
        run = steps // slots

        @pl.when(block == 0)
        def _():
            square = lax.dot_general(piece, piece, onto, preferred_element_type=jnp.float32)
            slot = step // run

            @pl.when(step % run == 0)
            def _():
                gram_ref[slot] = square

            @pl.when(step % run > 0)
            def _():
                gram_ref[slot] += square


def row_products(weight, pieces, ids, half, before, turned, with_gram):
    rows, wide = weight.shape[0], pieces[0].shape[0]
    halves = pieces[0].shape[1] // half
    steps = len(pieces) * halves
    tall = rows // 2 if rows % 256 == 0 else rows

    def piece_spec(at):
        low = at * halves
        return pl.BlockSpec((wide, half), lambda i, j, ids: (0, jnp.clip(j - low, 0, halves - 1)))

    in_specs = [pl.BlockSpec((tall, half), lambda i, j, ids: (i, ids[j]))]
    in_specs += [piece_spec(at) for at in range(len(pieces))]
    operands = [weight, *pieces]
    if before is not None:
        in_specs.append(pl.BlockSpec((tall, wide), lambda i, j, ids: (i, 0)))
        operands.append(before)
    if turned:
        out_shape = [jax.ShapeDtypeStruct((wide, rows), jnp.bfloat16)]
        out_specs = [pl.BlockSpec((wide, tall), lambda i, j, ids: (0, i))]
    else:
        out_shape = [jax.ShapeDtypeStruct((rows, wide), jnp.float32)]
        out_specs = [pl.BlockSpec((tall, wide), lambda i, j, ids: (i, 0))]
    if with_gram:
        slots = max(1, steps // 2)
        out_shape.append(jax.ShapeDtypeStruct((slots, wide, wide), jnp.float32))
        out_specs.append(pl.BlockSpec((slots, wide, wide), lambda i, j, ids: (0, 0, 0)))
    return pl.pallas_call(
        functools.partial(rows_kernel, len(pieces), halves, before is not None, turned, with_gram),
        out_shape=out_shape,
        grid_spec=pltpu.PrefetchScalarGridSpec(
            num_scalar_prefetch=1,
            grid=(rows // tall, steps),
            in_specs=in_specs,
            out_specs=out_specs,
            scratch_shapes=[pltpu.VMEM((tall, wide), jnp.float32)] if turned else [],
        ),
        input_output_aliases={len(operands): 0} if before is not None and not turned else {},
        compiler_params=pltpu.CompilerParams(
            dimension_semantics=("arbitrary", "arbitrary"), vmem_limit_bytes=40 * MIB
        ),
        cost_estimate=pl.CostEstimate(
            flops=2 * rows * wide * steps * half,
            bytes_accessed=2 * rows * steps * half + 8 * rows * wide,
            transcendentals=0,
        ),
    )(ids, *operands)


def ring_sum(ring, ids, left, weight, half):
    got = None
    for k in range(ring.far, 0, -1):
        keep, give = column_sums(left, weight, ids["sum", k], half, True)
        total = keep + lax.ppermute(give, "row", ring.pair).astype(jnp.float32)
        if got is not None:
            got = got.astype(jnp.float32)
            size = got.shape[1]
            if size < total.shape[1]:
                total = jnp.concatenate([total[:, :size] + got, total[:, size:]], 1)
            else:
                total = total + got
        got = lax.ppermute(total.astype(jnp.bfloat16), "row", ring.ahead)
    (keep,) = column_sums(left, weight, ids["sum", 0], half, False)
    mine = keep + got.astype(jnp.float32)
    other = lax.ppermute(mine, "row", ring.pair)
    return mine + jnp.concatenate([other[:, half:], other[:, :half]], 1)


def ring_apply(ring, ids, chunk, weight, half, turned, with_gram):
    grams, before = [], None
    moving = chunk
    for k in range(ring.far + 1):
        if k == 0:
            pieces = [chunk]
        else:
            moving = lax.ppermute(moving if k < ring.far else moving[:, :half], "row", ring.ahead)
            pieces = [moving, lax.ppermute(moving, "row", ring.pair)]
        last = k == ring.far
        before, *gram = row_products(
            weight, pieces, ids["use", k], half, before, turned and last, with_gram
        )
        grams += gram
    return before, grams


def group_sum(value, ring):
    rows = value.shape[0] // 2
    first = lax.axis_index("row") % 2 == 0
    low, high = value[:rows], value[rows:]
    part = jnp.where(first, low, high)
    part = part + lax.ppermute(jnp.where(first, high, low), "row", ring.pair)
    hop = 2
    while hop < 2 * ring.chips:
        swap = [(device, device ^ hop) for device in range(2 * ring.chips)]
        part = part + lax.ppermute(part, "row", swap)
        hop *= 2
    other = lax.ppermute(part, "row", ring.pair)
    return jnp.concatenate([jnp.where(first, part, other), jnp.where(first, other, part)], 0)


def ring_body(ring, weight, test_matrix, rank_mask):
    highest = lax.Precision.HIGHEST
    rows, features = weight.shape
    half = features // (2 * ring.chips)
    ids = ring.row()
    picker = selector(rank_mask, RANK)
    sketch = ring_sum(ring, ids, test_matrix.T, weight, half).astype(jnp.bfloat16)
    mixed, _ = ring_apply(ring, ids, sketch, weight, half, True, False)
    powered = ring_sum(ring, ids, mixed, weight, half)
    image, grams = ring_apply(
        ring, ids, powered.astype(jnp.bfloat16), weight, half, False, True
    )
    image_b = image.astype(jnp.bfloat16)
    square = lax.dot_general(
        image_b, image_b, (((0,), (0,)), ((), ())), preferred_element_type=jnp.float32
    )
    square = group_sum(square, ring)
    stack = jnp.concatenate(grams, 0)
    gram_matrix = sum(
        lax.dynamic_index_in_dim(stack, ids["arrival"][chip], 0, keepdims=False)
        for chip in range(ring.chips)
    )
    cholesky_factor = jnp.linalg.cholesky(gram_matrix)
    inverse = lax.linalg.triangular_solve(
        cholesky_factor,
        jnp.eye(gram_matrix.shape[0], dtype=jnp.float32),
        left_side=False,
        lower=True,
        transpose_a=True,
    )
    change = jnp.dot(inverse, picker, precision=highest)
    own = powered[:, :half]
    left_factor = lax.dot_general(
        own, change, (((0,), (0,)), ((), ())), precision=highest
    ) * math.sqrt(features)
    energy = jnp.sum(square * jnp.dot(change, change.T, precision=highest))
    spread = jnp.sqrt(energy / (rows * 2 * ring.chips * RANK) + 1e-06)
    right_factor = (jnp.dot(image, change, precision=highest) / spread).astype(jnp.bfloat16)
    return (left_factor, right_factor, spread.reshape(1))


def body(weight, test_matrix, rank_mask):
    members = lax.axis_size("row")
    chips = members // 2
    paired = members % 2 == 0 and chips > 2 and chips & (chips - 1) == 0
    if not paired or weight.shape[1] % (members * 128):
        return plain_body(weight, test_matrix, rank_mask)
    return ring_body(Ring(members), weight, test_matrix, rank_mask)


def solution(mesh):
    in_specs = (P(("groups", "row"), None), P("row", None), P("groups"))
    out_specs = (P(("groups", "row"), None), P(("groups", "row"), None), P("groups"))
    return jax.shard_map(body, mesh=mesh, in_specs=in_specs, out_specs=out_specs, check_vma=False)
```

```python
import functools
import math

import jax
import jax.numpy as jnp
import numpy as np
from jax import lax
from jax.experimental import pallas as pl
from jax.experimental.pallas import tpu as pltpu
from jax.sharding import PartitionSpec as P

RANK = 224
MIB = 1024 * 1024


def selector(rank_mask, kept):
    positions = jnp.cumsum(rank_mask) - 1
    targets = lax.iota(jnp.int32, kept)
    matches = (rank_mask[:, None] == 1) & (positions[:, None] == targets[None, :])
    return matches.astype(jnp.float32)


def plain_body(weight, test_matrix, rank_mask):
    across = (((0,), (0,)), ((), ()))
    members = lax.axis_size("row")
    picker = selector(rank_mask, RANK)
    sketch_part = lax.psum_scatter(
        lax.dot_general(weight, test_matrix, across, preferred_element_type=jnp.float32),
        "row",
        scatter_dimension=0,
        tiled=True,
    ).astype(jnp.bfloat16)

    def add_rows(piece_rows):
        return jnp.dot(weight, piece_rows, preferred_element_type=jnp.float32)

    mixed = add_rows(lax.all_gather(sketch_part, "row", axis=0, tiled=True)).astype(jnp.bfloat16)
    powered = lax.psum_scatter(
        lax.dot_general(weight, mixed, across, preferred_element_type=jnp.float32),
        "row",
        scatter_dimension=0,
        tiled=True,
    )
    local_gram = lax.dot_general(powered, powered, across, precision=lax.Precision.HIGHEST)
    gram_matrix = lax.psum(local_gram, "row")
    cholesky_factor = jnp.linalg.cholesky(gram_matrix)
    ortho_basis = lax.linalg.triangular_solve(
        cholesky_factor, powered, left_side=False, lower=True, transpose_a=True
    )
    own_chosen = jnp.dot(ortho_basis, picker, precision=lax.Precision.HIGHEST)
    projected = add_rows(lax.all_gather(own_chosen.astype(jnp.bfloat16), "row", axis=0, tiled=True))
    left_factor = own_chosen * math.sqrt(weight.shape[1])
    energy = lax.psum(jnp.sum(projected * projected), "row")
    spread = jnp.sqrt(energy / (weight.shape[0] * members * RANK) + 1e-06)
    right_factor = (projected / spread).astype(jnp.bfloat16)
    return (left_factor, right_factor, spread.reshape(1))


class Ring:
    def __init__(self, members):
        chips = members // 2
        order = list(range(0, chips, 2)) + list(range(chips - 1, 0, -2))
        place = {chip: at for at, chip in enumerate(order)}
        self.chips, self.far = chips, chips // 2
        self.pair = [(device, device ^ 1) for device in range(members)]
        self.ahead = []
        for at, chip in enumerate(order):
            self.ahead.append((2 * chip, 2 * order[(at + 1) % chips]))
            self.ahead.append((2 * chip + 1, 2 * order[at - 1] + 1))

        def halves(device, steps, core):
            at = place[device // 2] + (steps if device % 2 == 0 else -steps)
            chip = order[at % chips]
            return [2 * chip + core, 2 * chip + 1 - core]

        self.width, self.table = {}, []
        for device in range(members):
            core, row = device % 2, []

            def put(name, values):
                self.width[name] = (len(row), len(values))
                row.extend(values)

            for k in range(self.far + 1):
                one = k == self.far
                mine, other = halves(device, k, core), halves(device, -k, 1 - core)
                put(("sum", k), mine if k == 0 else (mine[:1] + other[:1] if one else mine + other))
                mine, other = halves(device, -k, core), halves(device, k, 1 - core)
                put(("use", k), mine if k == 0 else (mine[:1] + other[:1] if one else mine + other))
            arrival = [device // 2]
            for k in range(1, self.far):
                arrival += [halves(device, -k, core)[0] // 2, halves(device, k, core)[0] // 2]
            arrival.append(halves(device, self.far, core)[0] // 2)
            put("arrival", [arrival.index(chip) for chip in range(chips)])
            self.table.append(row)

    def row(self):
        table = jnp.asarray(np.array(self.table, np.int32))
        row = lax.dynamic_index_in_dim(table, lax.axis_index("row"), 0, keepdims=False)
        return {name: row[at : at + size] for name, (at, size) in self.width.items()}


def columns_kernel(kept, cuts, ids_ref, left_ref, weight_ref, keep_ref, *rest):
    step, cut = pl.program_id(0), pl.program_id(1)
    part = jnp.dot(left_ref[...], weight_ref[...], preferred_element_type=jnp.float32)
    if cuts > 1:
        total_ref = rest[-1]

        @pl.when(cut == 0)
        def _():
            total_ref[...] = part

        @pl.when((cut > 0) & (cut < cuts - 1))
        def _():
            total_ref[...] += part

    def finish():
        total = total_ref[...] + part if cuts > 1 else part

        @pl.when(step < kept)
        def _():
            keep_ref[...] = total

        @pl.when(step >= kept)
        def _():
            rest[0][...] = total.astype(jnp.bfloat16)

    def finish_all():
        keep_ref[...] = total_ref[...] + part if cuts > 1 else part

    pl.when(cut == cuts - 1)(finish if kept is not None else finish_all)


def column_sums(left, weight, ids, half, split, cuts):
    rows, wide = left.shape[1], left.shape[0]
    steps, tall = ids.shape[0], rows // cuts
    kept = steps // 2 if split else steps
    out_shape = [jax.ShapeDtypeStruct((wide, kept * half), jnp.float32)]
    out_specs = [pl.BlockSpec((wide, half), lambda j, c, ids: (0, jnp.minimum(j, kept - 1)))]
    if split:
        out_shape.append(jax.ShapeDtypeStruct((wide, kept * half), jnp.bfloat16))
        out_specs.append(pl.BlockSpec((wide, half), lambda j, c, ids: (0, jnp.maximum(j - kept, 0))))
    return pl.pallas_call(
        functools.partial(columns_kernel, kept if split else None, cuts),
        out_shape=out_shape,
        grid_spec=pltpu.PrefetchScalarGridSpec(
            num_scalar_prefetch=1,
            grid=(steps, cuts),
            in_specs=[
                pl.BlockSpec((wide, tall), lambda j, c, ids: (0, c)),
                pl.BlockSpec((tall, half), lambda j, c, ids: (c, ids[j])),
            ],
            out_specs=out_specs,
            scratch_shapes=[pltpu.VMEM((wide, half), jnp.float32)] if cuts > 1 else [],
        ),
        compiler_params=pltpu.CompilerParams(
            dimension_semantics=("arbitrary", "arbitrary"), vmem_limit_bytes=32 * MIB
        ),
        cost_estimate=pl.CostEstimate(
            flops=2 * wide * rows * steps * half,
            bytes_accessed=2 * rows * steps * half + 2 * rows * wide,
            transcendentals=0,
        ),
    )(ids, left, weight)


def invert_kernel(counts, order_ref, *refs):
    grams, out_ref = refs[:len(counts)], refs[len(counts)]
    all_ref, work_ref = refs[len(counts) + 1 :]
    at = 0
    for ref, count in zip(grams, counts):
        all_ref[at : at + count] = ref[...]
        at += count
    size = work_ref.shape[0]
    total = all_ref[order_ref[0]]
    for chip in range(1, at):
        total = total + all_ref[order_ref[chip]]
    work_ref[...] = jnp.zeros_like(work_ref)
    work_ref[:, :size] = total
    lanes = lax.broadcasted_iota(jnp.int32, (8, 128), 1)
    panels = size // 8
    for first in range(0, panels, 8):
        side = first // 16
        tall = size - 8 * first

        def panel(p, _, first=first, side=side, tall=tall):
            body = work_ref[8 * first :, :]
            low, high = body[:, :128], body[:, 128:]
            sides = [low, high]
            block = [work_ref[pl.ds(8 * p, 8), :128], work_ref[pl.ds(8 * p, 8), 128:]]
            below = lax.broadcasted_iota(jnp.int32, (tall, 128), 0) - 8 * (p - first)
            inside = lax.broadcasted_iota(jnp.int32, (8, 128), 0)
            pivots = jnp.zeros((8, 128), jnp.float32)
            for s in range(8):
                lane = 8 * p + s - 128 * side
                here = lanes == lane
                rows = [jnp.broadcast_to(b[s : s + 1], (8, 128)) for b in block]
                at = jnp.full((8, 128), lane, jnp.int32)
                pivot = jnp.take_along_axis(rows[side], at, axis=1)
                inverse = 1.0 / pivot
                pivots = jnp.where(inside == s, pivot, pivots)
                rows[side] = jnp.where(here, 1.0, rows[side])

                def reduce(parts, beyond):
                    count = parts[0].shape[0] // 8
                    spread = lambda x: jnp.tile(x, (count, 1)) if count > 1 else x
                    column = jnp.take_along_axis(parts[side], spread(at), axis=1)
                    factor = jnp.where(beyond, column * spread(inverse), 0.0)
                    parts = list(parts)
                    parts[side] = jnp.where(spread(here) & beyond, 0.0, parts[side])
                    return [part - factor * spread(row) for part, row in zip(parts, rows)]

                if s < 7:
                    block = reduce(block, inside > s)
                else:
                    block[side] = block[side]
                sides = reduce(sides, below > s)
            work_ref[8 * first :, :128] = sides[0]
            work_ref[8 * first :, 128:] = sides[1]
            scale = lax.rsqrt(pivots)
            final = [work_ref[pl.ds(8 * p, 8), :128], work_ref[pl.ds(8 * p, 8), 128:]]
            both = jnp.concatenate([final[0] * scale, final[1] * scale], 1)
            columns = lax.broadcasted_iota(jnp.int32, (8, 256), 1)
            rows_at = lax.broadcasted_iota(jnp.int32, (8, 256), 0) + 8 * p
            both = jnp.where(columns == rows_at, jnp.concatenate([scale, scale], 1), both)
            both = jnp.where(columns > rows_at, 0.0, both)
            out_ref[pl.ds(8 * p, 8), :] = both[:, :size]
            return 0

        lax.fori_loop(first, min(first + 8, panels), panel, 0)

def invert(order, grams):
    size = grams[0].shape[-1]
    counts = [g.shape[0] for g in grams]
    return pl.pallas_call(
        functools.partial(invert_kernel, counts),
        out_shape=jax.ShapeDtypeStruct((size, size), jnp.float32),
        grid_spec=pltpu.PrefetchScalarGridSpec(
            num_scalar_prefetch=1, grid=(),
            in_specs=[pl.BlockSpec(memory_space=pltpu.VMEM)] * len(grams),
            out_specs=pl.BlockSpec(memory_space=pltpu.VMEM),
            scratch_shapes=[pltpu.VMEM((sum(counts), size, size), jnp.float32), pltpu.VMEM((size, 256), jnp.float32)],
        ),
        compiler_params=pltpu.CompilerParams(vmem_limit_bytes=32 * MIB),
    )(order, *grams)


def rows_kernel(pieces, halves, chained, last, turned, with_gram, *refs):
    refs = list(refs[1:])
    weight_ref = refs.pop(0)
    piece_refs = [refs.pop(0) for _ in range(pieces)]
    before_ref = refs.pop(0) if chained else None
    out_ref = refs.pop(0)
    gram_ref = refs.pop(0) if with_gram else None
    narrow = out_ref.dtype != jnp.float32
    total_ref = refs.pop(0) if narrow else out_ref
    block, step = pl.program_id(0), pl.program_id(1)
    steps = pieces * halves
    onto = (((1,), (1,)), ((), ()))

    def chosen():
        piece = piece_refs[0][...]
        return piece if pieces == 1 else jnp.where(step < halves, piece, piece_refs[1][...])

    if turned:
        part = lax.dot_general(chosen(), weight_ref[...], onto, preferred_element_type=jnp.float32)
    else:
        upright_ref = refs.pop(0)

        @pl.when(block == 0)
        def _():
            upright_ref[step] = chosen().astype(jnp.float32).T.astype(jnp.bfloat16)

        part = jnp.dot(weight_ref[...], upright_ref[step], preferred_element_type=jnp.float32)

    @pl.when(step == 0)
    def _():
        total_ref[...] = before_ref[...] + part if chained else part

    @pl.when(step > 0)
    def _():
        total_ref[...] += part

    if narrow:

        @pl.when(step == steps - 1)
        def _():
            out_ref[...] = total_ref[...].astype(jnp.bfloat16)

    if with_gram:
        slots = gram_ref.shape[0]
        run = steps // slots

        @pl.when(block == 0)
        def _():
            piece = chosen()
            square = lax.dot_general(piece, piece, onto, preferred_element_type=jnp.float32)
            slot = step // run

            @pl.when(step % run == 0)
            def _():
                gram_ref[slot] = square

            @pl.when(step % run > 0)
            def _():
                gram_ref[slot] += square


def row_products(weight, pieces, ids, half, before, last, turned, with_gram):
    rows, wide = weight.shape[0], pieces[0].shape[0]
    halves = pieces[0].shape[1] // half
    steps = len(pieces) * halves
    tall = rows // 2 if rows % 256 == 0 else rows
    shape, tile = ((wide, rows), (wide, tall)) if turned else ((rows, wide), (tall, wide))
    place = (lambda i, j, ids: (0, i)) if turned else (lambda i, j, ids: (i, 0))
    narrow = turned and last

    def piece_spec(at):
        low = at * halves
        return pl.BlockSpec((wide, half), lambda i, j, ids: (0, jnp.clip(j - low, 0, halves - 1)))

    in_specs = [pl.BlockSpec((tall, half), lambda i, j, ids: (i, ids[j]))]
    in_specs += [piece_spec(at) for at in range(len(pieces))]
    operands = [weight, *pieces]
    if before is not None:
        in_specs.append(pl.BlockSpec(tile, place))
        operands.append(before)
    out_shape = [jax.ShapeDtypeStruct(shape, jnp.bfloat16 if narrow else jnp.float32)]
    out_specs = [pl.BlockSpec(tile, place)]
    if with_gram:
        slots = max(1, steps // 2)
        out_shape.append(jax.ShapeDtypeStruct((slots, wide, wide), jnp.float32))
        out_specs.append(pl.BlockSpec((slots, wide, wide), lambda i, j, ids: (0, 0, 0)))
    scratch = [pltpu.VMEM(tile, jnp.float32)] if narrow else []
    if not turned:
        scratch.append(pltpu.VMEM((steps, half, wide), jnp.bfloat16))
    return pl.pallas_call(
        functools.partial(
            rows_kernel, len(pieces), halves, before is not None, last, turned, with_gram
        ),
        out_shape=out_shape,
        grid_spec=pltpu.PrefetchScalarGridSpec(
            num_scalar_prefetch=1,
            grid=(rows // tall, steps),
            in_specs=in_specs,
            out_specs=out_specs,
            scratch_shapes=scratch,
        ),
        input_output_aliases={len(operands): 0} if before is not None and not narrow else {},
        compiler_params=pltpu.CompilerParams(
            dimension_semantics=("arbitrary", "arbitrary"), vmem_limit_bytes=40 * MIB
        ),
        cost_estimate=pl.CostEstimate(
            flops=2 * rows * wide * steps * half,
            bytes_accessed=2 * rows * steps * half + 8 * rows * wide,
            transcendentals=0,
        ),
    )(ids, *operands)


def ring_sum(ring, ids, left, weight, half, cuts):
    got = None
    for k in range(ring.far, 0, -1):
        keep, give = column_sums(left, weight, ids["sum", k], half, True, cuts)
        total = keep + lax.ppermute(give, "row", ring.pair).astype(jnp.float32)
        if got is not None:
            got = got.astype(jnp.float32)
            size = got.shape[1]
            if size < total.shape[1]:
                total = jnp.concatenate([total[:, :size] + got, total[:, size:]], 1)
            else:
                total = total + got
        total, left = lax.optimization_barrier((total.astype(jnp.bfloat16), left))
        got = lax.ppermute(total, "row", ring.ahead)
    (keep,) = column_sums(left, weight, ids["sum", 0], half, False, cuts)
    mine = keep + got.astype(jnp.float32)
    other = lax.ppermute(mine, "row", ring.pair)
    return mine + jnp.concatenate([other[:, half:], other[:, :half]], 1)


def ring_apply(ring, ids, chunk, weight, half, turned, with_gram):
    grams, before = [], None
    moving = chunk
    for k in range(ring.far + 1):
        if k == 0:
            pieces = [chunk]
        else:
            moving = lax.ppermute(moving if k < ring.far else moving[:, :half], "row", ring.ahead)
            moving, before = lax.optimization_barrier((moving, before))
            pieces = [moving, lax.ppermute(moving, "row", ring.pair)]
        last = k == ring.far
        before, *gram = row_products(
            weight, pieces, ids["use", k], half, before, last, turned, with_gram
        )
        grams += gram
    return before, grams


def group_sum(value, ring):
    rows = value.shape[0] // 2
    first = lax.axis_index("row") % 2 == 0
    low, high = value[:rows], value[rows:]
    part = jnp.where(first, low, high)
    part = part + lax.ppermute(jnp.where(first, high, low), "row", ring.pair)
    hop = 2
    while hop < 2 * ring.chips:
        swap = [(device, device ^ hop) for device in range(2 * ring.chips)]
        part = part + lax.ppermute(part, "row", swap)
        hop *= 2
    other = lax.ppermute(part, "row", ring.pair)
    return jnp.concatenate([jnp.where(first, part, other), jnp.where(first, other, part)], 0)


def ring_body(ring, weight, test_matrix, rank_mask):
    highest = lax.Precision.HIGHEST
    rows, features = weight.shape
    half = features // (2 * ring.chips)
    ids = ring.row()
    picker = selector(rank_mask, RANK)
    sketch = ring_sum(ring, ids, test_matrix.T, weight, half, 1).astype(jnp.bfloat16)
    mixed, _ = ring_apply(ring, ids, sketch, weight, half, True, False)
    powered = ring_sum(ring, ids, mixed, weight, half, 2)
    image, grams = ring_apply(
        ring, ids, powered.astype(jnp.bfloat16), weight, half, False, True
    )
    image_b = image.astype(jnp.bfloat16)
    square = lax.dot_general(
        image_b, image_b, (((0,), (0,)), ((), ())), preferred_element_type=jnp.float32
    )
    square = group_sum(square, ring)
    inverse = invert(ids["arrival"], grams)
    change = lax.dot_general(inverse, picker, (((0,), (0,)), ((), ())), precision=highest)
    own = powered[:, :half]
    left_factor = lax.dot_general(
        own, change, (((0,), (0,)), ((), ())), precision=highest
    ) * math.sqrt(features)
    energy = jnp.sum(square * jnp.dot(change, change.T, precision=highest))
    spread = jnp.sqrt(energy / (rows * 2 * ring.chips * RANK) + 1e-06)
    right_factor = (jnp.dot(image, change, precision=highest) / spread).astype(jnp.bfloat16)
    return (left_factor, right_factor, spread.reshape(1))


def body(weight, test_matrix, rank_mask):
    members = lax.axis_size("row")
    chips = members // 2
    paired = members % 2 == 0 and chips > 2 and chips & (chips - 1) == 0
    if not paired or weight.shape[1] % (members * 128):
        return plain_body(weight, test_matrix, rank_mask)
    return ring_body(Ring(members), weight, test_matrix, rank_mask)


def solution(mesh):
    in_specs = (P(("groups", "row"), None), P("row", None), P("groups"))
    out_specs = (P(("groups", "row"), None), P(("groups", "row"), None), P("groups"))
    return jax.shard_map(body, mesh=mesh, in_specs=in_specs, out_specs=out_specs, check_vma=False)
```

```python
import functools
import math

import jax
import jax.numpy as jnp
import numpy as np
from jax import lax
from jax.experimental import pallas as pl
from jax.experimental.pallas import tpu as pltpu
from jax.sharding import PartitionSpec as P

RANK = 224
MIB = 1024 * 1024


def selector(rank_mask, kept):
    positions = jnp.cumsum(rank_mask) - 1
    targets = lax.iota(jnp.int32, kept)
    matches = (rank_mask[:, None] == 1) & (positions[:, None] == targets[None, :])
    return matches.astype(jnp.float32)


def plain_body(weight, test_matrix, rank_mask):
    across = (((0,), (0,)), ((), ()))
    members = lax.axis_size("row")
    picker = selector(rank_mask, RANK)
    sketch_part = lax.psum_scatter(
        lax.dot_general(weight, test_matrix, across, preferred_element_type=jnp.float32),
        "row",
        scatter_dimension=0,
        tiled=True,
    ).astype(jnp.bfloat16)

    def add_rows(piece_rows):
        return jnp.dot(weight, piece_rows, preferred_element_type=jnp.float32)

    mixed = add_rows(lax.all_gather(sketch_part, "row", axis=0, tiled=True)).astype(jnp.bfloat16)
    powered = lax.psum_scatter(
        lax.dot_general(weight, mixed, across, preferred_element_type=jnp.float32),
        "row",
        scatter_dimension=0,
        tiled=True,
    )
    local_gram = lax.dot_general(powered, powered, across, precision=lax.Precision.HIGHEST)
    gram_matrix = lax.psum(local_gram, "row")
    cholesky_factor = jnp.linalg.cholesky(gram_matrix)
    ortho_basis = lax.linalg.triangular_solve(
        cholesky_factor, powered, left_side=False, lower=True, transpose_a=True
    )
    own_chosen = jnp.dot(ortho_basis, picker, precision=lax.Precision.HIGHEST)
    projected = add_rows(lax.all_gather(own_chosen.astype(jnp.bfloat16), "row", axis=0, tiled=True))
    left_factor = own_chosen * math.sqrt(weight.shape[1])
    energy = lax.psum(jnp.sum(projected * projected), "row")
    spread = jnp.sqrt(energy / (weight.shape[0] * members * RANK) + 1e-06)
    right_factor = (projected / spread).astype(jnp.bfloat16)
    return (left_factor, right_factor, spread.reshape(1))


class Ring:
    def __init__(self, members):
        chips = members // 2
        order = list(range(0, chips, 2)) + list(range(chips - 1, 0, -2))
        place = {chip: at for at, chip in enumerate(order)}
        self.chips, self.far = chips, chips // 2
        self.pair = [(device, device ^ 1) for device in range(members)]
        self.ahead = []
        for at, chip in enumerate(order):
            self.ahead.append((2 * chip, 2 * order[(at + 1) % chips]))
            self.ahead.append((2 * chip + 1, 2 * order[at - 1] + 1))

        def halves(device, steps, core):
            at = place[device // 2] + (steps if device % 2 == 0 else -steps)
            chip = order[at % chips]
            return [2 * chip + core, 2 * chip + 1 - core]

        self.width, self.table = {}, []
        for device in range(members):
            core, row = device % 2, []

            def put(name, values):
                self.width[name] = (len(row), len(values))
                row.extend(values)

            for k in range(self.far + 1):
                one = k == self.far
                mine, other = halves(device, k, core), halves(device, -k, 1 - core)
                put(("sum", k), mine if k == 0 else (mine[:1] + other[:1] if one else mine + other))
                mine, other = halves(device, -k, core), halves(device, k, 1 - core)
                put(("use", k), mine if k == 0 else (mine[:1] + other[:1] if one else mine + other))
            arrival = [device // 2]
            for k in range(1, self.far):
                arrival += [halves(device, -k, core)[0] // 2, halves(device, k, core)[0] // 2]
            arrival.append(halves(device, self.far, core)[0] // 2)
            put("arrival", [arrival.index(chip) for chip in range(chips)])
            self.table.append(row)

    def row(self):
        table = jnp.asarray(np.array(self.table, np.int32))
        row = lax.dynamic_index_in_dim(table, lax.axis_index("row"), 0, keepdims=False)
        return {name: row[at : at + size] for name, (at, size) in self.width.items()}


def block_copies(weight_ref, held_ref, sems, rows, columns):
    low, tall = rows
    return [
        pltpu.make_async_copy(
            weight_ref.at[pl.ds(low, tall), pl.ds(pl.multiple_of(start, 128), size)],
            held_ref.at[pl.ds(low, tall), pl.ds(at, size)],
            sems.at[number],
        )
        for number, (start, at, size) in enumerate(columns)
    ]


def in_turn(blocks, ahead, work):
    for block in blocks[:ahead]:
        for copy in block:
            copy.start()
    for at, block in enumerate(blocks):
        for copy in block:
            copy.wait()
        if at + ahead < len(blocks):
            for copy in blocks[at + ahead]:
                copy.start()
        work(at)


def columns_kernel(half, pieces, ids_ref, left_ref, weight_ref, *refs):
    outs, (held_ref, sems) = refs[:-2], refs[-2:]
    rows = weight_ref.shape[0]
    blocks = []
    for number, (turn, low, size, _, _) in enumerate(pieces):
        place = (ids_ref[turn] * half + low, turn * half + low, size)
        blocks.append(block_copies(weight_ref, held_ref, sems.at[number], (0, rows), [place]))

    def work(number):
        turn, low, size, out, at = pieces[number]
        part = jnp.dot(
            left_ref[...],
            held_ref[:, turn * half + low : turn * half + low + size],
            preferred_element_type=jnp.float32,
        )
        outs[out][:, at : at + size] = part.astype(outs[out].dtype)

    in_turn(blocks, 2, work)


def column_sums(left, weight, ids, half, split):
    rows, wide = left.shape[1], left.shape[0]
    turns = ids.shape[0]
    kept = turns // 2 if split else turns
    pieces = []
    for turn in range(turns):
        out, at = (0, turn * half) if turn < kept else (1, (turn - kept) * half)
        sizes = [half // 2] * 2 if turn == 0 and half % 256 == 0 else [half]
        low = 0
        for size in sizes:
            pieces.append((turn, low, size, out, at + low))
            low += size
    out_shape = [jax.ShapeDtypeStruct((wide, kept * half), jnp.float32)]
    if split:
        out_shape.append(jax.ShapeDtypeStruct((wide, kept * half), jnp.bfloat16))
    whole = pl.BlockSpec(memory_space=pltpu.VMEM)
    return pl.pallas_call(
        functools.partial(columns_kernel, half, pieces),
        out_shape=out_shape,
        in_specs=[
            pl.BlockSpec(memory_space=pltpu.SMEM),
            whole,
            pl.BlockSpec(memory_space=pl.ANY),
        ],
        out_specs=[whole] * len(out_shape),
        scratch_shapes=[
            pltpu.VMEM((rows, turns * half), jnp.bfloat16),
            pltpu.SemaphoreType.DMA((len(pieces), 1)),
        ],
        compiler_params=pltpu.CompilerParams(vmem_limit_bytes=40 * MIB),
        cost_estimate=pl.CostEstimate(
            flops=2 * wide * rows * turns * half,
            bytes_accessed=2 * rows * turns * half + 2 * rows * wide,
            transcendentals=0,
        ),
    )(ids, left, weight)


def invert_kernel(counts, first, *refs):
    refs = list(refs)
    lanes = lax.broadcasted_iota(jnp.int32, (8, 128), 1)
    if counts:
        order_ref = refs.pop(0)
        grams = [refs.pop(0) for _ in counts]
        work_ref, out_ref, all_ref = refs
        size = work_ref.shape[0]
        at = 0
        for ref, count in zip(grams, counts):
            all_ref[at : at + count] = ref[...]
            at += count
        total = all_ref[order_ref[0]]
        for chip in range(1, at):
            total = total + all_ref[order_ref[chip]]
        work_ref[...] = jnp.zeros_like(work_ref)
        work_ref[:, :size] = total
    else:
        before_ref, work_ref, out_ref = refs
        size = work_ref.shape[0]
        work_ref[...] = before_ref[...]
    side = first // 16
    tall = size - 8 * first

    def panel(p, _):
        body = work_ref[8 * first :, :]
        sides = [body[:, :128], body[:, 128:]]
        block = [work_ref[pl.ds(8 * p, 8), :128], work_ref[pl.ds(8 * p, 8), 128:]]
        below = lax.broadcasted_iota(jnp.int32, (tall, 128), 0) - 8 * (p - first)
        inside = lax.broadcasted_iota(jnp.int32, (8, 128), 0)
        pivots = jnp.zeros((8, 128), jnp.float32)
        for s in range(8):
            lane = 8 * p + s - 128 * side
            here = lanes == lane
            rows = [jnp.broadcast_to(b[s : s + 1], (8, 128)) for b in block]
            at = jnp.full((8, 128), lane, jnp.int32)
            pivot = jnp.take_along_axis(rows[side], at, axis=1)
            inverse = 1.0 / pivot
            pivots = jnp.where(inside == s, pivot, pivots)
            rows[side] = jnp.where(here, 1.0, rows[side])

            def reduce(parts, beyond):
                count = parts[0].shape[0] // 8
                spread = lambda x: jnp.tile(x, (count, 1)) if count > 1 else x
                column = jnp.take_along_axis(parts[side], spread(at), axis=1)
                factor = jnp.where(beyond, column * spread(inverse), 0.0)
                parts = list(parts)
                parts[side] = jnp.where(spread(here) & beyond, 0.0, parts[side])
                return [part - factor * spread(row) for part, row in zip(parts, rows)]

            if s < 7:
                block = reduce(block, inside > s)
            sides = reduce(sides, below > s)
        work_ref[8 * first :, :128] = sides[0]
        work_ref[8 * first :, 128:] = sides[1]
        scale = lax.rsqrt(pivots)
        final = [work_ref[pl.ds(8 * p, 8), :128], work_ref[pl.ds(8 * p, 8), 128:]]
        both = jnp.concatenate([final[0] * scale, final[1] * scale], 1)
        columns = lax.broadcasted_iota(jnp.int32, (8, 256), 1)
        rows_at = lax.broadcasted_iota(jnp.int32, (8, 256), 0) + 8 * p
        both = jnp.where(columns == rows_at, jnp.concatenate([scale, scale], 1), both)
        both = jnp.where(columns > rows_at, 0.0, both)
        out_ref[pl.ds(8 * (p - first), 8), :] = both[:, :size]
        return 0

    lax.fori_loop(first, first + out_ref.shape[0] // 8, panel, 0)


def invert_panels(first, size, work, order, grams):
    tall = min(64, size - 8 * first)
    whole = pl.BlockSpec(memory_space=pltpu.VMEM)
    counts = [] if grams is None else [gram.shape[0] for gram in grams]
    if grams is None:
        operands, in_specs, scratch = [work], [whole], []
    else:
        operands = [order, *grams]
        in_specs = [pl.BlockSpec(memory_space=pltpu.SMEM)] + [whole] * len(grams)
        scratch = [pltpu.VMEM((sum(counts), size, size), jnp.float32)]
    return pl.pallas_call(
        functools.partial(invert_kernel, counts, first),
        out_shape=[
            jax.ShapeDtypeStruct((size, 256), jnp.float32),
            jax.ShapeDtypeStruct((tall, size), jnp.float32),
        ],
        in_specs=in_specs,
        out_specs=[whole] * 2,
        scratch_shapes=scratch,
        input_output_aliases={} if counts else {0: 0},
        compiler_params=pltpu.CompilerParams(vmem_limit_bytes=32 * MIB),
        cost_estimate=pl.CostEstimate(flops=10**9, bytes_accessed=2 * 10**7, transcendentals=0),
    )(*operands)


def rows_kernel(half, pieces, spans, chained, turned, with_gram, ids_ref, weight_ref, *refs):
    refs = list(refs)
    piece_refs = [refs.pop(0) for _ in range(pieces)]
    before_ref = refs.pop(0) if chained else None
    out_ref = refs.pop(0)
    gram_ref = refs.pop(0) if with_gram else None
    held_ref, ready_ref, sems = refs
    halves = piece_refs[0].shape[1] // half
    columns = [(ids_ref[turn] * half, turn * half, half) for turn in range(pieces * halves)]
    blocks = [
        block_copies(weight_ref, held_ref, sems.at[number], span, columns)
        for number, span in enumerate(spans)
    ]
    onto = (((1,), (1,)), ((), ()))

    def work(number):
        low, tall = spans[number]
        span = pl.ds(low, tall)
        if number == 0:
            for turn in range(pieces * halves):
                at = turn % halves * half
                piece = piece_refs[turn // halves][:, at : at + half]
                if turned:
                    ready_ref[:, turn * half : (turn + 1) * half] = piece
                else:
                    upright = piece.astype(jnp.float32).T.astype(jnp.bfloat16)
                    ready_ref[turn * half : (turn + 1) * half, :] = upright
        if turned:
            part = lax.dot_general(
                ready_ref[...], held_ref[span, :], onto, preferred_element_type=jnp.float32
            )
            place = (slice(None), span)
        else:
            part = jnp.dot(held_ref[span, :], ready_ref[...], preferred_element_type=jnp.float32)
            place = (span, slice(None))
        if chained:
            part = before_ref[place] + part
        out_ref[place] = part.astype(out_ref.dtype)

    in_turn(blocks, 2, work)
    if with_gram:
        slots = gram_ref.shape[0]
        for slot in range(slots):
            total = None
            for turn in range(slot * 2, min(slot * 2 + 2, pieces * halves)):
                at = turn % halves * half
                piece = piece_refs[turn // halves][:, at : at + half]
                square = lax.dot_general(piece, piece, onto, preferred_element_type=jnp.float32)
                total = square if total is None else total + square
            gram_ref[slot] = total


def row_products(weight, pieces, ids, half, before, last, turned, with_gram):
    rows, wide = weight.shape[0], pieces[0].shape[0]
    turns = len(pieces) * (pieces[0].shape[1] // half)
    tall = 512 if turned else 416
    first = 256 if turned else 208
    spans, low = [], 0
    while low < rows:
        size = min(first if low == 0 else tall, rows - low)
        spans.append((low, size))
        low += size
    narrow = turned and last
    whole = pl.BlockSpec(memory_space=pltpu.VMEM)
    operands = [ids, weight, *pieces]
    in_specs = [pl.BlockSpec(memory_space=pltpu.SMEM), pl.BlockSpec(memory_space=pl.ANY)]
    in_specs += [whole] * len(pieces)
    if before is not None:
        in_specs.append(whole)
        operands.append(before)
    shape = (wide, rows) if turned else (rows, wide)
    out_shape = [jax.ShapeDtypeStruct(shape, jnp.bfloat16 if narrow else jnp.float32)]
    if with_gram:
        out_shape.append(jax.ShapeDtypeStruct((max(1, turns // 2), wide, wide), jnp.float32))
    depth = turns * half
    return pl.pallas_call(
        functools.partial(
            rows_kernel, half, len(pieces), spans, before is not None, turned, with_gram
        ),
        out_shape=out_shape,
        in_specs=in_specs,
        out_specs=[whole] * len(out_shape),
        scratch_shapes=[
            pltpu.VMEM((rows, depth), jnp.bfloat16),
            pltpu.VMEM((wide, depth) if turned else (depth, wide), jnp.bfloat16),
            pltpu.SemaphoreType.DMA((len(spans), turns)),
        ],
        input_output_aliases={len(operands) - 1: 0} if before is not None and not narrow else {},
        compiler_params=pltpu.CompilerParams(vmem_limit_bytes=40 * MIB),
        cost_estimate=pl.CostEstimate(
            flops=2 * rows * wide * turns * half,
            bytes_accessed=2 * rows * turns * half + 8 * rows * wide,
            transcendentals=0,
        ),
    )(*operands)


def ring_sum(ring, ids, left, weight, half):
    got = None
    for k in range(ring.far, 0, -1):
        keep, give = column_sums(left, weight, ids["sum", k], half, True)
        total = keep + lax.ppermute(give, "row", ring.pair).astype(jnp.float32)
        if got is not None:
            got = got.astype(jnp.float32)
            size = got.shape[1]
            if size < total.shape[1]:
                total = jnp.concatenate([total[:, :size] + got, total[:, size:]], 1)
            else:
                total = total + got
        total, left = lax.optimization_barrier((total.astype(jnp.bfloat16), left))
        got = lax.ppermute(total, "row", ring.ahead)
    (keep,) = column_sums(left, weight, ids["sum", 0], half, False)
    mine = keep + got.astype(jnp.float32)
    other = lax.ppermute(mine, "row", ring.pair)
    return mine + jnp.concatenate([other[:, half:], other[:, :half]], 1)


def ring_apply(ring, ids, chunk, weight, half, turned, with_gram):
    grams, before = [], None
    moving = chunk
    for k in range(ring.far + 1):
        if k == 0:
            pieces = [chunk]
        else:
            moving = lax.ppermute(moving if k < ring.far else moving[:, :half], "row", ring.ahead)
            moving, before = lax.optimization_barrier((moving, before))
            pieces = [moving, lax.ppermute(moving, "row", ring.pair)]
        last = k == ring.far
        before, *gram = row_products(
            weight, pieces, ids["use", k], half, before, last, turned, with_gram
        )
        grams += gram
    return before, grams


def sum_beside_inverse(value, ring, order, grams):
    size = value.shape[0]
    rows = size // 2
    first = lax.axis_index("row") % 2 == 0
    low, high = value[:rows], value[rows:]
    part = jnp.where(first, low, high)
    hops = [ring.pair]
    for bit in range(ring.chips.bit_length() - 1):
        hops.append([(device, device ^ (2 << bit)) for device in range(2 * ring.chips)])
    panels = list(range(0, size // 8, 8))
    work, strips = None, []
    for at in range(max(len(hops), len(panels))):
        got = None
        if at < len(hops):
            got = lax.ppermute(jnp.where(first, high, low) if at == 0 else part, "row", hops[at])
        if at < len(panels):
            work, strip = invert_panels(panels[at], size, work, order, grams if at == 0 else None)
            strips.append(strip)
        if got is not None:
            got, work = lax.optimization_barrier((got, work))
            part = part + got
    other = lax.ppermute(part, "row", ring.pair)
    total = jnp.concatenate([jnp.where(first, part, other), jnp.where(first, other, part)], 0)
    return total, jnp.concatenate(strips, 0)


def ring_body(ring, weight, test_matrix, rank_mask):
    highest = lax.Precision.HIGHEST
    rows, features = weight.shape
    half = features // (2 * ring.chips)
    ids = ring.row()
    picker = selector(rank_mask, RANK)
    sketch = ring_sum(ring, ids, test_matrix.T, weight, half).astype(jnp.bfloat16)
    mixed, _ = ring_apply(ring, ids, sketch, weight, half, True, False)
    powered = ring_sum(ring, ids, mixed, weight, half)
    image, grams = ring_apply(
        ring, ids, powered.astype(jnp.bfloat16), weight, half, False, True
    )
    image_b = image.astype(jnp.bfloat16)
    square = lax.dot_general(
        image_b, image_b, (((0,), (0,)), ((), ())), preferred_element_type=jnp.float32
    )
    square, inverse = sum_beside_inverse(square, ring, ids["arrival"], grams)
    change = lax.dot_general(inverse, picker, (((0,), (0,)), ((), ())), precision=highest)
    own = powered[:, :half]
    left_factor = lax.dot_general(
        own, change, (((0,), (0,)), ((), ())), precision=highest
    ) * math.sqrt(features)
    energy = jnp.sum(square * jnp.dot(change, change.T, precision=highest))
    spread = jnp.sqrt(energy / (rows * 2 * ring.chips * RANK) + 1e-06)
    right_factor = (jnp.dot(image, change, precision=lax.Precision.HIGH) / spread).astype(jnp.bfloat16)
    return (left_factor, right_factor, spread.reshape(1))


def body(weight, test_matrix, rank_mask):
    members = lax.axis_size("row")
    chips = members // 2
    paired = members % 2 == 0 and chips > 2 and chips & (chips - 1) == 0
    if not paired or weight.shape[1] % (members * 128):
        return plain_body(weight, test_matrix, rank_mask)
    return ring_body(Ring(members), weight, test_matrix, rank_mask)


def solution(mesh):
    in_specs = (P(("groups", "row"), None), P("row", None), P("groups"))
    out_specs = (P(("groups", "row"), None), P(("groups", "row"), None), P("groups"))
    return jax.shard_map(body, mesh=mesh, in_specs=in_specs, out_specs=out_specs, check_vma=False)
```

```python
import functools
import math

import jax
import jax.numpy as jnp
import numpy as np
from jax import lax
from jax.experimental import pallas as pl
from jax.experimental.pallas import tpu as pltpu
from jax.sharding import PartitionSpec as P

RANK = 224
MIB = 1024 * 1024


def selector(rank_mask, kept):
    positions = jnp.cumsum(rank_mask) - 1
    targets = lax.iota(jnp.int32, kept)
    matches = (rank_mask[:, None] == 1) & (positions[:, None] == targets[None, :])
    return matches.astype(jnp.float32)


def plain_body(weight, test_matrix, rank_mask):
    across = (((0,), (0,)), ((), ()))
    members = lax.axis_size("row")
    picker = selector(rank_mask, RANK)
    sketch_part = lax.psum_scatter(
        lax.dot_general(weight, test_matrix, across, preferred_element_type=jnp.float32),
        "row",
        scatter_dimension=0,
        tiled=True,
    ).astype(jnp.bfloat16)

    def add_rows(piece_rows):
        return jnp.dot(weight, piece_rows, preferred_element_type=jnp.float32)

    mixed = add_rows(lax.all_gather(sketch_part, "row", axis=0, tiled=True)).astype(jnp.bfloat16)
    powered = lax.psum_scatter(
        lax.dot_general(weight, mixed, across, preferred_element_type=jnp.float32),
        "row",
        scatter_dimension=0,
        tiled=True,
    )
    local_gram = lax.dot_general(powered, powered, across, precision=lax.Precision.HIGHEST)
    gram_matrix = lax.psum(local_gram, "row")
    cholesky_factor = jnp.linalg.cholesky(gram_matrix)
    ortho_basis = lax.linalg.triangular_solve(
        cholesky_factor, powered, left_side=False, lower=True, transpose_a=True
    )
    own_chosen = jnp.dot(ortho_basis, picker, precision=lax.Precision.HIGHEST)
    projected = add_rows(lax.all_gather(own_chosen.astype(jnp.bfloat16), "row", axis=0, tiled=True))
    left_factor = own_chosen * math.sqrt(weight.shape[1])
    energy = lax.psum(jnp.sum(projected * projected), "row")
    spread = jnp.sqrt(energy / (weight.shape[0] * members * RANK) + 1e-06)
    right_factor = (projected / spread).astype(jnp.bfloat16)
    return (left_factor, right_factor, spread.reshape(1))


class Ring:
    def __init__(self, members):
        chips = members // 2
        order = list(range(0, chips, 2)) + list(range(chips - 1, 0, -2))
        place = {chip: at for at, chip in enumerate(order)}
        self.chips, self.far = chips, chips // 2
        self.pair = [(device, device ^ 1) for device in range(members)]
        self.ahead = []
        for at, chip in enumerate(order):
            self.ahead.append((2 * chip, 2 * order[(at + 1) % chips]))
            self.ahead.append((2 * chip + 1, 2 * order[at - 1] + 1))

        def halves(device, steps, core):
            at = place[device // 2] + (steps if device % 2 == 0 else -steps)
            chip = order[at % chips]
            return [2 * chip + core, 2 * chip + 1 - core]

        self.width, self.table = {}, []
        for device in range(members):
            core, row = device % 2, []

            def put(name, values):
                self.width[name] = (len(row), len(values))
                row.extend(values)

            for k in range(self.far + 1):
                one = k == self.far
                mine, other = halves(device, k, core), halves(device, -k, 1 - core)
                put(("sum", k), mine if k == 0 else (mine[:1] + other[:1] if one else mine + other))
                mine, other = halves(device, -k, core), halves(device, k, 1 - core)
                put(("use", k), mine if k == 0 else (mine[:1] + other[:1] if one else mine + other))
            arrival = [device // 2]
            for k in range(1, self.far):
                arrival += [halves(device, -k, core)[0] // 2, halves(device, k, core)[0] // 2]
            arrival.append(halves(device, self.far, core)[0] // 2)
            put("arrival", [arrival.index(chip) for chip in range(chips)])
            self.table.append(row)

    def row(self):
        table = jnp.asarray(np.array(self.table, np.int32))
        return lax.dynamic_index_in_dim(table, lax.axis_index("row"), 0, keepdims=False)


def block_copies(weight_ref, held_ref, sems, rows, columns):
    low, tall = rows
    return [
        pltpu.make_async_copy(
            weight_ref.at[pl.ds(low, tall), pl.ds(pl.multiple_of(start, 128), size)],
            held_ref.at[pl.ds(low, tall), pl.ds(at, size)],
            sems.at[number],
        )
        for number, (start, at, size) in enumerate(columns)
    ]


def in_turn(blocks, ahead, work, prepare=None):
    for block in blocks[:ahead]:
        for copy in block:
            copy.start()
    if prepare is not None:
        prepare()
    for at, block in enumerate(blocks):
        for copy in block:
            copy.wait()
        if at + ahead < len(blocks):
            for copy in blocks[at + ahead]:
                copy.start()
        work(at)


def columns_kernel(half, base, pieces, ids_ref, left_ref, weight_ref, *refs):
    outs, (held_ref, sems) = refs[:-2], refs[-2:]
    rows = weight_ref.shape[0]
    blocks = []
    for number, (turn, low, size, _, _) in enumerate(pieces):
        place = (ids_ref[base + turn] * half + low, turn * half + low, size)
        blocks.append(block_copies(weight_ref, held_ref, sems.at[number], (0, rows), [place]))

    def work(number):
        turn, low, size, out, at = pieces[number]
        part = jnp.dot(
            left_ref[...],
            held_ref[:, turn * half + low : turn * half + low + size],
            preferred_element_type=jnp.float32,
        )
        outs[out][:, at : at + size] = part.astype(outs[out].dtype)

    in_turn(blocks, 2, work)


def column_sums(left, weight, ids, span, half, split):
    rows, wide = left.shape[1], left.shape[0]
    base, turns = span
    kept = turns // 2 if split else turns
    pieces = []
    for turn in range(turns):
        out, at = (0, turn * half) if turn < kept else (1, (turn - kept) * half)
        edge = turn in (0, turns - 1) and half % 256 == 0
        sizes = [half // 2] * 2 if edge else [half]
        low = 0
        for size in sizes:
            pieces.append((turn, low, size, out, at + low))
            low += size
    out_shape = [jax.ShapeDtypeStruct((wide, kept * half), jnp.float32)]
    if split:
        out_shape.append(jax.ShapeDtypeStruct((wide, kept * half), jnp.bfloat16))
    whole = pl.BlockSpec(memory_space=pltpu.VMEM)
    return pl.pallas_call(
        functools.partial(columns_kernel, half, base, pieces),
        out_shape=out_shape,
        in_specs=[
            pl.BlockSpec(memory_space=pltpu.SMEM),
            whole,
            pl.BlockSpec(memory_space=pl.ANY),
        ],
        out_specs=[whole] * len(out_shape),
        scratch_shapes=[
            pltpu.VMEM((rows, turns * half), jnp.bfloat16),
            pltpu.SemaphoreType.DMA((len(pieces), 1)),
        ],
        compiler_params=pltpu.CompilerParams(vmem_limit_bytes=40 * MIB),
        cost_estimate=pl.CostEstimate(
            flops=2 * wide * rows * turns * half,
            bytes_accessed=2 * rows * turns * half + 2 * rows * wide,
            transcendentals=0,
        ),
    )(ids, left, weight)


def invert_kernel(counts, base, first, *refs):
    refs = list(refs)
    lanes = lax.broadcasted_iota(jnp.int32, (8, 128), 1)
    if counts:
        order_ref = refs.pop(0)
        grams = [refs.pop(0) for _ in counts]
        work_ref, out_ref, all_ref = refs
        size = work_ref.shape[0]
        at = 0
        for ref, count in zip(grams, counts):
            all_ref[at : at + count] = ref[...]
            at += count
        total = all_ref[order_ref[base]]
        for chip in range(1, at):
            total = total + all_ref[order_ref[base + chip]]
        work_ref[...] = jnp.zeros_like(work_ref)
        work_ref[:, :size] = total
    else:
        before_ref, work_ref, out_ref = refs
        size = work_ref.shape[0]
        work_ref[...] = before_ref[...]
    side = first // 16
    tall = size - 8 * first

    rows_at = 8 * first + lax.broadcasted_iota(jnp.int32, (tall, 128), 0)
    inside = lax.broadcasted_iota(jnp.int32, (8, 128), 0)

    def packed(values):
        total = values[0]
        for s in range(1, 8):
            total = jnp.where(inside == s, values[s], total)
        return total

    def panel(p, _):
        raw = [work_ref[pl.ds(8 * p, 8), :128], work_ref[pl.ds(8 * p, 8), 128:]]
        entry, ratio, inverse = {}, {}, []
        for s in range(8):
            at = jnp.full((8, 128), 8 * p + s - 128 * side, jnp.int32)
            column = jnp.take_along_axis(raw[side], at, axis=1)
            for r in range(s + 1):
                entry[r, s] = jnp.broadcast_to(column[r : r + 1], (8, 128))
        for s in range(8):
            inverse.append(1.0 / entry[s, s])
            for t in range(s + 1, 8):
                ratio[t, s] = entry[s, t] * inverse[s]
            for t in range(s + 1, 8):
                for u in range(t, 8):
                    entry[t, u] = entry[t, u] - ratio[t, s] * entry[s, u]
        low = 8 * p - 128 * side
        own = (lanes >= low) & (lanes < low + 8)
        row = []
        for t in range(8):
            halves = [jnp.broadcast_to(part[t : t + 1], (8, 128)) for part in raw]
            unit = jnp.where(lanes == low + t, 1.0, 0.0)
            halves[side] = jnp.where(own, unit, halves[side])
            for s in range(t):
                halves = [half - ratio[t, s] * done for half, done in zip(halves, row[s])]
            row.append(halves)
        scale = lax.rsqrt(packed([entry[s, s] for s in range(8)]))
        inverses = packed(inverse)
        factors = []
        for half in range(2):
            whole = packed([row[s][half] for s in range(8)])
            beyond = lanes + 128 * half >= 8 * p + 8
            strip = jnp.where(beyond, 0.0, whole * scale)
            out_ref[pl.ds(8 * (p - first), 8), 128 * half : min(128 * half + 128, size)] = strip[
                :, : min(128, size - 128 * half)
            ]
            factors.append(jnp.where(beyond, whole * inverses, 0.0).T)
        factor = jnp.concatenate(factors, 0)[8 * first : size]
        spread = lambda x: jnp.tile(x, (tall // 8, 1))
        after = rows_at >= 8 * p + 8
        for half in range(2):
            place = (slice(8 * first, size), slice(128 * half, 128 * half + 128))
            rest = work_ref[place]
            if half == side:
                rest = jnp.where(spread(own) & after, 0.0, rest)
            for s in range(8):
                rest = rest - jnp.broadcast_to(factor[:, s : s + 1], (tall, 128)) * spread(row[s][half])
            work_ref[place] = rest
        return 0

    lax.fori_loop(first, first + out_ref.shape[0] // 8, panel, 0)


def invert_panels(first, size, work, ids, base, grams):
    tall = min(64, size - 8 * first)
    whole = pl.BlockSpec(memory_space=pltpu.VMEM)
    counts = [] if grams is None else [gram.shape[0] for gram in grams]
    if grams is None:
        operands, in_specs, scratch = [work], [whole], []
    else:
        operands = [ids, *grams]
        in_specs = [pl.BlockSpec(memory_space=pltpu.SMEM)] + [whole] * len(grams)
        scratch = [pltpu.VMEM((sum(counts), size, size), jnp.float32)]
    return pl.pallas_call(
        functools.partial(invert_kernel, counts, base, first),
        out_shape=[
            jax.ShapeDtypeStruct((size, 256), jnp.float32),
            jax.ShapeDtypeStruct((tall, size), jnp.float32),
        ],
        in_specs=in_specs,
        out_specs=[whole] * 2,
        scratch_shapes=scratch,
        input_output_aliases={} if counts else {0: 0},
        compiler_params=pltpu.CompilerParams(vmem_limit_bytes=32 * MIB),
        cost_estimate=pl.CostEstimate(flops=10**9, bytes_accessed=2 * 10**7, transcendentals=0),
    )(*operands)


def rows_kernel(half, base, pieces, spans, chained, with_gram, ids_ref, weight_ref, *refs):
    refs = list(refs)
    piece_refs = [refs.pop(0) for _ in range(pieces)]
    before_ref = refs.pop(0) if chained else None
    out_ref = refs.pop(0)
    gram_ref = refs.pop(0) if with_gram else None
    held_ref, ready_ref, sems = refs
    halves = piece_refs[0].shape[1] // half
    columns = [(ids_ref[base + turn] * half, turn * half, half) for turn in range(pieces * halves)]
    blocks = [
        block_copies(weight_ref, held_ref, sems.at[number], span, columns)
        for number, span in enumerate(spans)
    ]
    onto = (((1,), (1,)), ((), ()))

    grams = []
    if with_gram:
        slots = gram_ref.shape[0]
        grams = [range(2 * slot, min(2 * slot + 2, pieces * halves)) for slot in range(slots)]

    def piece(turn):
        at = turn % halves * half
        return piece_refs[turn // halves][:, at : at + half]

    def prepare():
        for turn in range(pieces * halves):
            ready_ref[:, turn * half : (turn + 1) * half] = piece(turn)

    def work(number):
        span = pl.ds(*spans[number])
        part = lax.dot_general(
            ready_ref[...], held_ref[span, :], onto, preferred_element_type=jnp.float32
        )
        if chained:
            part = before_ref[:, span] + part
        out_ref[:, span] = part.astype(out_ref.dtype)
        if 0 < number <= len(grams):
            squares = [
                lax.dot_general(piece(turn), piece(turn), onto, preferred_element_type=jnp.float32)
                for turn in grams[number - 1]
            ]
            gram_ref[number - 1] = sum(squares[1:], squares[0])

    in_turn(blocks, 2, work, prepare)


def row_products(weight, pieces, ids, base, half, before, narrow, with_gram):
    rows, wide = weight.shape[0], pieces[0].shape[0]
    turns = len(pieces) * (pieces[0].shape[1] // half)
    spans, low = [], 0
    while low < rows:
        edge = low == 0 or rows - low <= 512
        size = min(256 if edge else 512, rows - low)
        spans.append((low, size))
        low += size
    whole = pl.BlockSpec(memory_space=pltpu.VMEM)
    operands = [ids, weight, *pieces]
    in_specs = [pl.BlockSpec(memory_space=pltpu.SMEM), pl.BlockSpec(memory_space=pl.ANY)]
    in_specs += [whole] * len(pieces)
    if before is not None:
        in_specs.append(whole)
        operands.append(before)
    out_shape = [jax.ShapeDtypeStruct((wide, rows), jnp.bfloat16 if narrow else jnp.float32)]
    if with_gram:
        out_shape.append(jax.ShapeDtypeStruct((max(1, turns // 2), wide, wide), jnp.float32))
    depth = turns * half
    return pl.pallas_call(
        functools.partial(
            rows_kernel, half, base, len(pieces), spans, before is not None, with_gram
        ),
        out_shape=out_shape,
        in_specs=in_specs,
        out_specs=[whole] * len(out_shape),
        scratch_shapes=[
            pltpu.VMEM((rows, depth), jnp.bfloat16),
            pltpu.VMEM((wide, depth), jnp.bfloat16),
            pltpu.SemaphoreType.DMA((len(spans), turns)),
        ],
        input_output_aliases={len(operands) - 1: 0} if before is not None and not narrow else {},
        compiler_params=pltpu.CompilerParams(vmem_limit_bytes=40 * MIB),
        cost_estimate=pl.CostEstimate(
            flops=2 * rows * wide * turns * half,
            bytes_accessed=2 * rows * turns * half + 8 * rows * wide,
            transcendentals=0,
        ),
    )(*operands)


def ring_sum(ring, ids, left, weight, half):
    got = None
    for k in range(ring.far, 0, -1):
        keep, give = column_sums(left, weight, ids, ring.width["sum", k], half, True)
        given = lax.ppermute(give, "row", ring.pair)
        if got is not None:
            got = got.astype(jnp.float32)
            size = got.shape[1]
            if size < keep.shape[1]:
                keep = jnp.concatenate([keep[:, :size] + got, keep[:, size:]], 1)
            else:
                keep = keep + got
            keep, given = lax.optimization_barrier((keep, given))
        total = (keep + given.astype(jnp.float32)).astype(jnp.bfloat16)
        total, left = lax.optimization_barrier((total, left))
        got = lax.ppermute(total, "row", ring.ahead)
    (keep,) = column_sums(left, weight, ids, ring.width["sum", 0], half, False)
    mine = keep + got.astype(jnp.float32)
    other = lax.ppermute(mine, "row", ring.pair)
    return mine + jnp.concatenate([other[:, half:], other[:, :half]], 1)


def ring_apply(ring, ids, chunk, weight, half, narrow, with_gram):
    grams, before = [], None
    moving = chunk
    for k in range(ring.far + 1):
        if k == 0:
            pieces = [chunk]
        else:
            moving = lax.ppermute(moving if k < ring.far else moving[:, :half], "row", ring.ahead)
            moving, before = lax.optimization_barrier((moving, before))
            pieces = [moving, lax.ppermute(moving, "row", ring.pair)]
        last = k == ring.far
        before, *gram = row_products(
            weight, pieces, ids, ring.width["use", k][0], half, before, narrow and last, with_gram
        )
        grams += gram
    return before, grams


def sum_beside_inverse(value, ring, ids, grams):
    size = value.shape[0]
    rows = size // 2
    first = lax.axis_index("row") % 2 == 0
    low, high = value[:rows], value[rows:]
    part = jnp.where(first, low, high)
    hops = [ring.pair]
    for bit in range(ring.chips.bit_length() - 1):
        hops.append([(device, device ^ (2 << bit)) for device in range(2 * ring.chips)])
    panels = list(range(0, size // 8, 8))
    work, strips = None, []
    for at in range(max(len(hops), len(panels))):
        got = None
        if at < len(hops):
            got = lax.ppermute(jnp.where(first, high, low) if at == 0 else part, "row", hops[at])
        if at < len(panels):
            given = grams if at == 0 else None
            base = ring.width["arrival"][0]
            work, strip = invert_panels(panels[at], size, work, ids, base, given)
            strips.append(strip)
        if got is not None:
            got, work = lax.optimization_barrier((got, work))
            part = part + got
    other = lax.ppermute(part, "row", ring.pair)
    total = jnp.concatenate([jnp.where(first, part, other), jnp.where(first, other, part)], 0)
    return total, jnp.concatenate(strips, 0)


def ring_body(ring, weight, test_matrix, rank_mask):
    highest = lax.Precision.HIGHEST
    rows, features = weight.shape
    half = features // (2 * ring.chips)
    ids = ring.row()
    picker = selector(rank_mask, RANK)
    sketch = ring_sum(ring, ids, test_matrix.T, weight, half).astype(jnp.bfloat16)
    mixed, _ = ring_apply(ring, ids, sketch, weight, half, True, False)
    powered = ring_sum(ring, ids, mixed, weight, half)
    image, grams = ring_apply(
        ring, ids, powered.astype(jnp.bfloat16), weight, half, False, True
    )
    image_b = image.astype(jnp.bfloat16)
    square = lax.dot_general(
        image_b, image_b, (((1,), (1,)), ((), ())), preferred_element_type=jnp.float32
    )
    square, inverse = sum_beside_inverse(square, ring, ids, grams)
    change = lax.dot_general(inverse, picker, (((0,), (0,)), ((), ())), precision=highest)
    own = powered[:, :half]
    left_factor = lax.dot_general(
        own, change, (((0,), (0,)), ((), ())), precision=highest
    ) * math.sqrt(features)
    energy = jnp.sum(square * jnp.dot(change, change.T, precision=highest))
    spread = jnp.sqrt(energy / (rows * 2 * ring.chips * RANK) + 1e-06)
    projected = lax.dot_general(
        image, change, (((0,), (0,)), ((), ())), precision=lax.Precision.HIGH
    )
    right_factor = (projected / spread).astype(jnp.bfloat16)
    return (left_factor, right_factor, spread.reshape(1))


def body(weight, test_matrix, rank_mask):
    members = lax.axis_size("row")
    chips = members // 2
    paired = members % 2 == 0 and chips > 2 and chips & (chips - 1) == 0
    if not paired or weight.shape[1] % (members * 128):
        return plain_body(weight, test_matrix, rank_mask)
    return ring_body(Ring(members), weight, test_matrix, rank_mask)


def solution(mesh):
    in_specs = (P(("groups", "row"), None), P("row", None), P("groups"))
    out_specs = (P(("groups", "row"), None), P(("groups", "row"), None), P("groups"))
    return jax.shard_map(body, mesh=mesh, in_specs=in_specs, out_specs=out_specs, check_vma=False)
```

```python
import functools
import math

import jax
import jax.numpy as jnp
import numpy as np
from jax import lax
from jax.experimental import pallas as pl
from jax.experimental.pallas import tpu as pltpu
from jax.sharding import PartitionSpec as P

RANK = 224
MIB = 1024 * 1024


def selector(rank_mask, kept):
    positions = jnp.cumsum(rank_mask) - 1
    targets = lax.iota(jnp.int32, kept)
    matches = (rank_mask[:, None] == 1) & (positions[:, None] == targets[None, :])
    return matches.astype(jnp.float32)


def plain_body(weight, test_matrix, rank_mask):
    across = (((0,), (0,)), ((), ()))
    members = lax.axis_size("row")
    picker = selector(rank_mask, RANK)
    sketch_part = lax.psum_scatter(
        lax.dot_general(weight, test_matrix, across, preferred_element_type=jnp.float32),
        "row",
        scatter_dimension=0,
        tiled=True,
    ).astype(jnp.bfloat16)

    def add_rows(piece_rows):
        return jnp.dot(weight, piece_rows, preferred_element_type=jnp.float32)

    mixed = add_rows(lax.all_gather(sketch_part, "row", axis=0, tiled=True)).astype(jnp.bfloat16)
    powered = lax.psum_scatter(
        lax.dot_general(weight, mixed, across, preferred_element_type=jnp.float32),
        "row",
        scatter_dimension=0,
        tiled=True,
    )
    local_gram = lax.dot_general(powered, powered, across, precision=lax.Precision.HIGHEST)
    gram_matrix = lax.psum(local_gram, "row")
    cholesky_factor = jnp.linalg.cholesky(gram_matrix)
    ortho_basis = lax.linalg.triangular_solve(
        cholesky_factor, powered, left_side=False, lower=True, transpose_a=True
    )
    own_chosen = jnp.dot(ortho_basis, picker, precision=lax.Precision.HIGHEST)
    projected = add_rows(lax.all_gather(own_chosen.astype(jnp.bfloat16), "row", axis=0, tiled=True))
    left_factor = own_chosen * math.sqrt(weight.shape[1])
    energy = lax.psum(jnp.sum(projected * projected), "row")
    spread = jnp.sqrt(energy / (weight.shape[0] * members * RANK) + 1e-06)
    right_factor = (projected / spread).astype(jnp.bfloat16)
    return (left_factor, right_factor, spread.reshape(1))


class Ring:
    def __init__(self, members):
        chips = members // 2
        order = list(range(0, chips, 2)) + list(range(chips - 1, 0, -2))
        place = {chip: at for at, chip in enumerate(order)}
        self.chips, self.far = chips, chips // 2
        self.pair = [(device, device ^ 1) for device in range(members)]
        self.ahead = []
        for at, chip in enumerate(order):
            self.ahead.append((2 * chip, 2 * order[(at + 1) % chips]))
            self.ahead.append((2 * chip + 1, 2 * order[at - 1] + 1))

        def halves(device, steps, core):
            at = place[device // 2] + (steps if device % 2 == 0 else -steps)
            chip = order[at % chips]
            return [2 * chip + core, 2 * chip + 1 - core]

        self.width, self.table = {}, []
        for device in range(members):
            core, row = device % 2, []

            def put(name, values):
                self.width[name] = (len(row), len(values))
                row.extend(values)

            for k in range(self.far + 1):
                one = k == self.far
                mine, other = halves(device, k, core), halves(device, -k, 1 - core)
                put(("sum", k), mine if k == 0 else (mine[:1] + other[:1] if one else mine + other))
                mine, other = halves(device, -k, core), halves(device, k, 1 - core)
                put(("use", k), mine if k == 0 else (mine[:1] + other[:1] if one else mine + other))
            arrival = [device // 2]
            for k in range(1, self.far):
                arrival += [halves(device, -k, core)[0] // 2, halves(device, k, core)[0] // 2]
            arrival.append(halves(device, self.far, core)[0] // 2)
            put("arrival", [arrival.index(chip) for chip in range(chips)])
            self.table.append(row)

    def row(self):
        table = jnp.asarray(np.array(self.table, np.int32))
        return lax.dynamic_index_in_dim(table, lax.axis_index("row"), 0, keepdims=False)


def in_turn(blocks, ahead, work, prepare=None):
    for block in blocks[:ahead]:
        for copy in block:
            copy.start()
    if prepare is not None:
        prepare()
    for at, block in enumerate(blocks):
        for copy in block:
            copy.wait()
        if at + ahead < len(blocks):
            for copy in blocks[at + ahead]:
                copy.start()
        work(at)


def columns_kernel(half, base, pieces, ids_ref, left_ref, weight_ref, *refs):
    refs = list(refs)
    sems, held_ref = refs.pop(), refs.pop()
    blocks = []
    for number, (turn, low, tall, _, _) in enumerate(pieces):
        place = (pl.ds(low, tall), pl.ds(turn * half, half))
        source = pl.ds(pl.multiple_of(ids_ref[base + turn] * half, 128), half)
        blocks.append(
            [
                pltpu.make_async_copy(
                    weight_ref.at[pl.ds(low, tall), source], held_ref.at[place], sems.at[number]
                )
            ]
        )
    parts = {}

    def work(number):
        turn, low, tall, out, at = pieces[number]
        part = jnp.dot(
            left_ref[:, low : low + tall],
            held_ref[low : low + tall, turn * half : (turn + 1) * half],
            preferred_element_type=jnp.float32,
        )
        if turn in parts:
            part = parts.pop(turn) + part
        if low + tall < weight_ref.shape[0]:
            parts[turn] = part
        else:
            refs[out][:, at : at + half] = part.astype(refs[out].dtype)

    in_turn(blocks, 2, work)


def column_sums(left, weight, ids, span, half, split):
    rows, wide = left.shape[1], left.shape[0]
    base, turns = span
    kept = turns // 2 if split else turns
    short = 1024 if rows >= 2048 else rows // 2
    pieces = []
    for turn in range(turns):
        out, at = (0, turn * half) if turn < kept else (1, (turn - kept) * half)
        if turn == 0:
            cuts = [(0, short), (short, rows - short)]
        elif turn == turns - 1:
            cuts = [(0, rows - short), (rows - short, short)]
        else:
            cuts = [(0, rows)]
        pieces += [(turn, low, tall, out, at) for low, tall in cuts]
    out_shape = [jax.ShapeDtypeStruct((wide, kept * half), jnp.float32)]
    if split:
        out_shape.append(jax.ShapeDtypeStruct((wide, kept * half), jnp.bfloat16))
    whole = pl.BlockSpec(memory_space=pltpu.VMEM)
    return pl.pallas_call(
        functools.partial(columns_kernel, half, base, pieces),
        out_shape=out_shape,
        in_specs=[
            pl.BlockSpec(memory_space=pltpu.SMEM),
            whole,
            pl.BlockSpec(memory_space=pl.ANY),
        ],
        out_specs=[whole] * len(out_shape),
        scratch_shapes=[
            pltpu.VMEM((rows, turns * half), jnp.bfloat16),
            pltpu.SemaphoreType.DMA((len(pieces),)),
        ],
        compiler_params=pltpu.CompilerParams(vmem_limit_bytes=40 * MIB),
        cost_estimate=pl.CostEstimate(
            flops=2 * wide * rows * turns * half,
            bytes_accessed=2 * rows * turns * half + 2 * rows * wide,
            transcendentals=0,
        ),
    )(ids, left, weight)


def invert_kernel(counts, base, first, *refs):
    refs = list(refs)
    lanes = lax.broadcasted_iota(jnp.int32, (8, 128), 1)
    if counts:
        order_ref = refs.pop(0)
        grams = [refs.pop(0) for _ in counts]
        work_ref, out_ref, all_ref = refs
        size = work_ref.shape[0]
        at = 0
        for ref, count in zip(grams, counts):
            all_ref[at : at + count] = ref[...]
            at += count
        total = all_ref[order_ref[base]]
        for chip in range(1, at):
            total = total + all_ref[order_ref[base + chip]]
        work_ref[...] = jnp.zeros_like(work_ref)
        work_ref[:, :size] = total
    else:
        before_ref, work_ref, out_ref = refs
        size = work_ref.shape[0]
        work_ref[...] = before_ref[...]
    side = first // 16
    tall = size - 8 * first

    rows_at = 8 * first + lax.broadcasted_iota(jnp.int32, (tall, 128), 0)
    inside = lax.broadcasted_iota(jnp.int32, (8, 128), 0)

    def packed(values):
        total = values[0]
        for s in range(1, 8):
            total = jnp.where(inside == s, values[s], total)
        return total

    def panel(p, _):
        raw = [work_ref[pl.ds(8 * p, 8), :128], work_ref[pl.ds(8 * p, 8), 128:]]
        entry, ratio, inverse = {}, {}, []
        for s in range(8):
            at = jnp.full((8, 128), 8 * p + s - 128 * side, jnp.int32)
            column = jnp.take_along_axis(raw[side], at, axis=1)
            for r in range(s + 1):
                entry[r, s] = jnp.broadcast_to(column[r : r + 1], (8, 128))
        for s in range(8):
            inverse.append(1.0 / entry[s, s])
            for t in range(s + 1, 8):
                ratio[t, s] = entry[s, t] * inverse[s]
            for t in range(s + 1, 8):
                for u in range(t, 8):
                    entry[t, u] = entry[t, u] - ratio[t, s] * entry[s, u]
        low = 8 * p - 128 * side
        own = (lanes >= low) & (lanes < low + 8)
        row = []
        for t in range(8):
            halves = [jnp.broadcast_to(part[t : t + 1], (8, 128)) for part in raw]
            unit = jnp.where(lanes == low + t, 1.0, 0.0)
            halves[side] = jnp.where(own, unit, halves[side])
            for s in range(t):
                halves = [half - ratio[t, s] * done for half, done in zip(halves, row[s])]
            row.append(halves)
        scale = lax.rsqrt(packed([entry[s, s] for s in range(8)]))
        inverses = packed(inverse)
        factors = []
        for half in range(2):
            whole = packed([row[s][half] for s in range(8)])
            beyond = lanes + 128 * half >= 8 * p + 8
            strip = jnp.where(beyond, 0.0, whole * scale)
            out_ref[pl.ds(8 * (p - first), 8), 128 * half : min(128 * half + 128, size)] = strip[
                :, : min(128, size - 128 * half)
            ]
            factors.append(jnp.where(beyond, whole * inverses, 0.0).T)
        factor = jnp.concatenate(factors, 0)[8 * first : size]
        spread = lambda x: jnp.tile(x, (tall // 8, 1))
        after = rows_at >= 8 * p + 8
        for half in range(2):
            place = (slice(8 * first, size), slice(128 * half, 128 * half + 128))
            rest = work_ref[place]
            if half == side:
                rest = jnp.where(spread(own) & after, 0.0, rest)
            for s in range(8):
                rest = rest - jnp.broadcast_to(factor[:, s : s + 1], (tall, 128)) * spread(row[s][half])
            work_ref[place] = rest
        return 0

    lax.fori_loop(first, first + out_ref.shape[0] // 8, panel, 0)


def invert_panels(first, size, work, ids, base, grams):
    tall = min(64, size - 8 * first)
    whole = pl.BlockSpec(memory_space=pltpu.VMEM)
    counts = [] if grams is None else [gram.shape[0] for gram in grams]
    if grams is None:
        operands, in_specs, scratch = [work], [whole], []
    else:
        operands = [ids, *grams]
        in_specs = [pl.BlockSpec(memory_space=pltpu.SMEM)] + [whole] * len(grams)
        scratch = [pltpu.VMEM((sum(counts), size, size), jnp.float32)]
    return pl.pallas_call(
        functools.partial(invert_kernel, counts, base, first),
        out_shape=[
            jax.ShapeDtypeStruct((size, 256), jnp.float32),
            jax.ShapeDtypeStruct((tall, size), jnp.float32),
        ],
        in_specs=in_specs,
        out_specs=[whole] * 2,
        scratch_shapes=scratch,
        input_output_aliases={} if counts else {0: 0},
        compiler_params=pltpu.CompilerParams(vmem_limit_bytes=32 * MIB),
        cost_estimate=pl.CostEstimate(flops=10**9, bytes_accessed=2 * 10**7, transcendentals=0),
    )(*operands)


def rows_kernel(half, base, pieces, spans, chained, with_gram, ids_ref, weight_ref, *refs):
    refs = list(refs)
    piece_refs = [refs.pop(0) for _ in range(pieces)]
    before_ref = refs.pop(0) if chained else None
    out_ref = refs.pop(0)
    gram_ref = refs.pop(0) if with_gram else None
    held_ref, ready_ref, sems = refs
    halves = piece_refs[0].shape[1] // half
    turns = pieces * halves
    chunk = 2 * half
    blocks = []
    for number, (low, tall) in enumerate(spans):
        blocks.append([])
        for at in range(turns // 2):
            start = ids_ref[base + 2 * at] // 2 * chunk
            blocks[-1].append(
                pltpu.make_async_copy(
                    weight_ref.at[pl.ds(low, tall), pl.ds(pl.multiple_of(start, 128), chunk)],
                    held_ref.at[pl.ds(low, tall), pl.ds(at * chunk, chunk)],
                    sems.at[number, at],
                )
            )
    onto = (((1,), (1,)), ((), ()))

    grams = []
    if with_gram:
        slots = gram_ref.shape[0]
        grams = [range(2 * slot, 2 * slot + 2) for slot in range(slots)]

    def piece(turn):
        at = turn % halves * half
        return piece_refs[turn // halves][:, at : at + half]

    def prepare():
        for turn in range(turns):
            at = turn // 2 * chunk + ids_ref[base + turn] % 2 * half
            ready_ref[:, pl.ds(pl.multiple_of(at, 128), half)] = piece(turn)

    def work(number):
        span = pl.ds(*spans[number])
        part = lax.dot_general(
            ready_ref[...], held_ref[span, :], onto, preferred_element_type=jnp.float32
        )
        if chained:
            part = before_ref[:, span] + part
        out_ref[:, span] = part.astype(out_ref.dtype)
        if 0 < number <= len(grams):
            squares = [
                lax.dot_general(piece(turn), piece(turn), onto, preferred_element_type=jnp.float32)
                for turn in grams[number - 1]
            ]
            gram_ref[number - 1] = sum(squares[1:], squares[0])

    in_turn(blocks, 2, work, prepare)


def row_products(weight, pieces, ids, base, half, before, narrow, with_gram):
    rows, wide = weight.shape[0], pieces[0].shape[0]
    turns = len(pieces) * (pieces[0].shape[1] // half)
    spans, low = [], 0
    while low < rows:
        size = min(256 if low == 0 else 512 if turns > 2 else 1024, rows - low)
        spans.append((low, size))
        low += size
    whole = pl.BlockSpec(memory_space=pltpu.VMEM)
    operands = [ids, weight, *pieces]
    in_specs = [pl.BlockSpec(memory_space=pltpu.SMEM), pl.BlockSpec(memory_space=pl.ANY)]
    in_specs += [whole] * len(pieces)
    if before is not None:
        in_specs.append(whole)
        operands.append(before)
    out_shape = [jax.ShapeDtypeStruct((wide, rows), jnp.bfloat16 if narrow else jnp.float32)]
    if with_gram:
        out_shape.append(jax.ShapeDtypeStruct((max(1, turns // 2), wide, wide), jnp.float32))
    depth = turns * half
    return pl.pallas_call(
        functools.partial(
            rows_kernel, half, base, len(pieces), spans, before is not None, with_gram
        ),
        out_shape=out_shape,
        in_specs=in_specs,
        out_specs=[whole] * len(out_shape),
        scratch_shapes=[
            pltpu.VMEM((rows, depth), jnp.bfloat16),
            pltpu.VMEM((wide, depth), jnp.bfloat16),
            pltpu.SemaphoreType.DMA((len(spans), turns // 2)),
        ],
        input_output_aliases={len(operands) - 1: 0} if before is not None and not narrow else {},
        compiler_params=pltpu.CompilerParams(vmem_limit_bytes=40 * MIB),
        cost_estimate=pl.CostEstimate(
            flops=2 * rows * wide * turns * half,
            bytes_accessed=2 * rows * turns * half + 8 * rows * wide,
            transcendentals=0,
        ),
    )(*operands)


def ring_sum(ring, ids, left, weight, half):
    got = None
    for k in range(ring.far, 0, -1):
        keep, give = column_sums(left, weight, ids, ring.width["sum", k], half, True)
        given = lax.ppermute(give, "row", ring.pair)
        if got is not None:
            got = got.astype(jnp.float32)
            size = got.shape[1]
            if size < keep.shape[1]:
                keep = jnp.concatenate([keep[:, :size] + got, keep[:, size:]], 1)
            else:
                keep = keep + got
            keep, given = lax.optimization_barrier((keep, given))
        total = (keep + given.astype(jnp.float32)).astype(jnp.bfloat16)
        total, left = lax.optimization_barrier((total, left))
        got = lax.ppermute(total, "row", ring.ahead)
    (keep,) = column_sums(left, weight, ids, ring.width["sum", 0], half, False)
    mine = keep + got.astype(jnp.float32)
    other = lax.ppermute(mine, "row", ring.pair)
    return mine + jnp.concatenate([other[:, half:], other[:, :half]], 1)


def ring_apply(ring, ids, chunk, weight, half, narrow, with_gram):
    grams, before = [], None
    moving = chunk
    for k in range(ring.far + 1):
        if k == 0:
            pieces = [chunk]
        else:
            moving = lax.ppermute(moving if k < ring.far else moving[:, :half], "row", ring.ahead)
            moving, before = lax.optimization_barrier((moving, before))
            pieces = [moving, lax.ppermute(moving, "row", ring.pair)]
        last = k == ring.far
        before, *gram = row_products(
            weight, pieces, ids, ring.width["use", k][0], half, before, narrow and last, with_gram
        )
        grams += gram
    return before, grams


def sum_beside_inverse(value, ring, ids, grams):
    size = value.shape[0]
    rows = size // 2
    first = lax.axis_index("row") % 2 == 0
    low, high = value[:rows], value[rows:]
    part = jnp.where(first, low, high)
    part = part + lax.ppermute(jnp.where(first, high, low), "row", ring.pair)
    part, grams = lax.optimization_barrier((part, grams))
    hops = [
        [(device, device ^ (2 << bit)) for device in range(2 * ring.chips)]
        for bit in reversed(range(ring.chips.bit_length() - 1))
    ]
    panels = list(range(0, size // 8, 8))
    work, strips = None, []
    for at in range(max(len(hops), len(panels))):
        if at < len(hops):
            got = lax.ppermute(part, "row", hops[at])
        if at < len(panels):
            given = grams if at == 0 else None
            base = ring.width["arrival"][0]
            work, strip = invert_panels(panels[at], size, work, ids, base, given)
            strips.append(strip)
        if at < len(hops):
            got, work = lax.optimization_barrier((got, work))
            part = part + got
    other = lax.ppermute(part, "row", ring.pair)
    total = jnp.concatenate([jnp.where(first, part, other), jnp.where(first, other, part)], 0)
    return total, jnp.concatenate(strips, 0)


def ring_body(ring, weight, test_matrix, rank_mask):
    highest = lax.Precision.HIGHEST
    rows, features = weight.shape
    half = features // (2 * ring.chips)
    ids = ring.row()
    picker = selector(rank_mask, RANK)
    sketch = ring_sum(ring, ids, test_matrix.T, weight, half).astype(jnp.bfloat16)
    mixed, _ = ring_apply(ring, ids, sketch, weight, half, True, False)
    powered = ring_sum(ring, ids, mixed, weight, half)
    image, grams = ring_apply(
        ring, ids, powered.astype(jnp.bfloat16), weight, half, False, True
    )
    image_b = image.astype(jnp.bfloat16)
    square = lax.dot_general(
        image_b, image_b, (((1,), (1,)), ((), ())), preferred_element_type=jnp.float32
    )
    square, inverse = sum_beside_inverse(square, ring, ids, grams)
    change = lax.dot_general(inverse, picker, (((0,), (0,)), ((), ())), precision=highest)
    own = powered[:, :half]
    left_factor = lax.dot_general(
        own, change, (((0,), (0,)), ((), ())), precision=highest
    ) * math.sqrt(features)
    energy = jnp.sum(square * jnp.dot(change, change.T, precision=highest))
    spread = jnp.sqrt(energy / (rows * 2 * ring.chips * RANK) + 1e-06)
    projected = lax.dot_general(
        image, change, (((0,), (0,)), ((), ())), precision=lax.Precision.HIGH
    )
    right_factor = (projected / spread).astype(jnp.bfloat16)
    return (left_factor, right_factor, spread.reshape(1))


def body(weight, test_matrix, rank_mask):
    members = lax.axis_size("row")
    chips = members // 2
    paired = members % 2 == 0 and chips > 2 and chips & (chips - 1) == 0
    if not paired or weight.shape[1] % (members * 128):
        return plain_body(weight, test_matrix, rank_mask)
    return ring_body(Ring(members), weight, test_matrix, rank_mask)


def solution(mesh):
    in_specs = (P(("groups", "row"), None), P("row", None), P("groups"))
    out_specs = (P(("groups", "row"), None), P(("groups", "row"), None), P("groups"))
    return jax.shard_map(body, mesh=mesh, in_specs=in_specs, out_specs=out_specs, check_vma=False)
```

```python
import functools
import math

import jax
import jax.numpy as jnp
import numpy as np
from jax import lax
from jax.experimental import pallas as pl
from jax.experimental.pallas import tpu as pltpu
from jax.sharding import PartitionSpec as P

RANK = 224
MIB = 1024 * 1024


def selector(rank_mask, kept):
    positions = jnp.cumsum(rank_mask) - 1
    targets = lax.iota(jnp.int32, kept)
    matches = (rank_mask[:, None] == 1) & (positions[:, None] == targets[None, :])
    return matches.astype(jnp.float32)


def plain_body(weight, test_matrix, rank_mask):
    across = (((0,), (0,)), ((), ()))
    members = lax.axis_size("row")
    picker = selector(rank_mask, RANK)
    sketch_part = lax.psum_scatter(
        lax.dot_general(weight, test_matrix, across, preferred_element_type=jnp.float32),
        "row",
        scatter_dimension=0,
        tiled=True,
    ).astype(jnp.bfloat16)

    def add_rows(piece_rows):
        return jnp.dot(weight, piece_rows, preferred_element_type=jnp.float32)

    mixed = add_rows(lax.all_gather(sketch_part, "row", axis=0, tiled=True)).astype(jnp.bfloat16)
    powered = lax.psum_scatter(
        lax.dot_general(weight, mixed, across, preferred_element_type=jnp.float32),
        "row",
        scatter_dimension=0,
        tiled=True,
    )
    local_gram = lax.dot_general(powered, powered, across, precision=lax.Precision.HIGHEST)
    gram_matrix = lax.psum(local_gram, "row")
    cholesky_factor = jnp.linalg.cholesky(gram_matrix)
    ortho_basis = lax.linalg.triangular_solve(
        cholesky_factor, powered, left_side=False, lower=True, transpose_a=True
    )
    own_chosen = jnp.dot(ortho_basis, picker, precision=lax.Precision.HIGHEST)
    projected = add_rows(lax.all_gather(own_chosen.astype(jnp.bfloat16), "row", axis=0, tiled=True))
    left_factor = own_chosen * math.sqrt(weight.shape[1])
    energy = lax.psum(jnp.sum(projected * projected), "row")
    spread = jnp.sqrt(energy / (weight.shape[0] * members * RANK) + 1e-06)
    right_factor = (projected / spread).astype(jnp.bfloat16)
    return (left_factor, right_factor, spread.reshape(1))


class Ring:
    def __init__(self, members):
        chips = members // 2
        order = list(range(0, chips, 2)) + list(range(chips - 1, 0, -2))
        place = {chip: at for at, chip in enumerate(order)}
        self.chips, self.far = chips, chips // 2
        self.pair = [(device, device ^ 1) for device in range(members)]
        self.ahead = []
        for at, chip in enumerate(order):
            self.ahead.append((2 * chip, 2 * order[(at + 1) % chips]))
            self.ahead.append((2 * chip + 1, 2 * order[at - 1] + 1))

        def halves(device, steps, core):
            at = place[device // 2] + (steps if device % 2 == 0 else -steps)
            chip = order[at % chips]
            return [2 * chip + core, 2 * chip + 1 - core]

        self.width, self.table = {}, []
        for device in range(members):
            core, row = device % 2, []

            def put(name, values):
                self.width[name] = (len(row), len(values))
                row.extend(values)

            for k in range(self.far + 1):
                one = k == self.far
                mine, other = halves(device, k, core), halves(device, -k, 1 - core)
                put(("sum", k), mine if k == 0 else (mine[:1] + other[:1] if one else mine + other))
                mine, other = halves(device, -k, core), halves(device, k, 1 - core)
                put(("use", k), mine if k == 0 else (mine[:1] + other[:1] if one else mine + other))
            arrival = [device // 2]
            for k in range(1, self.far):
                arrival += [halves(device, -k, core)[0] // 2, halves(device, k, core)[0] // 2]
            arrival.append(halves(device, self.far, core)[0] // 2)
            put("arrival", [arrival.index(chip) for chip in range(chips)])
            self.table.append(row)

    def first(self, weight, name, k):
        half = weight.shape[1] // (2 * self.chips)
        base, turns = self.width[name, k]
        return First(weight.shape[0], half, base, turns, name == "use")

    def row(self):
        table = jnp.asarray(np.array(self.table, np.int32))
        return lax.dynamic_index_in_dim(table, lax.axis_index("row"), 0, keepdims=False)


class First:
    def __init__(self, rows, half, base, turns, by_rows):
        self.half, self.base, self.turns, self.by_rows = half, base, turns, by_rows
        self.tall = min(1024, rows) if by_rows else rows
        self.shape = (self.tall, turns * half) if by_rows else (rows, half)

    def copies(self, ids_ref, weight_ref, target_ref, sems):
        if not self.by_rows:
            start = pl.multiple_of(ids_ref[self.base] * self.half, 128)
            source = weight_ref.at[:, pl.ds(start, self.half)]
            return [pltpu.make_async_copy(source, target_ref, sems.at[0])]
        target = [target_ref.at[:, pl.ds(at * 2 * self.half, 2 * self.half)] for at in range(self.turns // 2)]
        return self.strips(ids_ref, weight_ref, 0, self.tall, target, sems)

    def strips(self, ids_ref, weight_ref, low, tall, targets, sems):
        chunk = 2 * self.half
        starts = [ids_ref[self.base + 2 * at] // 2 * chunk for at in range(len(targets))]
        return [
            pltpu.make_async_copy(
                weight_ref.at[pl.ds(low, tall), pl.ds(pl.multiple_of(start, 128), chunk)],
                target,
                sems.at[at],
            )
            for at, (start, target) in enumerate(zip(starts, targets))
        ]


def in_turn(blocks, ahead, work, prepare=None):
    for block in blocks[: ahead + 1]:
        for copy in block:
            copy.start()
    if prepare is not None:
        prepare()
    for at, block in enumerate(blocks):
        for copy in block:
            copy.wait()
        if at > 0 and at + ahead < len(blocks):
            for copy in blocks[at + ahead]:
                copy.start()
        work(at)


def columns_kernel(first, following, turns, kept, carried, ids_ref, left_ref, weight_ref, *refs):
    refs = list(refs)
    half = first.half
    sems, held_ref = refs.pop(), refs.pop()
    ready_ref = refs.pop(0) if carried else held_ref.at[turns - 1]
    next_ref = refs.pop() if following is not None else None
    blocks = [[] if carried else first.copies(ids_ref, weight_ref, ready_ref, sems.at[0])]
    for turn in range(1, turns):
        start = pl.multiple_of(ids_ref[first.base + turn] * half, 128)
        source = weight_ref.at[:, pl.ds(start, half)]
        blocks.append([pltpu.make_async_copy(source, held_ref.at[turn - 1], sems.at[turn, 0])])
    if following is not None:
        blocks.append(following.copies(ids_ref, weight_ref, next_ref, sems.at[turns]))

    def work(turn):
        if turn == turns:
            return
        block = ready_ref[...] if turn == 0 else held_ref[turn - 1]
        part = jnp.dot(left_ref[...], block, preferred_element_type=jnp.float32)
        out, at = (0, turn) if turn < kept else (1, turn - kept)
        refs[out][:, at * half : (at + 1) * half] = part.astype(refs[out].dtype)

    in_turn(blocks, 2, work)


def column_sums(left, weight, ids, first, half, split, carry, following):
    rows, wide = left.shape[1], left.shape[0]
    turns = first.turns
    kept = turns // 2 if split else turns
    out_shape = [jax.ShapeDtypeStruct((wide, kept * half), jnp.float32)]
    if split:
        out_shape.append(jax.ShapeDtypeStruct((wide, kept * half), jnp.bfloat16))
    if following is not None:
        out_shape.append(jax.ShapeDtypeStruct(following.shape, jnp.bfloat16))
    whole = pl.BlockSpec(memory_space=pltpu.VMEM)
    carried = carry is not None
    return pl.pallas_call(
        functools.partial(columns_kernel, first, following, turns, kept, carried),
        out_shape=out_shape,
        in_specs=[
            pl.BlockSpec(memory_space=pltpu.SMEM),
            whole,
            pl.BlockSpec(memory_space=pl.ANY),
        ]
        + [whole] * carried,
        out_specs=[whole] * len(out_shape),
        scratch_shapes=[
            pltpu.VMEM((turns - carried, rows, half), jnp.bfloat16),
            pltpu.SemaphoreType.DMA((turns + 1, 2)),
        ],
        compiler_params=pltpu.CompilerParams(vmem_limit_bytes=40 * MIB),
        cost_estimate=pl.CostEstimate(
            flops=2 * wide * rows * turns * half,
            bytes_accessed=2 * rows * turns * half + 2 * rows * wide,
            transcendentals=0,
        ),
    )(ids, left, weight, *([carry] if carried else []))


def invert_kernel(counts, base, first, *refs):
    refs = list(refs)
    lanes = lax.broadcasted_iota(jnp.int32, (8, 128), 1)
    if counts:
        order_ref = refs.pop(0)
        grams = [refs.pop(0) for _ in counts]
        work_ref, out_ref, all_ref = refs
        size = work_ref.shape[0]
        at = 0
        for ref, count in zip(grams, counts):
            all_ref[at : at + count] = ref[...]
            at += count
        total = all_ref[order_ref[base]]
        for chip in range(1, at):
            total = total + all_ref[order_ref[base + chip]]
        work_ref[...] = jnp.zeros_like(work_ref)
        work_ref[:, :size] = total
    else:
        before_ref, work_ref, out_ref = refs
        size = work_ref.shape[0]
        work_ref[...] = before_ref[...]
    side = first // 16
    tall = size - 8 * first

    rows_at = 8 * first + lax.broadcasted_iota(jnp.int32, (tall, 128), 0)
    inside = lax.broadcasted_iota(jnp.int32, (8, 128), 0)

    def packed(values):
        total = values[0]
        for s in range(1, 8):
            total = jnp.where(inside == s, values[s], total)
        return total

    def panel(p, _):
        raw = [work_ref[pl.ds(8 * p, 8), :128], work_ref[pl.ds(8 * p, 8), 128:]]
        entry, ratio, inverse = {}, {}, []
        for s in range(8):
            at = jnp.full((8, 128), 8 * p + s - 128 * side, jnp.int32)
            column = jnp.take_along_axis(raw[side], at, axis=1)
            for r in range(s + 1):
                entry[r, s] = jnp.broadcast_to(column[r : r + 1], (8, 128))
        for s in range(8):
            inverse.append(1.0 / entry[s, s])
            for t in range(s + 1, 8):
                ratio[t, s] = entry[s, t] * inverse[s]
            for t in range(s + 1, 8):
                for u in range(t, 8):
                    entry[t, u] = entry[t, u] - ratio[t, s] * entry[s, u]
        low = 8 * p - 128 * side
        own = (lanes >= low) & (lanes < low + 8)
        row = []
        for t in range(8):
            halves = [jnp.broadcast_to(part[t : t + 1], (8, 128)) for part in raw]
            unit = jnp.where(lanes == low + t, 1.0, 0.0)
            halves[side] = jnp.where(own, unit, halves[side])
            for s in range(t):
                halves = [half - ratio[t, s] * done for half, done in zip(halves, row[s])]
            row.append(halves)
        scale = lax.rsqrt(packed([entry[s, s] for s in range(8)]))
        inverses = packed(inverse)
        factors = []
        for half in range(2):
            whole = packed([row[s][half] for s in range(8)])
            beyond = lanes + 128 * half >= 8 * p + 8
            strip = jnp.where(beyond, 0.0, whole * scale)
            out_ref[pl.ds(8 * (p - first), 8), 128 * half : min(128 * half + 128, size)] = strip[
                :, : min(128, size - 128 * half)
            ]
            factors.append(jnp.where(beyond, whole * inverses, 0.0).T)
        factor = jnp.concatenate(factors, 0)[8 * first : size]
        spread = lambda x: jnp.tile(x, (tall // 8, 1))
        after = rows_at >= 8 * p + 8
        for half in range(2):
            place = (slice(8 * first, size), slice(128 * half, 128 * half + 128))
            rest = work_ref[place]
            if half == side:
                rest = jnp.where(spread(own) & after, 0.0, rest)
            for s in range(8):
                rest = rest - jnp.broadcast_to(factor[:, s : s + 1], (tall, 128)) * spread(row[s][half])
            work_ref[place] = rest
        return 0

    lax.fori_loop(first, first + out_ref.shape[0] // 8, panel, 0)


def invert_panels(first, size, work, ids, base, grams):
    tall = min(64, size - 8 * first)
    whole = pl.BlockSpec(memory_space=pltpu.VMEM)
    counts = [] if grams is None else [gram.shape[0] for gram in grams]
    if grams is None:
        operands, in_specs, scratch = [work], [whole], []
    else:
        operands = [ids, *grams]
        in_specs = [pl.BlockSpec(memory_space=pltpu.SMEM)] + [whole] * len(grams)
        scratch = [pltpu.VMEM((sum(counts), size, size), jnp.float32)]
    return pl.pallas_call(
        functools.partial(invert_kernel, counts, base, first),
        out_shape=[
            jax.ShapeDtypeStruct((size, 256), jnp.float32),
            jax.ShapeDtypeStruct((tall, size), jnp.float32),
        ],
        in_specs=in_specs,
        out_specs=[whole] * 2,
        scratch_shapes=scratch,
        input_output_aliases={} if counts else {0: 0},
        compiler_params=pltpu.CompilerParams(vmem_limit_bytes=32 * MIB),
        cost_estimate=pl.CostEstimate(flops=10**9, bytes_accessed=2 * 10**7, transcendentals=0),
    )(*operands)


def rows_kernel(first, following, pieces, spans, chained, with_gram, ids_ref, weight_ref, *refs):
    refs = list(refs)
    ready_ref = refs.pop(0)
    piece_refs = [refs.pop(0) for _ in range(pieces)]
    before_ref = refs.pop(0) if chained else None
    out_ref = refs.pop(0)
    gram_ref = refs.pop(0) if with_gram else None
    next_ref = refs.pop(0) if following is not None else None
    held_ref, joined_ref, sems = refs
    half, turns = first.half, first.turns
    halves = turns // pieces
    chunk = 2 * half
    blocks = [[]]
    for number, (low, tall) in enumerate(spans[1:], 1):
        place = pl.ds(low - first.tall, tall)
        targets = [held_ref.at[place, pl.ds(at * chunk, chunk)] for at in range(turns // 2)]
        blocks.append(first.strips(ids_ref, weight_ref, low, tall, targets, sems.at[number]))
    if following is not None:
        blocks.append(following.copies(ids_ref, weight_ref, next_ref, sems.at[0]))
    onto = (((1,), (1,)), ((), ()))
    grams = []
    if with_gram:
        grams = [range(2 * slot, 2 * slot + 2) for slot in range(gram_ref.shape[0])]

    def piece(turn):
        at = turn % halves * half
        return piece_refs[turn // halves][:, at : at + half]

    def prepare():
        for turn in range(turns):
            at = turn // 2 * chunk + ids_ref[first.base + turn] % 2 * half
            joined_ref[:, pl.ds(pl.multiple_of(at, 128), half)] = piece(turn)

    def work(number):
        if number == len(spans):
            return
        low, tall = spans[number]
        block = held_ref[low - first.tall : low - first.tall + tall, :] if number else ready_ref[...]
        part = lax.dot_general(joined_ref[...], block, onto, preferred_element_type=jnp.float32)
        if chained:
            part = before_ref[:, low : low + tall] + part
        out_ref[:, low : low + tall] = part.astype(out_ref.dtype)
        if 0 < number <= len(grams):
            squares = [
                lax.dot_general(piece(turn), piece(turn), onto, preferred_element_type=jnp.float32)
                for turn in grams[number - 1]
            ]
            gram_ref[number - 1] = sum(squares[1:], squares[0])

    in_turn(blocks, 2, work, prepare)


def row_products(weight, pieces, ids, first, before, narrow, with_gram, carry, following):
    rows, wide = weight.shape[0], pieces[0].shape[0]
    turns, half = first.turns, first.half
    spans, low = [(0, first.tall)], first.tall
    while low < rows:
        size = min(512 if turns > 2 else 1024, rows - low)
        spans.append((low, size))
        low += size
    whole = pl.BlockSpec(memory_space=pltpu.VMEM)
    operands = [ids, weight, carry, *pieces]
    in_specs = [pl.BlockSpec(memory_space=pltpu.SMEM), pl.BlockSpec(memory_space=pl.ANY), whole]
    in_specs += [whole] * len(pieces)
    if before is not None:
        in_specs.append(whole)
        operands.append(before)
    out_shape = [jax.ShapeDtypeStruct((wide, rows), jnp.bfloat16 if narrow else jnp.float32)]
    if with_gram:
        out_shape.append(jax.ShapeDtypeStruct((turns // 2, wide, wide), jnp.float32))
    if following is not None:
        out_shape.append(jax.ShapeDtypeStruct(following.shape, jnp.bfloat16))
    depth = turns * half
    return pl.pallas_call(
        functools.partial(
            rows_kernel, first, following, len(pieces), spans, before is not None, with_gram
        ),
        out_shape=out_shape,
        in_specs=in_specs,
        out_specs=[whole] * len(out_shape),
        scratch_shapes=[
            pltpu.VMEM((max(rows - first.tall, 16), depth), jnp.bfloat16),
            pltpu.VMEM((wide, depth), jnp.bfloat16),
            pltpu.SemaphoreType.DMA((len(spans) + 1, 2)),
        ],
        input_output_aliases={len(operands) - 1: 0} if before is not None and not narrow else {},
        compiler_params=pltpu.CompilerParams(vmem_limit_bytes=40 * MIB),
        cost_estimate=pl.CostEstimate(
            flops=2 * rows * wide * turns * half,
            bytes_accessed=2 * rows * turns * half + 8 * rows * wide,
            transcendentals=0,
        ),
    )(*operands)


def ring_sum(ring, ids, left, weight, half, carry):
    got = None
    for k in range(ring.far, 0, -1):
        first = ring.first(weight, "sum", k)
        keep, give, carry = column_sums(
            left, weight, ids, first, half, True, carry, ring.first(weight, "sum", k - 1)
        )
        given = lax.ppermute(give, "row", ring.pair)
        if got is not None:
            got = got.astype(jnp.float32)
            size = got.shape[1]
            if size < keep.shape[1]:
                keep = jnp.concatenate([keep[:, :size] + got, keep[:, size:]], 1)
            else:
                keep = keep + got
            keep, given = lax.optimization_barrier((keep, given))
        total = (keep + given.astype(jnp.float32)).astype(jnp.bfloat16)
        total, left = lax.optimization_barrier((total, left))
        got = lax.ppermute(total, "row", ring.ahead)
    first = ring.first(weight, "sum", 0)
    keep, carry = column_sums(
        left, weight, ids, first, half, False, carry, ring.first(weight, "use", 0)
    )
    mine = keep + got.astype(jnp.float32)
    other = lax.ppermute(mine, "row", ring.pair)
    return mine + jnp.concatenate([other[:, half:], other[:, :half]], 1), carry


def ring_apply(ring, ids, chunk, weight, half, narrow, with_gram, carry, following):
    grams, before = [], None
    moving = chunk
    for k in range(ring.far + 1):
        if k == 0:
            pieces = [chunk]
        else:
            moving = lax.ppermute(moving if k < ring.far else moving[:, :half], "row", ring.ahead)
            moving, before = lax.optimization_barrier((moving, before))
            pieces = [moving, lax.ppermute(moving, "row", ring.pair)]
        last = k == ring.far
        then = following if last else ring.first(weight, "use", k + 1)
        outs = row_products(
            weight,
            pieces,
            ids,
            ring.first(weight, "use", k),
            before,
            narrow and last,
            with_gram,
            carry,
            then,
        )
        outs = list(outs)
        carry = outs.pop() if then is not None else None
        before = outs.pop(0)
        grams += outs
    return before, grams, carry


def sum_beside_inverse(value, ring, ids, grams):
    size = value.shape[0]
    rows = size // 2
    first = lax.axis_index("row") % 2 == 0
    low, high = value[:rows], value[rows:]
    part = jnp.where(first, low, high)
    part = part + lax.ppermute(jnp.where(first, high, low), "row", ring.pair)
    part, ids = lax.optimization_barrier((part, ids))
    hops = [
        [(device, device ^ (2 << bit)) for device in range(2 * ring.chips)]
        for bit in reversed(range(ring.chips.bit_length() - 1))
    ]
    panels = list(range(0, size // 8, 8))
    work, strips = None, []
    for at in range(max(len(hops), len(panels))):
        if at < len(hops):
            got = lax.ppermute(part, "row", hops[at])
        if at < len(panels):
            given = grams if at == 0 else None
            base = ring.width["arrival"][0]
            work, strip = invert_panels(panels[at], size, work, ids, base, given)
            strips.append(strip)
        if at < len(hops):
            got, work = lax.optimization_barrier((got, work))
            part = part + got
    other = lax.ppermute(part, "row", ring.pair)
    total = jnp.concatenate([jnp.where(first, part, other), jnp.where(first, other, part)], 0)
    return total, jnp.concatenate(strips, 0)


def ring_body(ring, weight, test_matrix, rank_mask):
    highest = lax.Precision.HIGHEST
    rows, features = weight.shape
    half = features // (2 * ring.chips)
    ids = ring.row()
    picker = selector(rank_mask, RANK)
    sketch, carry = ring_sum(ring, ids, test_matrix.T, weight, half, None)
    sketch = sketch.astype(jnp.bfloat16)
    again = ring.first(weight, "sum", ring.far)
    mixed, _, carry = ring_apply(ring, ids, sketch, weight, half, True, False, carry, again)
    powered, carry = ring_sum(ring, ids, mixed, weight, half, carry)
    powered_b = powered.astype(jnp.bfloat16)
    image, grams, _ = ring_apply(ring, ids, powered_b, weight, half, False, True, carry, None)
    image_b = image.astype(jnp.bfloat16)
    square = lax.dot_general(
        image_b, image_b, (((1,), (1,)), ((), ())), preferred_element_type=jnp.float32
    )
    square, inverse = sum_beside_inverse(square, ring, ids, grams)
    change = lax.dot_general(inverse, picker, (((0,), (0,)), ((), ())), precision=highest)
    own = powered[:, :half]
    left_factor = lax.dot_general(
        own, change, (((0,), (0,)), ((), ())), precision=highest
    ) * math.sqrt(features)
    energy = jnp.sum(square * jnp.dot(change, change.T, precision=highest))
    spread = jnp.sqrt(energy / (rows * 2 * ring.chips * RANK) + 1e-06)
    projected = lax.dot_general(
        image, change, (((0,), (0,)), ((), ())), precision=lax.Precision.HIGH
    )
    right_factor = (projected / spread).astype(jnp.bfloat16)
    return (left_factor, right_factor, spread.reshape(1))


def body(weight, test_matrix, rank_mask):
    members = lax.axis_size("row")
    chips = members // 2
    paired = members % 2 == 0 and chips > 2 and chips & (chips - 1) == 0
    if not paired or weight.shape[1] % (members * 128):
        return plain_body(weight, test_matrix, rank_mask)
    return ring_body(Ring(members), weight, test_matrix, rank_mask)


def solution(mesh):
    in_specs = (P(("groups", "row"), None), P("row", None), P("groups"))
    out_specs = (P(("groups", "row"), None), P(("groups", "row"), None), P("groups"))
    return jax.shard_map(body, mesh=mesh, in_specs=in_specs, out_specs=out_specs, check_vma=False)
```

```python
import functools
import math

import jax
import jax.numpy as jnp
import numpy as np
from jax import lax
from jax.experimental import pallas as pl
from jax.experimental.pallas import tpu as pltpu
from jax.sharding import PartitionSpec as P

RANK = 224
MIB = 1024 * 1024


def selector(rank_mask, kept):
    positions = jnp.cumsum(rank_mask) - 1
    targets = lax.iota(jnp.int32, kept)
    matches = (rank_mask[:, None] == 1) & (positions[:, None] == targets[None, :])
    return matches.astype(jnp.float32)


def plain_body(weight, test_matrix, rank_mask):
    across = (((0,), (0,)), ((), ()))
    members = lax.axis_size("row")
    picker = selector(rank_mask, RANK)
    sketch_part = lax.psum_scatter(
        lax.dot_general(weight, test_matrix, across, preferred_element_type=jnp.float32),
        "row",
        scatter_dimension=0,
        tiled=True,
    ).astype(jnp.bfloat16)

    def add_rows(piece_rows):
        return jnp.dot(weight, piece_rows, preferred_element_type=jnp.float32)

    mixed = add_rows(lax.all_gather(sketch_part, "row", axis=0, tiled=True)).astype(jnp.bfloat16)
    powered = lax.psum_scatter(
        lax.dot_general(weight, mixed, across, preferred_element_type=jnp.float32),
        "row",
        scatter_dimension=0,
        tiled=True,
    )
    local_gram = lax.dot_general(powered, powered, across, precision=lax.Precision.HIGHEST)
    gram_matrix = lax.psum(local_gram, "row")
    cholesky_factor = jnp.linalg.cholesky(gram_matrix)
    ortho_basis = lax.linalg.triangular_solve(
        cholesky_factor, powered, left_side=False, lower=True, transpose_a=True
    )
    own_chosen = jnp.dot(ortho_basis, picker, precision=lax.Precision.HIGHEST)
    projected = add_rows(lax.all_gather(own_chosen.astype(jnp.bfloat16), "row", axis=0, tiled=True))
    left_factor = own_chosen * math.sqrt(weight.shape[1])
    energy = lax.psum(jnp.sum(projected * projected), "row")
    spread = jnp.sqrt(energy / (weight.shape[0] * members * RANK) + 1e-06)
    right_factor = (projected / spread).astype(jnp.bfloat16)
    return (left_factor, right_factor, spread.reshape(1))


class Ring:
    def __init__(self, members):
        chips = members // 2
        order = list(range(0, chips, 2)) + list(range(chips - 1, 0, -2))
        place = {chip: at for at, chip in enumerate(order)}
        self.chips, self.far = chips, chips // 2
        self.pair = [(device, device ^ 1) for device in range(members)]
        self.ahead = []
        for at, chip in enumerate(order):
            self.ahead.append((2 * chip, 2 * order[(at + 1) % chips]))
            self.ahead.append((2 * chip + 1, 2 * order[at - 1] + 1))

        def halves(device, steps, core):
            at = place[device // 2] + (steps if device % 2 == 0 else -steps)
            chip = order[at % chips]
            return [2 * chip + core, 2 * chip + 1 - core]

        self.width, self.table = {}, []
        for device in range(members):
            core, row = device % 2, []

            def put(name, values):
                self.width[name] = (len(row), len(values))
                row.extend(values)

            for k in range(self.far + 1):
                one = k == self.far
                mine, other = halves(device, k, core), halves(device, -k, 1 - core)
                put(("sum", k), mine if k == 0 else (mine[:1] + other[:1] if one else mine + other))
                mine, other = halves(device, -k, core), halves(device, k, 1 - core)
                put(("use", k), mine if k == 0 else (mine[:1] + other[:1] if one else mine + other))
            self.table.append(row)

    def first(self, weight, name, k):
        half = weight.shape[1] // (2 * self.chips)
        base, turns = self.width[name, k]
        return First(weight.shape[0], half, base, turns, name == "use")

    def row(self):
        table = jnp.asarray(np.array(self.table, np.int32))
        return lax.dynamic_index_in_dim(table, lax.axis_index("row"), 0, keepdims=False)


class First:
    def __init__(self, rows, half, base, turns, by_rows):
        self.half, self.base, self.turns, self.by_rows = half, base, turns, by_rows
        self.tall = rows // 4 if by_rows and rows % 128 == 0 else rows
        self.shape = (self.tall, turns * half) if by_rows else (rows, half)

    def copies(self, ids_ref, weight_ref, target_ref, sems):
        if not self.by_rows:
            start = pl.multiple_of(ids_ref[self.base] * self.half, 128)
            source = weight_ref.at[:, pl.ds(start, self.half)]
            return [pltpu.make_async_copy(source, target_ref, sems.at[0])]
        target = [target_ref.at[:, pl.ds(at * 2 * self.half, 2 * self.half)] for at in range(self.turns // 2)]
        return self.strips(ids_ref, weight_ref, 0, self.tall, target, sems)

    def strips(self, ids_ref, weight_ref, low, tall, targets, sems):
        chunk = 2 * self.half
        starts = [ids_ref[self.base + 2 * at] // 2 * chunk for at in range(len(targets))]
        return [
            pltpu.make_async_copy(
                weight_ref.at[pl.ds(low, tall), pl.ds(pl.multiple_of(start, 128), chunk)],
                target,
                sems.at[at],
            )
            for at, (start, target) in enumerate(zip(starts, targets))
        ]


def in_turn(blocks, ahead, work, prepare=None):
    for block in blocks[: ahead + 1]:
        for copy in block:
            copy.start()
    if prepare is not None:
        prepare()
    for at, block in enumerate(blocks):
        for copy in block:
            copy.wait()
        if at > 0 and at + ahead < len(blocks):
            for copy in blocks[at + ahead]:
                copy.start()
        work(at)


def columns_kernel(first, following, turns, kept, carried, ids_ref, left_ref, weight_ref, *refs):
    refs = list(refs)
    half = first.half
    sems, held_ref = refs.pop(), refs.pop()
    ready_ref = refs.pop(0) if carried else held_ref.at[turns - 1]
    next_ref = refs.pop() if following is not None else None
    blocks = [[] if carried else first.copies(ids_ref, weight_ref, ready_ref, sems.at[0])]
    for turn in range(1, turns):
        start = pl.multiple_of(ids_ref[first.base + turn] * half, 128)
        source = weight_ref.at[:, pl.ds(start, half)]
        blocks.append([pltpu.make_async_copy(source, held_ref.at[turn - 1], sems.at[turn, 0])])
    if following is not None:
        blocks.append(following.copies(ids_ref, weight_ref, next_ref, sems.at[turns]))

    def work(turn):
        if turn == turns:
            return
        block = ready_ref[...] if turn == 0 else held_ref[turn - 1]
        part = jnp.dot(left_ref[...], block, preferred_element_type=jnp.float32)
        out, at = (0, turn) if turn < kept else (1, turn - kept)
        refs[out][:, at * half : (at + 1) * half] = part.astype(refs[out].dtype)

    in_turn(blocks, 2, work)


def column_sums(left, weight, ids, first, half, split, carry, following):
    rows, wide = left.shape[1], left.shape[0]
    turns = first.turns
    kept = turns // 2 if split else turns
    out_shape = [jax.ShapeDtypeStruct((wide, kept * half), jnp.float32)]
    if split:
        out_shape.append(jax.ShapeDtypeStruct((wide, kept * half), jnp.bfloat16))
    if following is not None:
        out_shape.append(jax.ShapeDtypeStruct(following.shape, jnp.bfloat16))
    whole = pl.BlockSpec(memory_space=pltpu.VMEM)
    carried = carry is not None
    return pl.pallas_call(
        functools.partial(columns_kernel, first, following, turns, kept, carried),
        out_shape=out_shape,
        in_specs=[
            pl.BlockSpec(memory_space=pltpu.SMEM),
            whole,
            pl.BlockSpec(memory_space=pl.ANY),
        ]
        + [whole] * carried,
        out_specs=[whole] * len(out_shape),
        scratch_shapes=[
            pltpu.VMEM((turns - carried, rows, half), jnp.bfloat16),
            pltpu.SemaphoreType.DMA((turns + 1, 2)),
        ],
        compiler_params=pltpu.CompilerParams(vmem_limit_bytes=40 * MIB),
        cost_estimate=pl.CostEstimate(
            flops=2 * wide * rows * turns * half,
            bytes_accessed=2 * rows * turns * half + 2 * rows * wide,
            transcendentals=0,
        ),
    )(ids, left, weight, *([carry] if carried else []))


def invert_kernel(starts, first, *refs):
    refs = list(refs)
    lanes = lax.broadcasted_iota(jnp.int32, (8, 128), 1)
    if starts:
        gram_ref, work_ref, out_ref = refs
        size = work_ref.shape[0]
        total = gram_ref[0]
        for chip in range(1, gram_ref.shape[0]):
            total = total + gram_ref[chip]
        work_ref[...] = jnp.zeros_like(work_ref)
        work_ref[:, :size] = total
    else:
        before_ref, work_ref, out_ref = refs
        size = work_ref.shape[0]
        work_ref[...] = before_ref[...]
    side = first // 16
    tall = size - 8 * first

    rows_at = 8 * first + lax.broadcasted_iota(jnp.int32, (tall, 128), 0)
    inside = lax.broadcasted_iota(jnp.int32, (8, 128), 0)

    def packed(values):
        total = values[0]
        for s in range(1, 8):
            total = jnp.where(inside == s, values[s], total)
        return total

    def panel(p, _):
        raw = [work_ref[pl.ds(8 * p, 8), :128], work_ref[pl.ds(8 * p, 8), 128:]]
        entry, ratio, inverse = {}, {}, []
        for s in range(8):
            at = jnp.full((8, 128), 8 * p + s - 128 * side, jnp.int32)
            column = jnp.take_along_axis(raw[side], at, axis=1)
            for r in range(s + 1):
                entry[r, s] = jnp.broadcast_to(column[r : r + 1], (8, 128))
        for s in range(8):
            inverse.append(1.0 / entry[s, s])
            for t in range(s + 1, 8):
                ratio[t, s] = entry[s, t] * inverse[s]
            for t in range(s + 1, 8):
                for u in range(t, 8):
                    entry[t, u] = entry[t, u] - ratio[t, s] * entry[s, u]
        low = 8 * p - 128 * side
        own = (lanes >= low) & (lanes < low + 8)
        row = []
        for t in range(8):
            halves = [jnp.broadcast_to(part[t : t + 1], (8, 128)) for part in raw]
            unit = jnp.where(lanes == low + t, 1.0, 0.0)
            halves[side] = jnp.where(own, unit, halves[side])
            for s in range(t):
                halves = [half - ratio[t, s] * done for half, done in zip(halves, row[s])]
            row.append(halves)
        scale = lax.rsqrt(packed([entry[s, s] for s in range(8)]))
        inverses = packed(inverse)
        factors = []
        for half in range(2):
            whole = packed([row[s][half] for s in range(8)])
            beyond = lanes + 128 * half >= 8 * p + 8
            strip = jnp.where(beyond, 0.0, whole * scale)
            out_ref[pl.ds(8 * (p - first), 8), 128 * half : min(128 * half + 128, size)] = strip[
                :, : min(128, size - 128 * half)
            ]
            factors.append(jnp.where(beyond, whole * inverses, 0.0).T)
        factor = jnp.concatenate(factors, 0)[8 * first : size]
        spread = lambda x: jnp.tile(x, (tall // 8, 1))
        after = rows_at >= 8 * p + 8
        for half in range(2):
            place = (slice(8 * first, size), slice(128 * half, 128 * half + 128))
            rest = work_ref[place]
            if half == side:
                rest = jnp.where(spread(own) & after, 0.0, rest)
            for s in range(8):
                rest = rest - jnp.broadcast_to(factor[:, s : s + 1], (tall, 128)) * spread(row[s][half])
            work_ref[place] = rest
        return 0

    lax.fori_loop(first, first + out_ref.shape[0] // 8, panel, 0)


def invert_panels(first, size, source):
    tall = min(64, size - 8 * first)
    whole = pl.BlockSpec(memory_space=pltpu.VMEM)
    return pl.pallas_call(
        functools.partial(invert_kernel, first == 0, first),
        out_shape=[
            jax.ShapeDtypeStruct((size, 256), jnp.float32),
            jax.ShapeDtypeStruct((tall, size), jnp.float32),
        ],
        in_specs=[whole],
        out_specs=[whole] * 2,
        input_output_aliases={0: 0} if first else {},
        compiler_params=pltpu.CompilerParams(vmem_limit_bytes=32 * MIB),
        cost_estimate=pl.CostEstimate(flops=10**9, bytes_accessed=2 * 10**7, transcendentals=0),
    )(source)


def rows_kernel(first, following, pieces, spans, chained, narrow, by_depth, grams, ids_ref, weight_ref, *refs):
    refs = list(refs)
    ready_ref = refs.pop(0)
    piece_refs = [refs.pop(0) for _ in range(pieces)]
    before_ref = refs.pop(0) if chained else None
    if grams and chained:
        refs.pop(0)
    out_ref = refs.pop(0)
    gram_ref = refs.pop(0) if grams else None
    next_ref = refs.pop(0) if following is not None else None
    held_ref, joined_ref, sems = refs[:3]
    total_ref = refs[3] if narrow else out_ref
    half, turns = first.half, first.turns
    halves = turns // pieces
    chunk, depth = 2 * half, turns * half
    blocks = [[]]
    for number, (low, tall) in enumerate(spans[1:], 1):
        place = pl.ds(low - first.tall, tall)
        targets = [held_ref.at[place, pl.ds(at * chunk, chunk)] for at in range(turns // 2)]
        blocks.append(first.strips(ids_ref, weight_ref, low, tall, targets, sems.at[number]))
    if following is not None:
        blocks.append(following.copies(ids_ref, weight_ref, next_ref, sems.at[0]))
    onto = (((1,), (1,)), ((), ()))

    def piece(turn):
        at = turn % halves * half
        return piece_refs[turn // halves][:, at : at + half]

    def prepare():
        for turn in range(turns):
            at = turn // 2 * chunk + ids_ref[first.base + turn] % 2 * half
            upright = piece(turn).astype(jnp.float32).T.astype(jnp.bfloat16)
            joined_ref[pl.ds(pl.multiple_of(at, 128), half), :] = upright

    def product(block_ref, low, tall, at, size):
        return jnp.dot(
            block_ref[low : low + tall, at : at + size],
            joined_ref[at : at + size, :],
            preferred_element_type=jnp.float32,
        )

    def put(low, tall, part):
        if chained:
            part = before_ref[low : low + tall, :] + part
        total_ref[low : low + tall, :] = part

    def work(number):
        if number == len(spans):
            return
        low, tall = spans[number]
        block_ref, at = (held_ref, low - first.tall) if number else (ready_ref, 0)
        if by_depth:
            parts = [product(block_ref, at, tall, side * depth // 2, depth // 2) for side in range(2)]
            put(low, tall, parts[0] + parts[1])
        else:
            parts = [product(block_ref, at + side * tall // 2, tall // 2, 0, depth) for side in range(2)]
            for side in range(2):
                put(low + side * tall // 2, tall // 2, parts[side])
        if grams and 0 < number <= turns // 2:
            squares = [
                lax.dot_general(piece(turn), piece(turn), onto, preferred_element_type=jnp.float32)
                for turn in range(2 * number - 2, 2 * number)
            ]
            gram_ref[ids_ref[first.base + 2 * number - 2] // 2] = squares[0] + squares[1]

    in_turn(blocks, 2, work, prepare)
    if narrow:
        out_ref[...] = total_ref[...].T.astype(jnp.bfloat16)


def row_products(weight, pieces, ids, first, before, narrow, by_depth, grams, carry, following):
    rows, wide = weight.shape[0], pieces[0].shape[0]
    turns, half = first.turns, first.half
    chips = weight.shape[1] // (2 * half)
    spans = [(low, first.tall) for low in range(0, rows, first.tall)]
    whole = pl.BlockSpec(memory_space=pltpu.VMEM)
    operands = [ids, weight, carry, *pieces]
    in_specs = [pl.BlockSpec(memory_space=pltpu.SMEM), pl.BlockSpec(memory_space=pl.ANY), whole]
    in_specs += [whole] * len(pieces)
    shape = jax.ShapeDtypeStruct((rows, wide), jnp.float32)
    out_shape = [jax.ShapeDtypeStruct((wide, rows), jnp.bfloat16) if narrow else shape]
    aliases = {}
    if before is not None:
        if not narrow:
            aliases[len(operands)] = 0
        operands.append(before)
        in_specs.append(whole)
    if grams is not None:
        if before is not None:
            aliases[len(operands)] = 1
            operands.append(grams)
            in_specs.append(whole)
        out_shape.append(jax.ShapeDtypeStruct((chips, wide, wide), jnp.float32))
    if following is not None:
        out_shape.append(jax.ShapeDtypeStruct(following.shape, jnp.bfloat16))
    depth = turns * half
    return pl.pallas_call(
        functools.partial(
            rows_kernel,
            first,
            following,
            len(pieces),
            spans,
            before is not None,
            narrow,
            by_depth,
            grams is not None,
        ),
        out_shape=out_shape,
        in_specs=in_specs,
        out_specs=[whole] * len(out_shape),
        scratch_shapes=[
            pltpu.VMEM((max(rows - first.tall, 16), depth), jnp.bfloat16),
            pltpu.VMEM((depth, wide), jnp.bfloat16),
            pltpu.SemaphoreType.DMA((len(spans) + 1, 2)),
        ]
        + [pltpu.VMEM((rows, wide), jnp.float32)] * narrow,
        input_output_aliases=aliases,
        compiler_params=pltpu.CompilerParams(vmem_limit_bytes=40 * MIB),
        cost_estimate=pl.CostEstimate(
            flops=2 * rows * wide * turns * half,
            bytes_accessed=2 * rows * turns * half + 8 * rows * wide,
            transcendentals=0,
        ),
    )(*operands)


def ring_sum(ring, ids, left, weight, half, carry):
    got = None
    for k in range(ring.far, 0, -1):
        first = ring.first(weight, "sum", k)
        keep, give, carry = column_sums(
            left, weight, ids, first, half, True, carry, ring.first(weight, "sum", k - 1)
        )
        given = lax.ppermute(give, "row", ring.pair)
        if got is not None:
            got = got.astype(jnp.float32)
            size = got.shape[1]
            if size < keep.shape[1]:
                keep = jnp.concatenate([keep[:, :size] + got, keep[:, size:]], 1)
            else:
                keep = keep + got
            keep, given = lax.optimization_barrier((keep, given))
        total = (keep + given.astype(jnp.float32)).astype(jnp.bfloat16)
        total, left = lax.optimization_barrier((total, left))
        got = lax.ppermute(total, "row", ring.ahead)
    first = ring.first(weight, "sum", 0)
    keep, carry = column_sums(
        left, weight, ids, first, half, False, carry, ring.first(weight, "use", 0)
    )
    mine = keep + got.astype(jnp.float32)
    other = lax.ppermute(mine, "row", ring.pair)
    return mine + jnp.concatenate([other[:, half:], other[:, :half]], 1), carry


def ring_apply(ring, ids, chunk, weight, half, narrow, carry, following):
    before, grams = None, None if narrow else ()
    moving = chunk
    for k in range(ring.far + 1):
        if k == 0:
            pieces = [chunk]
        else:
            moving = lax.ppermute(moving if k < ring.far else moving[:, :half], "row", ring.ahead)
            moving, before = lax.optimization_barrier((moving, before))
            pieces = [moving, lax.ppermute(moving, "row", ring.pair)]
        last = k == ring.far
        then = following if last else ring.first(weight, "use", k + 1)
        first = ring.first(weight, "use", k)
        outs = list(
            row_products(
                weight, pieces, ids, first, before, narrow and last, not narrow, grams, carry, then
            )
        )
        carry = outs.pop() if then is not None else None
        before = outs.pop(0)
        grams = outs.pop() if outs else None
    return before, grams, carry


def sum_beside_inverse(value, ring, grams):
    size = value.shape[0]
    rows = size // 2
    first = lax.axis_index("row") % 2 == 0
    low, high = value[:rows], value[rows:]
    part = jnp.where(first, low, high)
    part = part + lax.ppermute(jnp.where(first, high, low), "row", ring.pair)
    hops = [
        [(device, device ^ (2 << bit)) for device in range(2 * ring.chips)]
        for bit in reversed(range(ring.chips.bit_length() - 1))
    ]
    panels = list(range(0, size // 8, 8))
    work, strips = grams, []
    for at in range(max(len(hops), len(panels))):
        if at < len(hops):
            got = lax.ppermute(part, "row", hops[at])
        if at < len(panels):
            work, strip = invert_panels(panels[at], size, work)
            strips.append(strip)
        if at < len(hops):
            got, work = lax.optimization_barrier((got, work))
            part = part + got
    other = lax.ppermute(part, "row", ring.pair)
    total = jnp.concatenate([jnp.where(first, part, other), jnp.where(first, other, part)], 0)
    return total, jnp.concatenate(strips, 0)


def ring_body(ring, weight, test_matrix, rank_mask):
    highest = lax.Precision.HIGHEST
    rows, features = weight.shape
    half = features // (2 * ring.chips)
    ids = ring.row()
    picker = selector(rank_mask, RANK)
    sketch, carry = ring_sum(ring, ids, test_matrix.T, weight, half, None)
    sketch = sketch.astype(jnp.bfloat16)
    again = ring.first(weight, "sum", ring.far)
    mixed, _, carry = ring_apply(ring, ids, sketch, weight, half, True, carry, again)
    powered, carry = ring_sum(ring, ids, mixed, weight, half, carry)
    powered_b = powered.astype(jnp.bfloat16)
    image, grams, _ = ring_apply(ring, ids, powered_b, weight, half, False, carry, None)
    image_b = image.astype(jnp.bfloat16)
    square = lax.dot_general(
        image_b, image_b, (((0,), (0,)), ((), ())), preferred_element_type=jnp.float32
    )
    square, inverse = sum_beside_inverse(square, ring, grams)
    change = lax.dot_general(inverse, picker, (((0,), (0,)), ((), ())), precision=highest)
    own = powered[:, :half]
    left_factor = lax.dot_general(
        own, change, (((0,), (0,)), ((), ())), precision=highest
    ) * math.sqrt(features)
    energy = jnp.sum(square * jnp.dot(change, change.T, precision=highest))
    spread = jnp.sqrt(energy / (rows * 2 * ring.chips * RANK) + 1e-06)
    projected = jnp.dot(image, change, precision=lax.Precision.HIGH)
    right_factor = (projected / spread).astype(jnp.bfloat16)
    return (left_factor, right_factor, spread.reshape(1))


def body(weight, test_matrix, rank_mask):
    members = lax.axis_size("row")
    chips = members // 2
    paired = members % 2 == 0 and chips > 2 and chips & (chips - 1) == 0
    if not paired or weight.shape[1] % (members * 128):
        return plain_body(weight, test_matrix, rank_mask)
    return ring_body(Ring(members), weight, test_matrix, rank_mask)


def solution(mesh):
    in_specs = (P(("groups", "row"), None), P("row", None), P("groups"))
    out_specs = (P(("groups", "row"), None), P(("groups", "row"), None), P("groups"))
    return jax.shard_map(body, mesh=mesh, in_specs=in_specs, out_specs=out_specs, check_vma=False)
```

```python
import functools
import math

import jax
import jax.numpy as jnp
import numpy as np
from jax import lax
from jax.experimental import pallas as pl
from jax.experimental.pallas import tpu as pltpu
from jax.sharding import PartitionSpec as P

RANK = 224
SPARE = 4 * 1024 * 1024


def selector(rank_mask, kept):
    positions = jnp.cumsum(rank_mask) - 1
    targets = lax.iota(jnp.int32, kept)
    matches = (rank_mask[:, None] == 1) & (positions[:, None] == targets[None, :])
    return matches.astype(jnp.float32)


def plain_body(weight, test_matrix, rank_mask):
    across = (((0,), (0,)), ((), ()))
    members = lax.axis_size("row")
    picker = selector(rank_mask, RANK)
    sketch_part = lax.psum_scatter(
        lax.dot_general(weight, test_matrix, across, preferred_element_type=jnp.float32),
        "row",
        scatter_dimension=0,
        tiled=True,
    ).astype(jnp.bfloat16)

    def add_rows(piece_rows):
        return jnp.dot(weight, piece_rows, preferred_element_type=jnp.float32)

    mixed = add_rows(lax.all_gather(sketch_part, "row", axis=0, tiled=True)).astype(jnp.bfloat16)
    powered = lax.psum_scatter(
        lax.dot_general(weight, mixed, across, preferred_element_type=jnp.float32),
        "row",
        scatter_dimension=0,
        tiled=True,
    )
    local_gram = lax.dot_general(powered, powered, across, precision=lax.Precision.HIGHEST)
    gram_matrix = lax.psum(local_gram, "row")
    cholesky_factor = jnp.linalg.cholesky(gram_matrix)
    ortho_basis = lax.linalg.triangular_solve(
        cholesky_factor, powered, left_side=False, lower=True, transpose_a=True
    )
    own_chosen = jnp.dot(ortho_basis, picker, precision=lax.Precision.HIGHEST)
    projected = add_rows(lax.all_gather(own_chosen.astype(jnp.bfloat16), "row", axis=0, tiled=True))
    left_factor = own_chosen * math.sqrt(weight.shape[1])
    energy = lax.psum(jnp.sum(projected * projected), "row")
    spread = jnp.sqrt(energy / (weight.shape[0] * members * RANK) + 1e-06)
    right_factor = (projected / spread).astype(jnp.bfloat16)
    return (left_factor, right_factor, spread.reshape(1))


class Ring:
    def __init__(self, members):
        chips = members // 2
        order = list(range(0, chips, 2)) + list(range(chips - 1, 0, -2))
        place = {chip: at for at, chip in enumerate(order)}
        self.chips, self.far = chips, chips // 2
        self.pair = [(device, device ^ 1) for device in range(members)]
        self.ahead = []
        for at, chip in enumerate(order):
            self.ahead.append((2 * chip, 2 * order[(at + 1) % chips]))
            self.ahead.append((2 * chip + 1, 2 * order[at - 1] + 1))

        def halves(device, steps, core):
            at = place[device // 2] + (steps if device % 2 == 0 else -steps)
            chip = order[at % chips]
            return [2 * chip + core, 2 * chip + 1 - core]

        self.width, self.table = {}, []
        for device in range(members):
            core, row = device % 2, []

            def put(name, values):
                self.width[name] = (len(row), len(values))
                row.extend(values)

            for k in range(self.far + 1):
                one = k == self.far
                mine, other = halves(device, k, core), halves(device, -k, 1 - core)
                put(("sum", k), mine if k == 0 else (mine[:1] + other[:1] if one else mine + other))
                mine, other = halves(device, -k, core), halves(device, k, 1 - core)
                put(("use", k), mine if k == 0 else (mine[:1] + other[:1] if one else mine + other))
            self.table.append(row)

    def first(self, weight, name, k):
        half = weight.shape[1] // (2 * self.chips)
        base, turns = self.width[name, k]
        return First(weight.shape[0], half, base, turns, name == "use")

    def row(self):
        table = jnp.asarray(np.array(self.table, np.int32))
        return lax.dynamic_index_in_dim(table, lax.axis_index("row"), 0, keepdims=False)


class First:
    def __init__(self, rows, half, base, turns, by_rows):
        self.half, self.base, self.turns, self.by_rows = half, base, turns, by_rows
        self.tall = rows // 4 if by_rows and rows % 128 == 0 else rows
        self.shape = (self.tall, turns * half) if by_rows else (rows, half)

    def copies(self, ids_ref, weight_ref, target_ref, sems):
        if not self.by_rows:
            start = pl.multiple_of(ids_ref[self.base] * self.half, 128)
            source = weight_ref.at[:, pl.ds(start, self.half)]
            return [pltpu.make_async_copy(source, target_ref, sems.at[0])]
        target = [target_ref.at[:, pl.ds(at * 2 * self.half, 2 * self.half)] for at in range(self.turns // 2)]
        return self.strips(ids_ref, weight_ref, 0, self.tall, target, sems)

    def strips(self, ids_ref, weight_ref, low, tall, targets, sems):
        chunk = 2 * self.half
        starts = [ids_ref[self.base + 2 * at] // 2 * chunk for at in range(len(targets))]
        return [
            pltpu.make_async_copy(
                weight_ref.at[pl.ds(low, tall), pl.ds(pl.multiple_of(start, 128), chunk)],
                target,
                sems.at[at],
            )
            for at, (start, target) in enumerate(zip(starts, targets))
        ]


def in_turn(blocks, ahead, work, prepare=None):
    for block in blocks[: ahead + 1]:
        for copy in block:
            copy.start()
    if prepare is not None:
        prepare()
    for at, block in enumerate(blocks):
        for copy in block:
            copy.wait()
        if at > 0 and at + ahead < len(blocks):
            for copy in blocks[at + ahead]:
                copy.start()
        work(at)


def columns_kernel(first, following, turns, kept, carried, ids_ref, left_ref, weight_ref, *refs):
    refs = list(refs)
    half = first.half
    sems, held_ref = refs.pop(), refs.pop()
    ready_ref = refs.pop(0) if carried else held_ref.at[turns - 1]
    next_ref = refs.pop() if following is not None else None
    blocks = [[] if carried else first.copies(ids_ref, weight_ref, ready_ref, sems.at[0])]
    for turn in range(1, turns):
        start = pl.multiple_of(ids_ref[first.base + turn] * half, 128)
        source = weight_ref.at[:, pl.ds(start, half)]
        blocks.append([pltpu.make_async_copy(source, held_ref.at[turn - 1], sems.at[turn, 0])])
    if following is not None:
        blocks.append(following.copies(ids_ref, weight_ref, next_ref, sems.at[turns]))

    def work(turn):
        if turn == turns:
            return
        block = ready_ref[...] if turn == 0 else held_ref[turn - 1]
        part = jnp.dot(left_ref[...], block, preferred_element_type=jnp.float32)
        out, at = (0, turn) if turn < kept else (1, turn - kept)
        refs[out][:, at * half : (at + 1) * half] = part.astype(refs[out].dtype)

    in_turn(blocks, 2, work)


def column_sums(left, weight, ids, first, half, split, carry, following):
    rows, wide = left.shape[1], left.shape[0]
    turns = first.turns
    kept = turns // 2 if split else turns
    out_shape = [jax.ShapeDtypeStruct((wide, kept * half), jnp.float32)]
    if split:
        out_shape.append(jax.ShapeDtypeStruct((wide, kept * half), jnp.bfloat16))
    if following is not None:
        out_shape.append(jax.ShapeDtypeStruct(following.shape, jnp.bfloat16))
    whole = pl.BlockSpec(memory_space=pltpu.VMEM)
    carried = carry is not None
    return pl.pallas_call(
        functools.partial(columns_kernel, first, following, turns, kept, carried),
        out_shape=out_shape,
        in_specs=[
            pl.BlockSpec(memory_space=pltpu.SMEM),
            whole,
            pl.BlockSpec(memory_space=pl.ANY),
        ]
        + [whole] * carried,
        out_specs=[whole] * len(out_shape),
        scratch_shapes=[
            pltpu.VMEM((turns - carried, rows, half), jnp.bfloat16),
            pltpu.SemaphoreType.DMA((turns + 1, 2)),
        ],
        compiler_params=pltpu.CompilerParams(
            vmem_limit_bytes=2 * (turns - carried) * rows * half + SPARE
        ),
        cost_estimate=pl.CostEstimate(
            flops=2 * wide * rows * turns * half,
            bytes_accessed=2 * rows * turns * half + 2 * rows * wide,
            transcendentals=0,
        ),
    )(ids, left, weight, *([carry] if carried else []))


def invert_kernel(starts, first, *refs):
    refs = list(refs)
    lanes = lax.broadcasted_iota(jnp.int32, (8, 128), 1)
    if starts:
        gram_ref, work_ref, out_ref = refs
        size = work_ref.shape[0]
        total = gram_ref[0]
        for chip in range(1, gram_ref.shape[0]):
            total = total + gram_ref[chip]
        work_ref[...] = jnp.zeros_like(work_ref)
        work_ref[:, :size] = total
    else:
        before_ref, work_ref, out_ref = refs
        size = work_ref.shape[0]
        work_ref[...] = before_ref[...]
    side = first // 16
    tall = size - 8 * first

    rows_at = 8 * first + lax.broadcasted_iota(jnp.int32, (tall, 128), 0)
    inside = lax.broadcasted_iota(jnp.int32, (8, 128), 0)

    def packed(values):
        total = values[0]
        for s in range(1, 8):
            total = jnp.where(inside == s, values[s], total)
        return total

    def panel(p, _):
        raw = [work_ref[pl.ds(8 * p, 8), :128], work_ref[pl.ds(8 * p, 8), 128:]]
        entry, ratio, inverse = {}, {}, []
        for s in range(8):
            at = jnp.full((8, 128), 8 * p + s - 128 * side, jnp.int32)
            column = jnp.take_along_axis(raw[side], at, axis=1)
            for r in range(s + 1):
                entry[r, s] = jnp.broadcast_to(column[r : r + 1], (8, 128))
        for s in range(8):
            inverse.append(1.0 / entry[s, s])
            for t in range(s + 1, 8):
                ratio[t, s] = entry[s, t] * inverse[s]
            for t in range(s + 1, 8):
                for u in range(t, 8):
                    entry[t, u] = entry[t, u] - ratio[t, s] * entry[s, u]
        low = 8 * p - 128 * side
        own = (lanes >= low) & (lanes < low + 8)
        row = []
        for t in range(8):
            halves = [jnp.broadcast_to(part[t : t + 1], (8, 128)) for part in raw]
            unit = jnp.where(lanes == low + t, 1.0, 0.0)
            halves[side] = jnp.where(own, unit, halves[side])
            for s in range(t):
                halves = [half - ratio[t, s] * done for half, done in zip(halves, row[s])]
            row.append(halves)
        scale = lax.rsqrt(packed([entry[s, s] for s in range(8)]))
        inverses = packed(inverse)
        factors = []
        for half in range(2):
            whole = packed([row[s][half] for s in range(8)])
            beyond = lanes + 128 * half >= 8 * p + 8
            strip = jnp.where(beyond, 0.0, whole * scale)
            out_ref[pl.ds(8 * (p - first), 8), 128 * half : min(128 * half + 128, size)] = strip[
                :, : min(128, size - 128 * half)
            ]
            factors.append(jnp.where(beyond, whole * inverses, 0.0).T)
        factor = jnp.concatenate(factors, 0)[8 * first : size]
        spread = lambda x: jnp.tile(x, (tall // 8, 1))
        after = rows_at >= 8 * p + 8
        for half in range(2):
            place = (slice(8 * first, size), slice(128 * half, 128 * half + 128))
            rest = work_ref[place]
            if half == side:
                rest = jnp.where(spread(own) & after, 0.0, rest)
            for s in range(8):
                rest = rest - jnp.broadcast_to(factor[:, s : s + 1], (tall, 128)) * spread(row[s][half])
            work_ref[place] = rest
        return 0

    lax.fori_loop(first, first + out_ref.shape[0] // 8, panel, 0)


def invert_panels(first, size, source):
    tall = min(64, size - 8 * first)
    whole = pl.BlockSpec(memory_space=pltpu.VMEM)
    return pl.pallas_call(
        functools.partial(invert_kernel, first == 0, first),
        out_shape=[
            jax.ShapeDtypeStruct((size, 256), jnp.float32),
            jax.ShapeDtypeStruct((tall, size), jnp.float32),
        ],
        in_specs=[whole],
        out_specs=[whole] * 2,
        input_output_aliases={0: 0} if first else {},
        compiler_params=pltpu.CompilerParams(vmem_limit_bytes=SPARE),
        cost_estimate=pl.CostEstimate(flops=10**9, bytes_accessed=2 * 10**7, transcendentals=0),
    )(source)


def rows_kernel(first, following, pieces, spans, chained, narrow, grams, ids_ref, weight_ref, *refs):
    refs = list(refs)
    ready_ref = refs.pop(0)
    piece_refs = [refs.pop(0) for _ in range(pieces)]
    before_ref = refs.pop(0) if chained else None
    if grams and chained:
        refs.pop(0)
    out_ref = refs.pop(0)
    gram_ref = refs.pop(0) if grams else None
    next_ref = refs.pop(0) if following is not None else None
    held_ref, joined_ref, sems = refs[:3]
    total_ref = refs[3] if narrow else out_ref
    half, turns = first.half, first.turns
    halves = turns // pieces
    chunk = 2 * half
    blocks = [[]]
    for number, (low, tall) in enumerate(spans[1:], 1):
        place = pl.ds(low - first.tall, tall)
        targets = [held_ref.at[place, pl.ds(at * chunk, chunk)] for at in range(turns // 2)]
        blocks.append(first.strips(ids_ref, weight_ref, low, tall, targets, sems.at[number]))
    if following is not None:
        blocks.append(following.copies(ids_ref, weight_ref, next_ref, sems.at[0]))
    onto = (((1,), (1,)), ((), ()))

    def piece(turn):
        at = turn % halves * half
        return piece_refs[turn // halves][:, at : at + half]

    def prepare():
        for turn in range(turns):
            at = turn // 2 * chunk + ids_ref[first.base + turn] % 2 * half
            upright = piece(turn).astype(jnp.float32).T.astype(jnp.bfloat16)
            joined_ref[pl.ds(pl.multiple_of(at, 128), half), :] = upright

    def work(number):
        if number == len(spans):
            return
        low, tall = spans[number]
        block_ref, at = (held_ref, low - first.tall) if number else (ready_ref, 0)
        parts = [
            jnp.dot(
                block_ref[at + side * tall // 2 : at + (side + 1) * tall // 2, :],
                joined_ref[...],
                preferred_element_type=jnp.float32,
            )
            for side in range(2)
        ]
        for side, part in enumerate(parts):
            place = (slice(low + side * tall // 2, low + (side + 1) * tall // 2), slice(None))
            total_ref[place] = before_ref[place] + part if chained else part
        if grams and 0 < number <= turns // 2:
            squares = [
                lax.dot_general(piece(turn), piece(turn), onto, preferred_element_type=jnp.float32)
                for turn in range(2 * number - 2, 2 * number)
            ]
            gram_ref[ids_ref[first.base + 2 * number - 2] // 2] = squares[0] + squares[1]

    in_turn(blocks, 2, work, prepare)
    if narrow:
        out_ref[...] = total_ref[...].T.astype(jnp.bfloat16)


def row_products(weight, pieces, ids, first, before, narrow, grams, carry, following):
    rows, wide = weight.shape[0], pieces[0].shape[0]
    turns, half = first.turns, first.half
    chips = weight.shape[1] // (2 * half)
    spans = [(low, first.tall) for low in range(0, rows, first.tall)]
    whole = pl.BlockSpec(memory_space=pltpu.VMEM)
    operands = [ids, weight, carry, *pieces]
    in_specs = [pl.BlockSpec(memory_space=pltpu.SMEM), pl.BlockSpec(memory_space=pl.ANY), whole]
    in_specs += [whole] * len(pieces)
    shape = jax.ShapeDtypeStruct((rows, wide), jnp.float32)
    out_shape = [jax.ShapeDtypeStruct((wide, rows), jnp.bfloat16) if narrow else shape]
    aliases = {}
    if before is not None:
        if not narrow:
            aliases[len(operands)] = 0
        operands.append(before)
        in_specs.append(whole)
    if grams is not None:
        if before is not None:
            aliases[len(operands)] = 1
            operands.append(grams)
            in_specs.append(whole)
        out_shape.append(jax.ShapeDtypeStruct((chips, wide, wide), jnp.float32))
    if following is not None:
        out_shape.append(jax.ShapeDtypeStruct(following.shape, jnp.bfloat16))
    depth = turns * half
    return pl.pallas_call(
        functools.partial(
            rows_kernel,
            first,
            following,
            len(pieces),
            spans,
            before is not None,
            narrow,
            grams is not None,
        ),
        out_shape=out_shape,
        in_specs=in_specs,
        out_specs=[whole] * len(out_shape),
        scratch_shapes=[
            pltpu.VMEM((max(rows - first.tall, 16), depth), jnp.bfloat16),
            pltpu.VMEM((depth, wide), jnp.bfloat16),
            pltpu.SemaphoreType.DMA((len(spans) + 1, 2)),
        ]
        + [pltpu.VMEM((rows, wide), jnp.float32)] * narrow,
        input_output_aliases=aliases,
        compiler_params=pltpu.CompilerParams(
            vmem_limit_bytes=2 * depth * (rows - first.tall + 256) + 1024 * rows * narrow + SPARE
        ),
        cost_estimate=pl.CostEstimate(
            flops=2 * rows * wide * turns * half,
            bytes_accessed=2 * rows * turns * half + 8 * rows * wide,
            transcendentals=0,
        ),
    )(*operands)


def ring_sum(ring, ids, left, weight, half, carry):
    got = None
    for k in range(ring.far, 0, -1):
        first = ring.first(weight, "sum", k)
        keep, give, carry = column_sums(
            left, weight, ids, first, half, True, carry, ring.first(weight, "sum", k - 1)
        )
        given = lax.ppermute(give, "row", ring.pair)
        if got is not None:
            got = got.astype(jnp.float32)
            size = got.shape[1]
            if size < keep.shape[1]:
                keep = jnp.concatenate([keep[:, :size] + got, keep[:, size:]], 1)
            else:
                keep = keep + got
            keep, given = lax.optimization_barrier((keep, given))
        total = (keep + given.astype(jnp.float32)).astype(jnp.bfloat16)
        total, left = lax.optimization_barrier((total, left))
        got = lax.ppermute(total, "row", ring.ahead)
    first = ring.first(weight, "sum", 0)
    keep, carry = column_sums(
        left, weight, ids, first, half, False, carry, ring.first(weight, "use", 0)
    )
    mine = keep + got.astype(jnp.float32)
    other = lax.ppermute(mine, "row", ring.pair)
    return mine + jnp.concatenate([other[:, half:], other[:, :half]], 1), carry


def ring_apply(ring, ids, chunk, weight, half, narrow, carry, following):
    before, grams = None, None if narrow else ()
    moving = chunk
    for k in range(ring.far + 1):
        if k == 0:
            pieces = [chunk]
        else:
            moving = lax.ppermute(moving if k < ring.far else moving[:, :half], "row", ring.ahead)
            moving, before = lax.optimization_barrier((moving, before))
            pieces = [moving, lax.ppermute(moving, "row", ring.pair)]
        last = k == ring.far
        then = following if last else ring.first(weight, "use", k + 1)
        first = ring.first(weight, "use", k)
        outs = list(
            row_products(
                weight, pieces, ids, first, before, narrow and last, grams, carry, then
            )
        )
        carry = outs.pop() if then is not None else None
        before = outs.pop(0)
        grams = outs.pop() if outs else None
    return before, grams, carry


def sum_beside_inverse(value, ring, grams):
    size = value.shape[0]
    rows = size // 2
    first = lax.axis_index("row") % 2 == 0
    low, high = value[:rows], value[rows:]
    part = jnp.where(first, low, high)
    part = part + lax.ppermute(jnp.where(first, high, low), "row", ring.pair)
    hops = [
        [(device, device ^ (2 << bit)) for device in range(2 * ring.chips)]
        for bit in reversed(range(ring.chips.bit_length() - 1))
    ]
    panels = list(range(0, size // 8, 8))
    work, strips = grams, []
    for at in range(max(len(hops), len(panels))):
        if at < len(hops):
            got = lax.ppermute(part, "row", hops[at])
        if at < len(panels):
            work, strip = invert_panels(panels[at], size, work)
            strips.append(strip)
        if at < len(hops):
            got, work = lax.optimization_barrier((got, work))
            part = part + got
    other = lax.ppermute(part, "row", ring.pair)
    total = jnp.concatenate([jnp.where(first, part, other), jnp.where(first, other, part)], 0)
    return total, jnp.concatenate(strips, 0)


def ring_body(ring, weight, test_matrix, rank_mask):
    highest = lax.Precision.HIGHEST
    rows, features = weight.shape
    half = features // (2 * ring.chips)
    ids = ring.row()
    picker = selector(rank_mask, RANK)
    sketch, carry = ring_sum(ring, ids, test_matrix.T, weight, half, None)
    sketch = sketch.astype(jnp.bfloat16)
    again = ring.first(weight, "sum", ring.far)
    mixed, _, carry = ring_apply(ring, ids, sketch, weight, half, True, carry, again)
    powered, carry = ring_sum(ring, ids, mixed, weight, half, carry)
    powered_b = powered.astype(jnp.bfloat16)
    image, grams, _ = ring_apply(ring, ids, powered_b, weight, half, False, carry, None)
    image_b = image.astype(jnp.bfloat16)
    square = lax.dot_general(
        image_b, image_b, (((0,), (0,)), ((), ())), preferred_element_type=jnp.float32
    )
    square, inverse = sum_beside_inverse(square, ring, grams)
    change = lax.dot_general(inverse, picker, (((0,), (0,)), ((), ())), precision=highest)
    own = powered[:, :half]
    left_factor = lax.dot_general(
        own, change, (((0,), (0,)), ((), ())), precision=highest
    ) * math.sqrt(features)
    energy = jnp.sum(square * jnp.dot(change, change.T, precision=highest))
    spread = jnp.sqrt(energy / (rows * 2 * ring.chips * RANK) + 1e-06)
    right_factor = jnp.dot(image, change / spread, precision=lax.Precision.HIGH).astype(jnp.bfloat16)
    return (left_factor, right_factor, spread.reshape(1))


def body(weight, test_matrix, rank_mask):
    members = lax.axis_size("row")
    chips = members // 2
    paired = members % 2 == 0 and chips > 2 and chips & (chips - 1) == 0
    if not paired or weight.shape[1] % (members * 128):
        return plain_body(weight, test_matrix, rank_mask)
    return ring_body(Ring(members), weight, test_matrix, rank_mask)


def solution(mesh):
    in_specs = (P(("groups", "row"), None), P("row", None), P("groups"))
    out_specs = (P(("groups", "row"), None), P(("groups", "row"), None), P("groups"))
    return jax.shard_map(body, mesh=mesh, in_specs=in_specs, out_specs=out_specs, check_vma=False)
```

```python
import functools
import math

import jax
import jax.numpy as jnp
import numpy as np
from jax import lax
from jax.experimental import pallas as pl
from jax.experimental.pallas import tpu as pltpu
from jax.sharding import PartitionSpec as P

RANK = 224
SPARE = 4 * 1024 * 1024


def selector(rank_mask, kept):
    at = lax.iota(jnp.int32, rank_mask.shape[0])
    positions = jnp.sum(jnp.where(at[:, None] <= at[None, :], rank_mask[:, None], 0), axis=0) - 1
    targets = lax.iota(jnp.int32, kept)
    matches = (rank_mask[:, None] == 1) & (positions[:, None] == targets[None, :])
    return matches.astype(jnp.float32)


def plain_body(weight, test_matrix, rank_mask):
    across = (((0,), (0,)), ((), ()))
    members = lax.axis_size("row")
    picker = selector(rank_mask, RANK)
    sketch_part = lax.psum_scatter(
        lax.dot_general(weight, test_matrix, across, preferred_element_type=jnp.float32),
        "row",
        scatter_dimension=0,
        tiled=True,
    ).astype(jnp.bfloat16)

    def add_rows(piece_rows):
        return jnp.dot(weight, piece_rows, preferred_element_type=jnp.float32)

    mixed = add_rows(lax.all_gather(sketch_part, "row", axis=0, tiled=True)).astype(jnp.bfloat16)
    powered = lax.psum_scatter(
        lax.dot_general(weight, mixed, across, preferred_element_type=jnp.float32),
        "row",
        scatter_dimension=0,
        tiled=True,
    )
    local_gram = lax.dot_general(powered, powered, across, precision=lax.Precision.HIGHEST)
    gram_matrix = lax.psum(local_gram, "row")
    cholesky_factor = jnp.linalg.cholesky(gram_matrix)
    ortho_basis = lax.linalg.triangular_solve(
        cholesky_factor, powered, left_side=False, lower=True, transpose_a=True
    )
    own_chosen = jnp.dot(ortho_basis, picker, precision=lax.Precision.HIGHEST)
    projected = add_rows(lax.all_gather(own_chosen.astype(jnp.bfloat16), "row", axis=0, tiled=True))
    left_factor = own_chosen * math.sqrt(weight.shape[1])
    energy = lax.psum(jnp.sum(projected * projected), "row")
    spread = jnp.sqrt(energy / (weight.shape[0] * members * RANK) + 1e-06)
    right_factor = (projected / spread).astype(jnp.bfloat16)
    return (left_factor, right_factor, spread.reshape(1))


class Ring:
    def __init__(self, members):
        chips = members // 2
        order = list(range(0, chips, 2)) + list(range(chips - 1, 0, -2))
        place = {chip: at for at, chip in enumerate(order)}
        self.chips, self.far = chips, chips // 2
        self.pair = [(device, device ^ 1) for device in range(members)]
        self.ahead = []
        for at, chip in enumerate(order):
            self.ahead.append((2 * chip, 2 * order[(at + 1) % chips]))
            self.ahead.append((2 * chip + 1, 2 * order[at - 1] + 1))

        def halves(device, steps, core):
            at = place[device // 2] + (steps if device % 2 == 0 else -steps)
            chip = order[at % chips]
            return [2 * chip + core, 2 * chip + 1 - core]

        self.width, self.table = {}, []
        for device in range(members):
            core, row = device % 2, []

            def put(name, values):
                self.width[name] = (len(row), len(values))
                row.extend(values)

            for k in range(self.far + 1):
                one = k == self.far
                mine, other = halves(device, k, core), halves(device, -k, 1 - core)
                put(("sum", k), mine if k == 0 else (mine[:1] + other[:1] if one else mine + other))
                mine, other = halves(device, -k, core), halves(device, k, 1 - core)
                put(("use", k), mine if k == 0 else (mine[:1] + other[:1] if one else mine + other))
            put("core", [core])
            self.table.append(row)

    def first(self, weight, name, k):
        half = weight.shape[1] // (2 * self.chips)
        base, turns = self.width[name, k]
        return First(weight.shape[0], half, base, turns, name == "use")

    def row(self):
        table = jnp.asarray(np.array(self.table, np.int32))
        return lax.dynamic_index_in_dim(table, lax.axis_index("row"), 0, keepdims=False)


class First:
    def __init__(self, rows, half, base, turns, by_rows):
        self.half, self.base, self.turns, self.by_rows = half, base, turns, by_rows
        self.tall = rows // 4 if by_rows and rows % 128 == 0 else rows
        self.shape = (self.tall, turns * half) if by_rows else (rows, half)

    def copies(self, ids_ref, weight_ref, target_ref, sems):
        if not self.by_rows:
            start = pl.multiple_of(ids_ref[self.base] * self.half, 128)
            source = weight_ref.at[:, pl.ds(start, self.half)]
            return [pltpu.make_async_copy(source, target_ref, sems.at[0])]
        return self.strips(ids_ref, weight_ref, 0, target_ref, sems)

    def strips(self, ids_ref, weight_ref, low, target_ref, sems):
        copies = []
        for turn in range(self.turns):
            start = pl.multiple_of(ids_ref[self.base + turn] * self.half, 128)
            source = weight_ref.at[pl.ds(low, self.tall), pl.ds(start, self.half)]
            target = target_ref.at[:, pl.ds(turn * self.half, self.half)]
            copies.append(pltpu.make_async_copy(source, target, sems.at[turn]))
        return copies


def in_turn(blocks, ahead, work, prepare=None):
    for block in blocks[: ahead + 1]:
        for copy in block:
            copy.start()
    if prepare is not None:
        prepare()
    for at, block in enumerate(blocks):
        for copy in block:
            copy.wait()
        if at > 0 and at + ahead < len(blocks):
            for copy in blocks[at + ahead]:
                copy.start()
        work(at)


def columns_kernel(first, following, turns, kept, carried, ids_ref, left_ref, weight_ref, *refs):
    refs = list(refs)
    half = first.half
    sems, held_ref = refs.pop(), refs.pop()
    ready_ref = refs.pop(0) if carried else held_ref.at[turns - 1]
    next_ref = refs.pop() if following is not None else None
    blocks = [[] if carried else first.copies(ids_ref, weight_ref, ready_ref, sems.at[0])]
    for turn in range(1, turns):
        start = pl.multiple_of(ids_ref[first.base + turn] * half, 128)
        source = weight_ref.at[:, pl.ds(start, half)]
        blocks.append([pltpu.make_async_copy(source, held_ref.at[turn - 1], sems.at[turn, 0])])
    if following is not None:
        blocks.append(following.copies(ids_ref, weight_ref, next_ref, sems.at[turns]))

    def work(turn):
        if turn == turns:
            return
        block = ready_ref[...] if turn == 0 else held_ref[turn - 1]
        part = jnp.dot(left_ref[...], block, preferred_element_type=jnp.float32)
        out, at = (0, turn) if turn < kept else (1, turn - kept)
        refs[out][:, at * half : (at + 1) * half] = part.astype(refs[out].dtype)

    in_turn(blocks, 2, work)


def column_sums(left, weight, ids, first, half, split, carry, following):
    rows, wide = left.shape[1], left.shape[0]
    turns = first.turns
    kept = turns // 2 if split else turns
    out_shape = [jax.ShapeDtypeStruct((wide, kept * half), jnp.float32)]
    if split:
        out_shape.append(jax.ShapeDtypeStruct((wide, kept * half), jnp.bfloat16))
    if following is not None:
        out_shape.append(jax.ShapeDtypeStruct(following.shape, jnp.bfloat16))
    whole = pl.BlockSpec(memory_space=pltpu.VMEM)
    carried = carry is not None
    return pl.pallas_call(
        functools.partial(columns_kernel, first, following, turns, kept, carried),
        out_shape=out_shape,
        in_specs=[
            pl.BlockSpec(memory_space=pltpu.SMEM),
            whole,
            pl.BlockSpec(memory_space=pl.ANY),
        ]
        + [whole] * carried,
        out_specs=[whole] * len(out_shape),
        scratch_shapes=[
            pltpu.VMEM((turns - carried, rows, half), jnp.bfloat16),
            pltpu.SemaphoreType.DMA((turns + 1, 4)),
        ],
        compiler_params=pltpu.CompilerParams(
            vmem_limit_bytes=2 * (turns - carried) * rows * half + SPARE
        ),
        cost_estimate=pl.CostEstimate(
            flops=2 * wide * rows * turns * half,
            bytes_accessed=2 * rows * turns * half + 2 * rows * wide,
            transcendentals=0,
        ),
    )(ids, left, weight, *([carry] if carried else []))


def invert_kernel(starts, first, *refs):
    refs = list(refs)
    lanes = lax.broadcasted_iota(jnp.int32, (8, 128), 1)
    if starts:
        gram_ref, work_ref, out_ref = refs
        size = work_ref.shape[0]
        total = gram_ref[0]
        for chip in range(1, gram_ref.shape[0]):
            total = total + gram_ref[chip]
        work_ref[...] = jnp.zeros_like(work_ref)
        work_ref[:, :size] = total
    else:
        before_ref, work_ref, out_ref = refs
        size = work_ref.shape[0]
        work_ref[...] = before_ref[...]
    side = first // 16
    tall = size - 8 * first

    rows_at = 8 * first + lax.broadcasted_iota(jnp.int32, (tall, 128), 0)
    inside = lax.broadcasted_iota(jnp.int32, (8, 128), 0)

    def packed(values):
        total = values[0]
        for s in range(1, 8):
            total = jnp.where(inside == s, values[s], total)
        return total

    def panel(p, _):
        raw = [work_ref[pl.ds(8 * p, 8), :128], work_ref[pl.ds(8 * p, 8), 128:]]
        entry, ratio, inverse = {}, {}, []
        for s in range(8):
            at = jnp.full((8, 128), 8 * p + s - 128 * side, jnp.int32)
            column = jnp.take_along_axis(raw[side], at, axis=1)
            for r in range(s + 1):
                entry[r, s] = jnp.broadcast_to(column[r : r + 1], (8, 128))
        for s in range(8):
            inverse.append(1.0 / entry[s, s])
            for t in range(s + 1, 8):
                ratio[t, s] = entry[s, t] * inverse[s]
            for t in range(s + 1, 8):
                for u in range(t, 8):
                    entry[t, u] = entry[t, u] - ratio[t, s] * entry[s, u]
        low = 8 * p - 128 * side
        own = (lanes >= low) & (lanes < low + 8)
        row = []
        for t in range(8):
            halves = [jnp.broadcast_to(part[t : t + 1], (8, 128)) for part in raw]
            unit = jnp.where(lanes == low + t, 1.0, 0.0)
            halves[side] = jnp.where(own, unit, halves[side])
            for s in range(t):
                halves = [half - ratio[t, s] * done for half, done in zip(halves, row[s])]
            row.append(halves)
        scale = lax.rsqrt(packed([entry[s, s] for s in range(8)]))
        inverses = packed(inverse)
        factors = []
        for half in range(2):
            whole = packed([row[s][half] for s in range(8)])
            beyond = lanes + 128 * half >= 8 * p + 8
            strip = jnp.where(beyond, 0.0, whole * scale)
            out_ref[pl.ds(8 * (p - first), 8), 128 * half : min(128 * half + 128, size)] = strip[
                :, : min(128, size - 128 * half)
            ]
            factors.append(jnp.where(beyond, whole * inverses, 0.0).T)
        factor = jnp.concatenate(factors, 0)[8 * first : size]
        spread = lambda x: jnp.tile(x, (tall // 8, 1))
        after = rows_at >= 8 * p + 8
        for half in range(2):
            place = (slice(8 * first, size), slice(128 * half, 128 * half + 128))
            rest = work_ref[place]
            if half == side:
                rest = jnp.where(spread(own) & after, 0.0, rest)
            for s in range(8):
                rest = rest - jnp.broadcast_to(factor[:, s : s + 1], (tall, 128)) * spread(row[s][half])
            work_ref[place] = rest
        return 0

    lax.fori_loop(first, first + out_ref.shape[0] // 8, panel, 0)


def invert_panels(first, size, source):
    tall = min(64, size - 8 * first)
    whole = pl.BlockSpec(memory_space=pltpu.VMEM)
    return pl.pallas_call(
        functools.partial(invert_kernel, first == 0, first),
        out_shape=[
            jax.ShapeDtypeStruct((size, 256), jnp.float32),
            jax.ShapeDtypeStruct((tall, size), jnp.float32),
        ],
        in_specs=[whole],
        out_specs=[whole] * 2,
        input_output_aliases={0: 0} if first else {},
        compiler_params=pltpu.CompilerParams(vmem_limit_bytes=SPARE),
        cost_estimate=pl.CostEstimate(flops=10**9, bytes_accessed=2 * 10**7, transcendentals=0),
    )(source)


def rows_kernel(first, following, pieces, spans, chained, turned, grams, ids_ref, weight_ref, *refs):
    refs = list(refs)
    ready_ref = refs.pop(0)
    piece_refs = [refs.pop(0) for _ in range(pieces)]
    before_ref = refs.pop(0) if chained else None
    if grams and chained:
        refs.pop(0)
    out_ref = refs.pop(0)
    gram_ref = refs.pop(0) if grams else None
    next_ref = refs.pop(0) if following is not None else None
    held_ref, joined_ref, sems = refs[:3]
    total_ref = refs[3] if turned else out_ref
    half, turns = first.half, first.turns
    halves = turns // pieces
    blocks = [[]]
    for number, (low, tall) in enumerate(spans[1:], 1):
        target_ref = held_ref.at[pl.ds(low - first.tall, tall)]
        blocks.append(first.strips(ids_ref, weight_ref, low, target_ref, sems.at[number]))
    if following is not None:
        blocks.append(following.copies(ids_ref, weight_ref, next_ref, sems.at[0]))

    def piece(turn):
        at = turn % halves * half
        return piece_refs[turn // halves][:, at : at + half]

    def prepare():
        for turn in range(turns):
            upright = piece(turn).astype(jnp.float32).T.astype(jnp.bfloat16)
            joined_ref[turn * half : (turn + 1) * half, :] = upright

    def work(number):
        if number == len(spans):
            return
        low, tall = spans[number]
        block_ref, at = (held_ref, low - first.tall) if number else (ready_ref, 0)
        parts = [
            jnp.dot(
                block_ref[at + side * tall // 2 : at + (side + 1) * tall // 2, :],
                joined_ref[...],
                preferred_element_type=jnp.float32,
            )
            for side in range(2)
        ]
        for side, part in enumerate(parts):
            place = (slice(low + side * tall // 2, low + (side + 1) * tall // 2), slice(None))
            total_ref[place] = before_ref[place] + part if chained else part
        if grams and 0 < number <= turns // 2:
            squares = [
                jnp.dot(
                    piece(turn),
                    joined_ref[turn * half : (turn + 1) * half, :],
                    preferred_element_type=jnp.float32,
                )
                for turn in range(2 * number - 2, 2 * number)
            ]
            gram_ref[ids_ref[first.base + 2 * number - 2] // 2] = squares[0] + squares[1]

    in_turn(blocks, 2, work, prepare)
    if turned:
        out_ref[...] = total_ref[...].T.astype(out_ref.dtype)


def row_products(weight, pieces, ids, first, before, turned, grams, carry, following):
    rows, wide = weight.shape[0], pieces[0].shape[0]
    turns, half = first.turns, first.half
    chips = weight.shape[1] // (2 * half)
    spans = [(low, first.tall) for low in range(0, rows, first.tall)]
    whole = pl.BlockSpec(memory_space=pltpu.VMEM)
    operands = [ids, weight, carry, *pieces]
    in_specs = [pl.BlockSpec(memory_space=pltpu.SMEM), pl.BlockSpec(memory_space=pl.ANY), whole]
    in_specs += [whole] * len(pieces)
    kind = jnp.bfloat16 if turned and grams is None else jnp.float32
    out_shape = [jax.ShapeDtypeStruct((wide, rows) if turned else (rows, wide), kind)]
    aliases = {}
    if before is not None:
        if not turned:
            aliases[len(operands)] = 0
        operands.append(before)
        in_specs.append(whole)
    if grams is not None:
        if before is not None:
            aliases[len(operands)] = 1
            operands.append(grams)
            in_specs.append(whole)
        out_shape.append(jax.ShapeDtypeStruct((chips, wide, wide), jnp.float32))
    if following is not None:
        out_shape.append(jax.ShapeDtypeStruct(following.shape, jnp.bfloat16))
    depth = turns * half
    return pl.pallas_call(
        functools.partial(
            rows_kernel,
            first,
            following,
            len(pieces),
            spans,
            before is not None,
            turned,
            grams is not None,
        ),
        out_shape=out_shape,
        in_specs=in_specs,
        out_specs=[whole] * len(out_shape),
        scratch_shapes=[
            pltpu.VMEM((max(rows - first.tall, 16), depth), jnp.bfloat16),
            pltpu.VMEM((depth, wide), jnp.bfloat16),
            pltpu.SemaphoreType.DMA((len(spans) + 1, 4)),
        ]
        + [pltpu.VMEM((rows, wide), jnp.float32)] * turned,
        input_output_aliases=aliases,
        compiler_params=pltpu.CompilerParams(
            vmem_limit_bytes=2 * depth * (rows - first.tall + 256) + 1024 * rows * turned + SPARE
        ),
        cost_estimate=pl.CostEstimate(
            flops=2 * rows * wide * turns * half,
            bytes_accessed=2 * rows * turns * half + 8 * rows * wide,
            transcendentals=0,
        ),
    )(*operands)


def ring_sum(ring, ids, left, weight, half, carry):
    got = None
    for k in range(ring.far, 0, -1):
        first = ring.first(weight, "sum", k)
        keep, give, carry = column_sums(
            left, weight, ids, first, half, True, carry, ring.first(weight, "sum", k - 1)
        )
        given = lax.ppermute(give, "row", ring.pair)
        if got is not None:
            got = got.astype(jnp.float32)
            size = got.shape[1]
            if size < keep.shape[1]:
                keep = jnp.concatenate([keep[:, :size] + got, keep[:, size:]], 1)
            else:
                keep = keep + got
            keep, given = lax.optimization_barrier((keep, given))
        total = (keep + given.astype(jnp.float32)).astype(jnp.bfloat16)
        total, left = lax.optimization_barrier((total, left))
        got = lax.ppermute(total, "row", ring.ahead)
    first = ring.first(weight, "sum", 0)
    keep, carry = column_sums(
        left, weight, ids, first, half, False, carry, ring.first(weight, "use", 0)
    )
    mine = keep + got.astype(jnp.float32)
    other = lax.ppermute(mine, "row", ring.pair)
    return mine + jnp.concatenate([other[:, half:], other[:, :half]], 1), carry


def ring_apply(ring, ids, chunk, weight, half, with_grams, carry, following):
    before, grams = None, () if with_grams else None
    moving = chunk
    for k in range(ring.far + 1):
        if k == 0:
            pieces = [chunk]
        else:
            moving = lax.ppermute(moving if k < ring.far else moving[:, :half], "row", ring.ahead)
            moving, before = lax.optimization_barrier((moving, before))
            pieces = [moving, lax.ppermute(moving, "row", ring.pair)]
        last = k == ring.far
        then = following if last else ring.first(weight, "use", k + 1)
        first = ring.first(weight, "use", k)
        outs = list(
            row_products(
                weight, pieces, ids, first, before, last, grams, carry, then
            )
        )
        carry = outs.pop() if then is not None else None
        before = outs.pop(0)
        grams = outs.pop() if outs else None
    return before, grams, carry


def sum_beside_inverse(value, ring, ids, grams):
    size = value.shape[0]
    rows = size // 2
    core = ring.width["core"][0]
    first = ids[core : core + 1, None] == 0
    low, high = value[:rows], value[rows:]
    part = jnp.where(first, low, high)
    part = part + lax.ppermute(jnp.where(first, high, low), "row", ring.pair)
    hops = [
        [(device, device ^ (2 << bit)) for device in range(2 * ring.chips)]
        for bit in reversed(range(ring.chips.bit_length() - 1))
    ]
    panels = list(range(0, size // 8, 8))
    work, strips = grams, []
    for at in range(max(len(hops), len(panels))):
        if at < len(hops):
            got = lax.ppermute(part, "row", hops[at])
        if at < len(panels):
            work, strip = invert_panels(panels[at], size, work)
            strips.append(strip)
        if at < len(hops):
            got, work = lax.optimization_barrier((got, work))
            part = part + got
    other = lax.ppermute(part, "row", ring.pair)
    total = jnp.concatenate([jnp.where(first, part, other), jnp.where(first, other, part)], 0)
    return total, jnp.concatenate(strips, 0)


def ring_body(ring, weight, test_matrix, rank_mask):
    highest = lax.Precision.HIGHEST
    rows, features = weight.shape
    half = features // (2 * ring.chips)
    ids = ring.row()
    picker = selector(rank_mask, RANK)
    sketch, carry = ring_sum(ring, ids, test_matrix.T, weight, half, None)
    sketch = sketch.astype(jnp.bfloat16)
    again = ring.first(weight, "sum", ring.far)
    mixed, _, carry = ring_apply(ring, ids, sketch, weight, half, False, carry, again)
    powered, carry = ring_sum(ring, ids, mixed, weight, half, carry)
    powered_b = powered.astype(jnp.bfloat16)
    image, grams, _ = ring_apply(ring, ids, powered_b, weight, half, True, carry, None)
    image_b = image.astype(jnp.bfloat16)
    square = lax.dot_general(
        image_b, image_b, (((1,), (1,)), ((), ())), preferred_element_type=jnp.float32
    )
    square, inverse = sum_beside_inverse(square, ring, ids, grams)
    change = lax.dot_general(inverse, picker, (((0,), (0,)), ((), ())), precision=highest)
    own = powered[:, :half]
    left_factor = lax.dot_general(
        own, change, (((0,), (0,)), ((), ())), precision=highest
    ) * math.sqrt(features)
    energy = jnp.sum(square * jnp.dot(change, change.T, precision=highest), keepdims=True)
    spread = jnp.sqrt(energy / (rows * 2 * ring.chips * RANK) + 1e-06)
    right_factor = lax.dot_general(
        image, change / spread, (((0,), (0,)), ((), ())), precision=lax.Precision.HIGH
    ).astype(jnp.bfloat16)
    return (left_factor, right_factor, spread.reshape(1))


def body(weight, test_matrix, rank_mask):
    members = lax.axis_size("row")
    chips = members // 2
    paired = members % 2 == 0 and chips > 2 and chips & (chips - 1) == 0
    if not paired or weight.shape[1] % (members * 128):
        return plain_body(weight, test_matrix, rank_mask)
    return ring_body(Ring(members), weight, test_matrix, rank_mask)


def solution(mesh):
    in_specs = (P(("groups", "row"), None), P("row", None), P("groups"))
    out_specs = (P(("groups", "row"), None), P(("groups", "row"), None), P("groups"))
    return jax.shard_map(body, mesh=mesh, in_specs=in_specs, out_specs=out_specs, check_vma=False)
```

```python
import functools
import math

import jax
import jax.numpy as jnp
import numpy as np
from jax import lax
from jax.experimental import pallas as pl
from jax.experimental.pallas import tpu as pltpu
from jax.sharding import PartitionSpec as P

RANK = 224
SPARE = 4 * 1024 * 1024


def selector(rank_mask, kept):
    at = lax.iota(jnp.int32, rank_mask.shape[0])
    positions = jnp.sum(jnp.where(at[:, None] <= at[None, :], rank_mask[:, None], 0), axis=0) - 1
    targets = lax.iota(jnp.int32, kept)
    matches = (rank_mask[:, None] == 1) & (positions[:, None] == targets[None, :])
    return matches.astype(jnp.float32)


def plain_body(weight, test_matrix, rank_mask):
    across = (((0,), (0,)), ((), ()))
    members = lax.axis_size("row")
    picker = selector(rank_mask, RANK)
    sketch_part = lax.psum_scatter(
        lax.dot_general(weight, test_matrix, across, preferred_element_type=jnp.float32),
        "row",
        scatter_dimension=0,
        tiled=True,
    ).astype(jnp.bfloat16)

    def add_rows(piece_rows):
        return jnp.dot(weight, piece_rows, preferred_element_type=jnp.float32)

    mixed = add_rows(lax.all_gather(sketch_part, "row", axis=0, tiled=True)).astype(jnp.bfloat16)
    powered = lax.psum_scatter(
        lax.dot_general(weight, mixed, across, preferred_element_type=jnp.float32),
        "row",
        scatter_dimension=0,
        tiled=True,
    )
    local_gram = lax.dot_general(powered, powered, across, precision=lax.Precision.HIGHEST)
    gram_matrix = lax.psum(local_gram, "row")
    cholesky_factor = jnp.linalg.cholesky(gram_matrix)
    ortho_basis = lax.linalg.triangular_solve(
        cholesky_factor, powered, left_side=False, lower=True, transpose_a=True
    )
    own_chosen = jnp.dot(ortho_basis, picker, precision=lax.Precision.HIGHEST)
    projected = add_rows(lax.all_gather(own_chosen.astype(jnp.bfloat16), "row", axis=0, tiled=True))
    left_factor = own_chosen * math.sqrt(weight.shape[1])
    energy = lax.psum(jnp.sum(projected * projected), "row")
    spread = jnp.sqrt(energy / (weight.shape[0] * members * RANK) + 1e-06)
    right_factor = (projected / spread).astype(jnp.bfloat16)
    return (left_factor, right_factor, spread.reshape(1))


class Ring:
    def __init__(self, members):
        chips = members // 2
        order = list(range(0, chips, 2)) + list(range(chips - 1, 0, -2))
        place = {chip: at for at, chip in enumerate(order)}
        self.chips, self.far = chips, chips // 2
        self.pair = [(device, device ^ 1) for device in range(members)]
        self.ahead = []
        for at, chip in enumerate(order):
            self.ahead.append((2 * chip, 2 * order[(at + 1) % chips]))
            self.ahead.append((2 * chip + 1, 2 * order[at - 1] + 1))

        def halves(device, steps, core):
            at = place[device // 2] + (steps if device % 2 == 0 else -steps)
            chip = order[at % chips]
            return [2 * chip + core, 2 * chip + 1 - core]

        self.width, self.table = {}, []
        for device in range(members):
            core, row = device % 2, []

            def put(name, values):
                self.width[name] = (len(row), len(values))
                row.extend(values)

            for k in range(self.far + 1):
                one = k == self.far
                mine, other = halves(device, k, core), halves(device, -k, 1 - core)
                put(("keep", k), mine[:1] if one else mine)
                put(("give", k), [] if k == 0 else other[:1] if one else other)
                mine, other = halves(device, -k, core), halves(device, k, 1 - core)
                put(("use", k), mine if k == 0 else (mine[:1] + other[:1] if one else mine + other))
            put("core", [core])
            self.table.append(row)

    def first(self, weight, name, k):
        half = weight.shape[1] // (2 * self.chips)
        base, turns = self.width[name, k]
        return First(weight.shape[0], half, base, turns, name == "use")

    def calls(self):
        far = self.far
        calls = [[("keep", far), ("give", far), ("give", far - 1)]]
        for k in range(far - 1, 0, -1):
            calls.append([("keep", k), ("give", k - 1) if k > 1 else ("keep", 0)])
        return calls

    def row(self):
        table = jnp.asarray(np.array(self.table, np.int32))
        return lax.dynamic_index_in_dim(table, lax.axis_index("row"), 0, keepdims=False)


class First:
    def __init__(self, rows, half, base, turns, by_rows):
        self.half, self.base, self.turns, self.by_rows = half, base, turns, by_rows
        self.rows = rows
        self.tall = -(-rows // 512) * 128 if by_rows and rows % 128 == 0 else rows
        self.shape = (self.tall, turns * half) if by_rows else (rows, half)

    def copies(self, ids_ref, weight_ref, target_ref, sems):
        if not self.by_rows:
            start = pl.multiple_of(ids_ref[self.base] * self.half, 128)
            source = weight_ref.at[:, pl.ds(start, self.half)]
            return [pltpu.make_async_copy(source, target_ref, sems.at[0])]
        return self.strips(ids_ref, weight_ref, 0, target_ref, sems)

    def strips(self, ids_ref, weight_ref, low, target_ref, sems):
        copies = []
        for turn in range(self.turns):
            start = pl.multiple_of(ids_ref[self.base + turn] * self.half, 128)
            source = weight_ref.at[pl.ds(low, min(self.tall, self.rows - low)), pl.ds(start, self.half)]
            target = target_ref.at[:, pl.ds(turn * self.half, self.half)]
            copies.append(pltpu.make_async_copy(source, target, sems.at[turn]))
        return copies


def in_turn(blocks, ahead, work, prepare=None):
    for block in blocks[: ahead + 1]:
        for copy in block:
            copy.start()
    if prepare is not None:
        prepare()
    for at, block in enumerate(blocks):
        for copy in block:
            copy.wait()
        if at > 0 and at + ahead < len(blocks):
            for copy in blocks[at + ahead]:
                copy.start()
        work(at)


def columns_kernel(half, entries, following, outs, carried, ids_ref, left_ref, weight_ref, *refs):
    refs = list(refs)
    sems, held_ref = refs.pop(), refs.pop()
    turns = len(entries)
    ready_ref = refs.pop(0) if carried else held_ref.at[turns - 1]
    next_ref = refs.pop()
    blocks = [[]] if carried else []
    for turn in range(len(blocks), turns):
        start = pl.multiple_of(ids_ref[entries[turn]] * half, 128)
        source = weight_ref.at[:, pl.ds(start, half)]
        target_ref = held_ref.at[turn - 1] if turn else ready_ref
        blocks.append([pltpu.make_async_copy(source, target_ref, sems.at[turn, 0])])
    blocks.append(following.copies(ids_ref, weight_ref, next_ref, sems.at[turns]))
    places = [(out, at) for out, count in enumerate(outs) for at in range(count)]

    def work(turn):
        if turn == turns:
            return
        block = held_ref[turn - 1] if turn else ready_ref[...]
        part = jnp.dot(left_ref[...], block, preferred_element_type=jnp.float32)
        out, at = places[turn]
        refs[out][:, at * half : (at + 1) * half] = part.astype(refs[out].dtype)

    in_turn(blocks, 2, work)


def column_sums(left, weight, ids, ring, groups, carry, following):
    rows, wide = left.shape[1], left.shape[0]
    half = weight.shape[1] // (2 * ring.chips)
    entries, outs, out_shape = [], [], []
    for name, k in groups:
        base, count = ring.width[name, k]
        entries += range(base, base + count)
        outs.append(count)
        kind = jnp.float32 if name == "keep" else jnp.bfloat16
        out_shape.append(jax.ShapeDtypeStruct((wide, count * half), kind))
    turns = len(entries)
    out_shape.append(jax.ShapeDtypeStruct(following.shape, jnp.bfloat16))
    whole = pl.BlockSpec(memory_space=pltpu.VMEM)
    carried = carry is not None
    return pl.pallas_call(
        functools.partial(columns_kernel, half, entries, following, outs, carried),
        out_shape=out_shape,
        in_specs=[
            pl.BlockSpec(memory_space=pltpu.SMEM),
            whole,
            pl.BlockSpec(memory_space=pl.ANY),
        ]
        + [whole] * carried,
        out_specs=[whole] * len(out_shape),
        scratch_shapes=[
            pltpu.VMEM((turns - carried, rows, half), jnp.bfloat16),
            pltpu.SemaphoreType.DMA((turns + 1, 4)),
        ],
        compiler_params=pltpu.CompilerParams(
            vmem_limit_bytes=2 * (turns - carried) * rows * half + SPARE
        ),
        cost_estimate=pl.CostEstimate(
            flops=2 * wide * rows * turns * half,
            bytes_accessed=2 * rows * turns * half + 2 * rows * wide,
            transcendentals=0,
        ),
    )(ids, left, weight, *([carry] if carried else []))


def invert_kernel(starts, first, *refs):
    refs = list(refs)
    lanes = lax.broadcasted_iota(jnp.int32, (8, 128), 1)
    if starts:
        gram_ref, work_ref, out_ref = refs
        size = work_ref.shape[0]
        total = gram_ref[0]
        for chip in range(1, gram_ref.shape[0]):
            total = total + gram_ref[chip]
        work_ref[...] = jnp.zeros_like(work_ref)
        work_ref[:, :size] = total
    else:
        before_ref, work_ref, out_ref = refs
        size = work_ref.shape[0]
        work_ref[...] = before_ref[...]
    side = first // 16
    tall = size - 8 * first

    rows_at = 8 * first + lax.broadcasted_iota(jnp.int32, (tall, 128), 0)
    inside = lax.broadcasted_iota(jnp.int32, (8, 128), 0)

    def packed(values):
        total = values[0]
        for s in range(1, 8):
            total = jnp.where(inside == s, values[s], total)
        return total

    def panel(p, _):
        raw = [work_ref[pl.ds(8 * p, 8), :128], work_ref[pl.ds(8 * p, 8), 128:]]
        entry, ratio, inverse = {}, {}, []
        for s in range(8):
            at = jnp.full((8, 128), 8 * p + s - 128 * side, jnp.int32)
            column = jnp.take_along_axis(raw[side], at, axis=1)
            for r in range(s + 1):
                entry[r, s] = jnp.broadcast_to(column[r : r + 1], (8, 128))
        for s in range(8):
            inverse.append(1.0 / entry[s, s])
            for t in range(s + 1, 8):
                ratio[t, s] = entry[s, t] * inverse[s]
            for t in range(s + 1, 8):
                for u in range(t, 8):
                    entry[t, u] = entry[t, u] - ratio[t, s] * entry[s, u]
        low = 8 * p - 128 * side
        own = (lanes >= low) & (lanes < low + 8)
        row = []
        for t in range(8):
            halves = [jnp.broadcast_to(part[t : t + 1], (8, 128)) for part in raw]
            unit = jnp.where(lanes == low + t, 1.0, 0.0)
            halves[side] = jnp.where(own, unit, halves[side])
            for s in range(t):
                halves = [half - ratio[t, s] * done for half, done in zip(halves, row[s])]
            row.append(halves)
        scale = lax.rsqrt(packed([entry[s, s] for s in range(8)]))
        inverses = packed(inverse)
        factors = []
        for half in range(2):
            whole = packed([row[s][half] for s in range(8)])
            beyond = lanes + 128 * half >= 8 * p + 8
            strip = jnp.where(beyond, 0.0, whole * scale)
            out_ref[pl.ds(8 * (p - first), 8), 128 * half : min(128 * half + 128, size)] = strip[
                :, : min(128, size - 128 * half)
            ]
            factors.append(jnp.where(beyond, whole * inverses, 0.0).T)
        factor = jnp.concatenate(factors, 0)[8 * first : size]
        spread = lambda x: jnp.tile(x, (tall // 8, 1))
        after = rows_at >= 8 * p + 8
        for half in range(2):
            place = (slice(8 * first, size), slice(128 * half, 128 * half + 128))
            rest = work_ref[place]
            if half == side:
                rest = jnp.where(spread(own) & after, 0.0, rest)
            for s in range(8):
                rest = rest - jnp.broadcast_to(factor[:, s : s + 1], (tall, 128)) * spread(row[s][half])
            work_ref[place] = rest
        return 0

    lax.fori_loop(first, first + out_ref.shape[0] // 8, panel, 0)


def invert_panels(first, size, source):
    tall = min(64, size - 8 * first)
    whole = pl.BlockSpec(memory_space=pltpu.VMEM)
    return pl.pallas_call(
        functools.partial(invert_kernel, first == 0, first),
        out_shape=[
            jax.ShapeDtypeStruct((size, 256), jnp.float32),
            jax.ShapeDtypeStruct((tall, size), jnp.float32),
        ],
        in_specs=[whole],
        out_specs=[whole] * 2,
        input_output_aliases={0: 0} if first else {},
        compiler_params=pltpu.CompilerParams(vmem_limit_bytes=SPARE),
        cost_estimate=pl.CostEstimate(flops=10**9, bytes_accessed=2 * 10**7, transcendentals=0),
    )(source)


def rows_kernel(first, following, pieces, spans, chained, turned, grams, ids_ref, weight_ref, *refs):
    refs = list(refs)
    ready_ref = refs.pop(0)
    piece_refs = [refs.pop(0) for _ in range(pieces)]
    before_ref = refs.pop(0) if chained else None
    if grams and chained:
        refs.pop(0)
    out_ref = refs.pop(0)
    gram_ref = refs.pop(0) if grams else None
    next_ref = refs.pop(0) if following is not None else None
    held_ref, joined_ref, sems = refs
    half, turns = first.half, first.turns
    halves = turns // pieces
    blocks = [[]]
    for number, (low, tall) in enumerate(spans[1:], 1):
        target_ref = held_ref.at[pl.ds(low - first.tall, tall)]
        blocks.append(first.strips(ids_ref, weight_ref, low, target_ref, sems.at[number]))
    if following is not None:
        blocks.append(following.copies(ids_ref, weight_ref, next_ref, sems.at[0]))

    def piece(turn):
        at = turn % halves * half
        return piece_refs[turn // halves][:, at : at + half]

    def prepare():
        for turn in range(turns):
            upright = piece(turn).astype(jnp.float32).T.astype(jnp.bfloat16)
            joined_ref[turn * half : (turn + 1) * half, :] = upright

    def work(number):
        if number == len(spans):
            return
        low, tall = spans[number]
        block_ref, at = (held_ref, low - first.tall) if number else (ready_ref, 0)
        parts = [
            jnp.dot(
                block_ref[at + side * tall // 2 : at + (side + 1) * tall // 2, :],
                joined_ref[...],
                preferred_element_type=jnp.float32,
            )
            for side in range(2)
        ]
        for side, part in enumerate(parts):
            place = (slice(low + side * tall // 2, low + (side + 1) * tall // 2), slice(None))
            parts[side] = before_ref[place] + part if chained else part
            if not turned:
                out_ref[place] = parts[side]
        if turned:
            out_ref[:, low : low + tall] = jnp.concatenate(parts, 0).T.astype(out_ref.dtype)
        if grams and 0 < number <= turns // 2:
            squares = [
                jnp.dot(
                    piece(turn),
                    joined_ref[turn * half : (turn + 1) * half, :],
                    preferred_element_type=jnp.float32,
                )
                for turn in range(2 * number - 2, 2 * number)
            ]
            gram_ref[ids_ref[first.base + 2 * number - 2] // 2] = squares[0] + squares[1]

    in_turn(blocks, 2, work, prepare)


def row_products(weight, pieces, ids, first, before, turned, grams, carry, following):
    rows, wide = weight.shape[0], pieces[0].shape[0]
    turns, half = first.turns, first.half
    chips = weight.shape[1] // (2 * half)
    spans = [(low, min(first.tall, rows - low)) for low in range(0, rows, first.tall)]
    whole = pl.BlockSpec(memory_space=pltpu.VMEM)
    operands = [ids, weight, carry, *pieces]
    in_specs = [pl.BlockSpec(memory_space=pltpu.SMEM), pl.BlockSpec(memory_space=pl.ANY), whole]
    in_specs += [whole] * len(pieces)
    kind = jnp.bfloat16 if turned and grams is None else jnp.float32
    out_shape = [jax.ShapeDtypeStruct((wide, rows) if turned else (rows, wide), kind)]
    aliases = {}
    if before is not None:
        if not turned:
            aliases[len(operands)] = 0
        operands.append(before)
        in_specs.append(whole)
    if grams is not None:
        if before is not None:
            aliases[len(operands)] = 1
            operands.append(grams)
            in_specs.append(whole)
        out_shape.append(jax.ShapeDtypeStruct((chips, wide, wide), jnp.float32))
    if following is not None:
        out_shape.append(jax.ShapeDtypeStruct(following.shape, jnp.bfloat16))
    depth = turns * half
    return pl.pallas_call(
        functools.partial(
            rows_kernel,
            first,
            following,
            len(pieces),
            spans,
            before is not None,
            turned,
            grams is not None,
        ),
        out_shape=out_shape,
        in_specs=in_specs,
        out_specs=[whole] * len(out_shape),
        scratch_shapes=[
            pltpu.VMEM((max(rows - first.tall, 16), depth), jnp.bfloat16),
            pltpu.VMEM((depth, wide), jnp.bfloat16),
            pltpu.SemaphoreType.DMA((len(spans) + 1, 4)),
        ],
        input_output_aliases=aliases,
        compiler_params=pltpu.CompilerParams(
            vmem_limit_bytes=2 * depth * (rows - first.tall + 256) + SPARE
        ),
        cost_estimate=pl.CostEstimate(
            flops=2 * rows * wide * turns * half,
            bytes_accessed=2 * rows * turns * half + 8 * rows * wide,
            transcendentals=0,
        ),
    )(*operands)


def ring_sum(ring, ids, left, weight, half, carry):
    calls = ring.calls()
    got, parts = None, {}
    for number, groups in enumerate(calls):
        k = ring.far - number
        if number:
            left, parts["give", k] = lax.optimization_barrier((left, parts["give", k]))
        if number + 1 < len(calls):
            following = ring.first(weight, *calls[number + 1][0])
        else:
            following = ring.first(weight, "use", 0)
        *outs, carry = column_sums(left, weight, ids, ring, groups, carry, following)
        for (name, at), out in zip(groups, outs):
            parts[name, at] = lax.ppermute(out, "row", ring.pair) if name == "give" else out
        keep, given = parts["keep", k], parts["give", k]
        if got is not None:
            got = got.astype(jnp.float32)
            size = got.shape[1]
            if size < keep.shape[1]:
                keep = jnp.concatenate([keep[:, :size] + got, keep[:, size:]], 1)
            else:
                keep = keep + got
            keep, given = lax.optimization_barrier((keep, given))
        total = (keep + given.astype(jnp.float32)).astype(jnp.bfloat16)
        total, left = lax.optimization_barrier((total, left))
        got = lax.ppermute(total, "row", ring.ahead)
    keep = parts["keep", 0]
    swap = lambda x: jnp.concatenate([x[:, half:], x[:, :half]], 1)
    own = keep + swap(lax.ppermute(keep, "row", ring.pair))
    own, got = lax.optimization_barrier((own, got))
    other = swap(lax.ppermute(got, "row", ring.pair))
    return own + (got.astype(jnp.float32) + other.astype(jnp.float32)), carry


def ring_apply(ring, ids, chunk, weight, half, with_grams, carry, following):
    before, grams = None, () if with_grams else None
    moving = chunk
    for k in range(ring.far + 1):
        if k == 0:
            pieces = [chunk]
        else:
            moving = lax.ppermute(moving if k < ring.far else moving[:, :half], "row", ring.ahead)
            moving, before = lax.optimization_barrier((moving, before))
            pieces = [moving, lax.ppermute(moving, "row", ring.pair)]
        last = k == ring.far
        then = following if last else ring.first(weight, "use", k + 1)
        first = ring.first(weight, "use", k)
        outs = list(
            row_products(
                weight, pieces, ids, first, before, last, grams, carry, then
            )
        )
        carry = outs.pop() if then is not None else None
        before = outs.pop(0)
        grams = outs.pop() if outs else None
    return before, grams, carry


def sum_beside_inverse(value, ring, ids, grams):
    size = value.shape[0]
    rows = size // 2
    core = ring.width["core"][0]
    first = ids[core : core + 1, None] == 0
    low, high = value[:rows], value[rows:]
    part = jnp.where(first, low, high)
    part = part + lax.ppermute(jnp.where(first, high, low), "row", ring.pair)
    hops = [
        [(device, device ^ (2 << bit)) for device in range(2 * ring.chips)]
        for bit in reversed(range(ring.chips.bit_length() - 1))
    ]
    panels = list(range(0, size // 8, 8))
    work, strips = grams, []
    for at in range(max(len(hops), len(panels))):
        if at < len(hops):
            got = lax.ppermute(part, "row", hops[at])
        if at < len(panels):
            work, strip = invert_panels(panels[at], size, work)
            strips.append(strip)
        if at < len(hops):
            got, work = lax.optimization_barrier((got, work))
            part = part + got
    other = lax.ppermute(part, "row", ring.pair)
    total = jnp.concatenate([jnp.where(first, part, other), jnp.where(first, other, part)], 0)
    return total, jnp.concatenate(strips, 0)


def ring_body(ring, weight, test_matrix, rank_mask):
    highest = lax.Precision.HIGHEST
    rows, features = weight.shape
    half = features // (2 * ring.chips)
    ids = ring.row()
    picker = selector(rank_mask, RANK)
    sketch, carry = ring_sum(ring, ids, test_matrix.T, weight, half, None)
    sketch = sketch.astype(jnp.bfloat16)
    again = ring.first(weight, "keep", ring.far)
    mixed, _, carry = ring_apply(ring, ids, sketch, weight, half, False, carry, again)
    powered, carry = ring_sum(ring, ids, mixed, weight, half, carry)
    powered_b = powered.astype(jnp.bfloat16)
    image, grams, _ = ring_apply(ring, ids, powered_b, weight, half, True, carry, None)
    image_b = image.astype(jnp.bfloat16)
    square = lax.dot_general(
        image_b, image_b, (((1,), (1,)), ((), ())), preferred_element_type=jnp.float32
    )
    square, inverse = sum_beside_inverse(square, ring, ids, grams)
    change = lax.dot_general(inverse, picker, (((0,), (0,)), ((), ())), precision=highest)
    own = powered[:, :half]
    left_factor = lax.dot_general(
        own, change, (((0,), (0,)), ((), ())), precision=highest
    ) * math.sqrt(features)
    energy = jnp.sum(square * jnp.dot(change, change.T, precision=highest), keepdims=True)
    spread = jnp.sqrt(energy / (rows * 2 * ring.chips * RANK) + 1e-06)
    right_factor = lax.dot_general(
        image, change / spread, (((0,), (0,)), ((), ())), precision=lax.Precision.HIGH
    ).astype(jnp.bfloat16)
    return (left_factor, right_factor, spread.reshape(1))


def body(weight, test_matrix, rank_mask):
    members = lax.axis_size("row")
    chips = members // 2
    paired = members % 2 == 0 and chips > 2 and chips & (chips - 1) == 0
    if not paired or weight.shape[1] % (members * 128):
        return plain_body(weight, test_matrix, rank_mask)
    return ring_body(Ring(members), weight, test_matrix, rank_mask)


def solution(mesh):
    in_specs = (P(("groups", "row"), None), P("row", None), P("groups"))
    out_specs = (P(("groups", "row"), None), P(("groups", "row"), None), P("groups"))
    return jax.shard_map(body, mesh=mesh, in_specs=in_specs, out_specs=out_specs, check_vma=False)
```

```python
import functools
import math

import jax
import jax.numpy as jnp
import numpy as np
from jax import lax
from jax.experimental import pallas as pl
from jax.experimental.pallas import tpu as pltpu
from jax.sharding import PartitionSpec as P

RANK = 224
SPARE = 4 * 1024 * 1024


def selector(rank_mask, kept):
    at = lax.iota(jnp.int32, rank_mask.shape[0])
    positions = jnp.sum(jnp.where(at[:, None] <= at[None, :], rank_mask[:, None], 0), axis=0) - 1
    targets = lax.iota(jnp.int32, kept)
    matches = (rank_mask[:, None] == 1) & (positions[:, None] == targets[None, :])
    return matches.astype(jnp.float32)


def plain_body(weight, test_matrix, rank_mask):
    across = (((0,), (0,)), ((), ()))
    members = lax.axis_size("row")
    picker = selector(rank_mask, RANK)
    sketch_part = lax.psum_scatter(
        lax.dot_general(weight, test_matrix, across, preferred_element_type=jnp.float32),
        "row",
        scatter_dimension=0,
        tiled=True,
    ).astype(jnp.bfloat16)

    def add_rows(piece_rows):
        return jnp.dot(weight, piece_rows, preferred_element_type=jnp.float32)

    mixed = add_rows(lax.all_gather(sketch_part, "row", axis=0, tiled=True)).astype(jnp.bfloat16)
    powered = lax.psum_scatter(
        lax.dot_general(weight, mixed, across, preferred_element_type=jnp.float32),
        "row",
        scatter_dimension=0,
        tiled=True,
    )
    local_gram = lax.dot_general(powered, powered, across, precision=lax.Precision.HIGHEST)
    gram_matrix = lax.psum(local_gram, "row")
    cholesky_factor = jnp.linalg.cholesky(gram_matrix)
    ortho_basis = lax.linalg.triangular_solve(
        cholesky_factor, powered, left_side=False, lower=True, transpose_a=True
    )
    own_chosen = jnp.dot(ortho_basis, picker, precision=lax.Precision.HIGHEST)
    projected = add_rows(lax.all_gather(own_chosen.astype(jnp.bfloat16), "row", axis=0, tiled=True))
    left_factor = own_chosen * math.sqrt(weight.shape[1])
    energy = lax.psum(jnp.sum(projected * projected), "row")
    spread = jnp.sqrt(energy / (weight.shape[0] * members * RANK) + 1e-06)
    right_factor = (projected / spread).astype(jnp.bfloat16)
    return (left_factor, right_factor, spread.reshape(1))


class Ring:
    def __init__(self, members):
        chips = members // 2
        order = list(range(0, chips, 2)) + list(range(chips - 1, 0, -2))
        place = {chip: at for at, chip in enumerate(order)}
        self.chips, self.far = chips, chips // 2
        self.pair = [(device, device ^ 1) for device in range(members)]
        self.ahead = []
        for at, chip in enumerate(order):
            self.ahead.append((2 * chip, 2 * order[(at + 1) % chips]))
            self.ahead.append((2 * chip + 1, 2 * order[at - 1] + 1))

        def halves(device, steps, core):
            at = place[device // 2] + (steps if device % 2 == 0 else -steps)
            chip = order[at % chips]
            return [2 * chip + core, 2 * chip + 1 - core]

        self.width, self.table = {}, []
        for device in range(members):
            core, row = device % 2, []

            def put(name, values):
                self.width[name] = (len(row), len(values))
                row.extend(values)

            for k in range(self.far + 1):
                one = k == self.far
                mine, other = halves(device, k, core), halves(device, -k, 1 - core)
                put(("keep", k), mine[:1] if one else mine)
                put(("give", k), [] if k == 0 else other[:1] if one else other)
                mine, other = halves(device, -k, core), halves(device, k, 1 - core)
                put(("use", k), mine if k == 0 else (mine[:1] + other[:1] if one else mine + other))
            put("core", [core])
            self.table.append(row)

    def first(self, weight, name, k):
        half = weight.shape[1] // (2 * self.chips)
        base, turns = self.width[name, k]
        return First(weight.shape[0], half, base, turns, name == "use")

    def calls(self):
        far = self.far
        calls = [[("keep", far), ("give", far), ("give", far - 1)]]
        for k in range(far - 1, 0, -1):
            calls.append([("keep", k), ("give", k - 1) if k > 1 else ("keep", 0)])
        return calls

    def row(self):
        table = jnp.asarray(np.array(self.table, np.int32))
        return lax.dynamic_index_in_dim(table, lax.axis_index("row"), 0, keepdims=False)


class First:
    def __init__(self, rows, half, base, turns, by_rows):
        self.half, self.base, self.turns, self.by_rows = half, base, turns, by_rows
        self.rows = rows
        self.tall = -(-rows // 512) * 128 if by_rows and rows % 128 == 0 else rows
        self.shape = (self.tall, turns * half) if by_rows else (rows, half)

    def copies(self, ids_ref, weight_ref, target_ref, sems):
        if not self.by_rows:
            start = pl.multiple_of(ids_ref[self.base] * self.half, 128)
            source = weight_ref.at[:, pl.ds(start, self.half)]
            return [pltpu.make_async_copy(source, target_ref, sems.at[0])]
        return self.strips(ids_ref, weight_ref, 0, target_ref, sems)

    def strips(self, ids_ref, weight_ref, low, target_ref, sems):
        copies = []
        for turn in range(self.turns):
            start = pl.multiple_of(ids_ref[self.base + turn] * self.half, 128)
            source = weight_ref.at[pl.ds(low, min(self.tall, self.rows - low)), pl.ds(start, self.half)]
            target = target_ref.at[:, pl.ds(turn * self.half, self.half)]
            copies.append(pltpu.make_async_copy(source, target, sems.at[turn]))
        return copies


def in_turn(blocks, ahead, work, prepare=None):
    for block in blocks[: ahead + 1]:
        for copy in block:
            copy.start()
    if prepare is not None:
        prepare()
    for at, block in enumerate(blocks):
        for copy in block:
            copy.wait()
        if at > 0 and at + ahead < len(blocks):
            for copy in blocks[at + ahead]:
                copy.start()
        work(at)


def columns_kernel(half, entries, following, outs, carried, ids_ref, left_ref, weight_ref, *refs):
    refs = list(refs)
    sems, held_ref = refs.pop(), refs.pop()
    turns = len(entries)
    ready_ref = refs.pop(0) if carried else held_ref.at[turns - 1]
    next_ref = refs.pop()
    blocks = [[]] if carried else []
    for turn in range(len(blocks), turns):
        start = pl.multiple_of(ids_ref[entries[turn]] * half, 128)
        source = weight_ref.at[:, pl.ds(start, half)]
        target_ref = held_ref.at[turn - 1] if turn else ready_ref
        blocks.append([pltpu.make_async_copy(source, target_ref, sems.at[turn, 0])])
    blocks.append(following.copies(ids_ref, weight_ref, next_ref, sems.at[turns]))
    places = [(out, at) for out, count in enumerate(outs) for at in range(count)]

    def work(turn):
        if turn == turns:
            return
        block = held_ref[turn - 1] if turn else ready_ref[...]
        part = jnp.dot(left_ref[...], block, preferred_element_type=jnp.float32)
        out, at = places[turn]
        refs[out][:, at * half : (at + 1) * half] = part.astype(refs[out].dtype)

    in_turn(blocks, 2, work)


def column_sums(left, weight, ids, ring, groups, carry, following):
    rows, wide = left.shape[1], left.shape[0]
    half = weight.shape[1] // (2 * ring.chips)
    entries, outs, out_shape = [], [], []
    for name, k in groups:
        base, count = ring.width[name, k]
        entries += range(base, base + count)
        outs.append(count)
        kind = jnp.float32 if name == "keep" else jnp.bfloat16
        out_shape.append(jax.ShapeDtypeStruct((wide, count * half), kind))
    turns = len(entries)
    out_shape.append(jax.ShapeDtypeStruct(following.shape, jnp.bfloat16))
    whole = pl.BlockSpec(memory_space=pltpu.VMEM)
    carried = carry is not None
    return pl.pallas_call(
        functools.partial(columns_kernel, half, entries, following, outs, carried),
        out_shape=out_shape,
        in_specs=[
            pl.BlockSpec(memory_space=pltpu.SMEM),
            whole,
            pl.BlockSpec(memory_space=pl.ANY),
        ]
        + [whole] * carried,
        out_specs=[whole] * len(out_shape),
        scratch_shapes=[
            pltpu.VMEM((turns - carried, rows, half), jnp.bfloat16),
            pltpu.SemaphoreType.DMA((turns + 1, 4)),
        ],
        compiler_params=pltpu.CompilerParams(
            vmem_limit_bytes=2 * (turns - carried) * rows * half + SPARE
        ),
        cost_estimate=pl.CostEstimate(
            flops=2 * wide * rows * turns * half,
            bytes_accessed=2 * rows * turns * half + 2 * rows * wide,
            transcendentals=0,
        ),
    )(ids, left, weight, *([carry] if carried else []))


def invert_kernel(starts, first, *refs):
    refs = list(refs)
    lanes = lax.broadcasted_iota(jnp.int32, (8, 128), 1)
    if starts:
        gram_ref, work_ref, out_ref = refs
        size = work_ref.shape[0]
        total = gram_ref[0]
        for chip in range(1, gram_ref.shape[0]):
            total = total + gram_ref[chip]
        work_ref[...] = jnp.zeros_like(work_ref)
        work_ref[:, :size] = total
    else:
        before_ref, work_ref, out_ref = refs
        size = work_ref.shape[0]
        work_ref[...] = before_ref[...]
    side = first // 16
    tall = size - 8 * first

    rows_at = 8 * first + lax.broadcasted_iota(jnp.int32, (tall, 128), 0)
    inside = lax.broadcasted_iota(jnp.int32, (8, 128), 0)

    def packed(values):
        total = values[0]
        for s in range(1, 8):
            total = jnp.where(inside == s, values[s], total)
        return total

    def panel(p, _):
        raw = [work_ref[pl.ds(8 * p, 8), :128], work_ref[pl.ds(8 * p, 8), 128:]]
        entry, ratio, inverse = {}, {}, []
        for s in range(8):
            at = jnp.full((8, 128), 8 * p + s - 128 * side, jnp.int32)
            column = jnp.take_along_axis(raw[side], at, axis=1)
            for r in range(s + 1):
                entry[r, s] = jnp.broadcast_to(column[r : r + 1], (8, 128))
        for s in range(8):
            inverse.append(1.0 / entry[s, s])
            for t in range(s + 1, 8):
                ratio[t, s] = entry[s, t] * inverse[s]
            for t in range(s + 1, 8):
                for u in range(t, 8):
                    entry[t, u] = entry[t, u] - ratio[t, s] * entry[s, u]
        low = 8 * p - 128 * side
        own = (lanes >= low) & (lanes < low + 8)
        row = []
        for t in range(8):
            halves = [jnp.broadcast_to(part[t : t + 1], (8, 128)) for part in raw]
            unit = jnp.where(lanes == low + t, 1.0, 0.0)
            halves[side] = jnp.where(own, unit, halves[side])
            for s in range(t):
                halves = [half - ratio[t, s] * done for half, done in zip(halves, row[s])]
            row.append(halves)
        scale = lax.rsqrt(packed([entry[s, s] for s in range(8)]))
        inverses = packed(inverse)
        factors = []
        for half in range(2):
            whole = packed([row[s][half] for s in range(8)])
            beyond = lanes + 128 * half >= 8 * p + 8
            strip = jnp.where(beyond, 0.0, whole * scale)
            out_ref[pl.ds(8 * (p - first), 8), 128 * half : min(128 * half + 128, size)] = strip[
                :, : min(128, size - 128 * half)
            ]
            factors.append(jnp.where(beyond, whole * inverses, 0.0).T)
        factor = jnp.concatenate(factors, 0)[8 * first : size]
        spread = lambda x: jnp.tile(x, (tall // 8, 1))
        after = rows_at >= 8 * p + 8
        for half in range(2):
            place = (slice(8 * first, size), slice(128 * half, 128 * half + 128))
            rest = work_ref[place]
            if half == side:
                rest = jnp.where(spread(own) & after, 0.0, rest)
            for s in range(8):
                rest = rest - jnp.broadcast_to(factor[:, s : s + 1], (tall, 128)) * spread(row[s][half])
            work_ref[place] = rest
        return 0

    lax.fori_loop(first, first + out_ref.shape[0] // 8, panel, 0)


def invert_panels(first, size, source):
    tall = min(64, size - 8 * first)
    whole = pl.BlockSpec(memory_space=pltpu.VMEM)
    return pl.pallas_call(
        functools.partial(invert_kernel, first == 0, first),
        out_shape=[
            jax.ShapeDtypeStruct((size, 256), jnp.float32),
            jax.ShapeDtypeStruct((tall, size), jnp.float32),
        ],
        in_specs=[whole],
        out_specs=[whole] * 2,
        input_output_aliases={0: 0} if first else {},
        compiler_params=pltpu.CompilerParams(vmem_limit_bytes=SPARE),
        cost_estimate=pl.CostEstimate(flops=10**9, bytes_accessed=2 * 10**7, transcendentals=0),
    )(source)


def rows_kernel(first, following, pieces, spans, chained, turned, grams, ids_ref, weight_ref, *refs):
    refs = list(refs)
    ready_ref = refs.pop(0)
    piece_refs = [refs.pop(0) for _ in range(pieces)]
    before_ref = refs.pop(0) if chained else None
    if grams and chained:
        refs.pop(0)
    out_ref = refs.pop(0)
    gram_ref = refs.pop(0) if grams else None
    next_ref = refs.pop(0) if following is not None else None
    held_ref, joined_ref, sems = refs
    half, turns = first.half, first.turns
    halves = turns // pieces
    blocks = [[]]
    for number, (low, tall) in enumerate(spans[1:], 1):
        target_ref = held_ref.at[pl.ds(low - first.tall, tall)]
        blocks.append(first.strips(ids_ref, weight_ref, low, target_ref, sems.at[number]))
    if following is not None:
        blocks.append(following.copies(ids_ref, weight_ref, next_ref, sems.at[0]))

    def piece(turn):
        at = turn % halves * half
        return piece_refs[turn // halves][:, at : at + half]

    def prepare():
        for turn in range(turns):
            upright = piece(turn).astype(jnp.float32).T.astype(jnp.bfloat16)
            joined_ref[turn * half : (turn + 1) * half, :] = upright

    def work(number):
        if number == len(spans):
            return
        low, tall = spans[number]
        block_ref, at = (held_ref, low - first.tall) if number else (ready_ref, 0)
        parts = [
            jnp.dot(
                block_ref[at + side * tall // 2 : at + (side + 1) * tall // 2, :],
                joined_ref[...],
                preferred_element_type=jnp.float32,
            )
            for side in range(2)
        ]
        for side, part in enumerate(parts):
            place = (slice(low + side * tall // 2, low + (side + 1) * tall // 2), slice(None))
            parts[side] = before_ref[place] + part if chained else part
            if not turned:
                out_ref[place] = parts[side]
        if turned:
            out_ref[:, low : low + tall] = jnp.concatenate(parts, 0).T.astype(out_ref.dtype)
        if grams and 0 < number <= turns // 2:
            squares = [
                jnp.dot(
                    piece(turn),
                    joined_ref[turn * half : (turn + 1) * half, :],
                    preferred_element_type=jnp.float32,
                )
                for turn in range(2 * number - 2, 2 * number)
            ]
            gram_ref[ids_ref[first.base + 2 * number - 2] // 2] = squares[0] + squares[1]

    in_turn(blocks, 2, work, prepare)


def row_products(weight, pieces, ids, first, before, turned, grams, carry, following):
    rows, wide = weight.shape[0], pieces[0].shape[0]
    turns, half = first.turns, first.half
    chips = weight.shape[1] // (2 * half)
    spans = [(low, min(first.tall, rows - low)) for low in range(0, rows, first.tall)]
    whole = pl.BlockSpec(memory_space=pltpu.VMEM)
    operands = [ids, weight, carry, *pieces]
    in_specs = [pl.BlockSpec(memory_space=pltpu.SMEM), pl.BlockSpec(memory_space=pl.ANY), whole]
    in_specs += [whole] * len(pieces)
    kind = jnp.bfloat16 if turned and grams is None else jnp.float32
    out_shape = [jax.ShapeDtypeStruct((wide, rows) if turned else (rows, wide), kind)]
    aliases = {}
    if before is not None:
        if not turned:
            aliases[len(operands)] = 0
        operands.append(before)
        in_specs.append(whole)
    if grams is not None:
        if before is not None:
            aliases[len(operands)] = 1
            operands.append(grams)
            in_specs.append(whole)
        out_shape.append(jax.ShapeDtypeStruct((chips, wide, wide), jnp.float32))
    if following is not None:
        out_shape.append(jax.ShapeDtypeStruct(following.shape, jnp.bfloat16))
    depth = turns * half
    return pl.pallas_call(
        functools.partial(
            rows_kernel,
            first,
            following,
            len(pieces),
            spans,
            before is not None,
            turned,
            grams is not None,
        ),
        out_shape=out_shape,
        in_specs=in_specs,
        out_specs=[whole] * len(out_shape),
        scratch_shapes=[
            pltpu.VMEM((max(rows - first.tall, 16), depth), jnp.bfloat16),
            pltpu.VMEM((depth, wide), jnp.bfloat16),
            pltpu.SemaphoreType.DMA((len(spans) + 1, 4)),
        ],
        input_output_aliases=aliases,
        compiler_params=pltpu.CompilerParams(
            vmem_limit_bytes=2 * depth * (rows - first.tall + 256) + SPARE
        ),
        cost_estimate=pl.CostEstimate(
            flops=2 * rows * wide * turns * half,
            bytes_accessed=2 * rows * turns * half + 8 * rows * wide,
            transcendentals=0,
        ),
    )(*operands)


def ring_sum(ring, ids, left, weight, half, carry):
    calls = ring.calls()
    got, parts = None, {}
    for number, groups in enumerate(calls):
        k = ring.far - number
        if number:
            left, parts["give", k] = lax.optimization_barrier((left, parts["give", k]))
        if number + 1 < len(calls):
            following = ring.first(weight, *calls[number + 1][0])
        else:
            following = ring.first(weight, "use", 0)
        *outs, carry = column_sums(left, weight, ids, ring, groups, carry, following)
        for (name, at), out in zip(groups, outs):
            parts[name, at] = lax.ppermute(out, "row", ring.pair) if name == "give" else out
        keep, given = parts["keep", k], parts["give", k]
        if got is not None:
            got = got.astype(jnp.float32)
            size = got.shape[1]
            if size < keep.shape[1]:
                keep = jnp.concatenate([keep[:, :size] + got, keep[:, size:]], 1)
            else:
                keep = keep + got
            keep, given = lax.optimization_barrier((keep, given))
        total = (keep + given.astype(jnp.float32)).astype(jnp.bfloat16)
        total, left = lax.optimization_barrier((total, left))
        got = lax.ppermute(total, "row", ring.ahead)
    keep = parts["keep", 0]
    swap = lambda x: jnp.concatenate([x[:, half:], x[:, :half]], 1)
    own = keep + swap(lax.ppermute(keep, "row", ring.pair))
    own, got = lax.optimization_barrier((own, got))
    other = swap(lax.ppermute(got, "row", ring.pair))
    return own + (got.astype(jnp.float32) + other.astype(jnp.float32)), carry


def ring_apply(ring, ids, chunk, weight, half, with_grams, carry, following):
    before, grams = None, () if with_grams else None
    moving = chunk
    for k in range(ring.far + 1):
        if k == 0:
            pieces = [chunk]
        else:
            moving = lax.ppermute(moving if k < ring.far else moving[:, :half], "row", ring.ahead)
            moving, before = lax.optimization_barrier((moving, before))
            pieces = [moving, lax.ppermute(moving, "row", ring.pair)]
        last = k == ring.far
        then = following if last else ring.first(weight, "use", k + 1)
        first = ring.first(weight, "use", k)
        outs = list(
            row_products(
                weight, pieces, ids, first, before, last, grams, carry, then
            )
        )
        carry = outs.pop() if then is not None else None
        before = outs.pop(0)
        grams = outs.pop() if outs else None
    return before, grams, carry


def sum_beside_inverse(value, ring, ids, grams):
    size = value.shape[0]
    rows = size // 2
    core = ring.width["core"][0]
    first = ids[core : core + 1, None] == 0
    at, to = (lax.broadcasted_iota(jnp.int32, (rows, rows), axis) for axis in range(2))
    top, corner, bottom = value[:rows, :rows], value[:rows, rows:], value[rows:, rows:]
    diagonal = jnp.sum(jnp.where(at == to, bottom, 0.0), axis=0, keepdims=True)
    low = jnp.concatenate([corner, jnp.zeros_like(diagonal)], 0)
    high = jnp.concatenate([jnp.where(at <= to, top, bottom), diagonal], 0)
    part = jnp.where(first, low, high)
    part = part + lax.ppermute(jnp.where(first, high, low), "row", ring.pair)
    hops = [
        [(device, device ^ (2 << bit)) for device in range(2 * ring.chips)]
        for bit in reversed(range(ring.chips.bit_length() - 1))
    ]
    panels = list(range(0, size // 8, 8))
    work, strips = grams, []
    for turn in range(max(len(hops), len(panels))):
        if turn < len(hops):
            got = lax.ppermute(part, "row", hops[turn])
        if turn < len(panels):
            work, strip = invert_panels(panels[turn], size, work)
            strips.append(strip)
        if turn < len(hops):
            got, work = lax.optimization_barrier((got, work))
            part = part + got
    other = lax.ppermute(part, "row", ring.pair)
    low, high = jnp.where(first, part, other), jnp.where(first, other, part)
    mixed, diagonal = high[:rows], high[rows:]
    top = jnp.where(at < to, 2.0 * mixed, jnp.where(at == to, mixed, 0.0))
    bottom = jnp.where(at > to, 2.0 * mixed, jnp.where(at == to, diagonal, 0.0))
    top = jnp.concatenate([top, 2.0 * low[:rows]], 1)
    bottom = jnp.concatenate([jnp.zeros_like(bottom), bottom], 1)
    return jnp.concatenate([top, bottom], 0), strips


def finish_kernel(strips, count, scale, *refs):
    strip_refs = refs[:strips]
    pick_ref, square_ref, own_ref, image_ref = refs[strips : strips + 4]
    left_ref, right_ref, spread_ref, inverse_ref = refs[strips + 4 :]

    def exact(a, b):
        return jnp.dot(a, b, precision=lax.Precision.HIGHEST, preferred_element_type=jnp.float32)

    def halves(value):
        high = value.astype(jnp.bfloat16)
        return high, (value - high.astype(jnp.float32)).astype(jnp.bfloat16)

    low = 0
    for strip_ref in strip_refs:
        inverse_ref[low : low + strip_ref.shape[0], :] = strip_ref[...]
        low += strip_ref.shape[0]
    change = exact(pick_ref[...], inverse_ref[...])
    energy = jnp.sum(change * exact(change, square_ref[...]), axis=1, keepdims=True)
    spread = jnp.sqrt(jnp.sum(energy, axis=0, keepdims=True) / count + 1e-06)
    spread_ref[...] = spread
    left_ref[...] = exact(change, own_ref[...]) * scale
    high, low = halves(change / spread)
    rows = image_ref.shape[1]
    for at in range(0, rows, 512):
        place = (slice(None), slice(at, min(at + 512, rows)))
        image_high, image_low = halves(image_ref[place])
        total = jnp.dot(high, image_high, preferred_element_type=jnp.float32)
        total += jnp.dot(high, image_low, preferred_element_type=jnp.float32)
        total += jnp.dot(low, image_high, preferred_element_type=jnp.float32)
        right_ref[place] = total.astype(jnp.bfloat16)


def finish(strips, pick, square, own, image, count, scale):
    kept, size = pick.shape
    whole = pl.BlockSpec(memory_space=pltpu.VMEM)
    operands = [*strips, pick, square, own, image]
    return pl.pallas_call(
        functools.partial(finish_kernel, len(strips), count, scale),
        out_shape=[
            jax.ShapeDtypeStruct((kept, own.shape[1]), jnp.float32),
            jax.ShapeDtypeStruct((kept, image.shape[1]), jnp.bfloat16),
            jax.ShapeDtypeStruct((1, 1), jnp.float32),
        ],
        in_specs=[whole] * len(operands),
        out_specs=[whole] * 3,
        scratch_shapes=[pltpu.VMEM((size, size), jnp.float32)],
        compiler_params=pltpu.CompilerParams(vmem_limit_bytes=2 * SPARE),
    )(*operands)


def ring_body(ring, weight, test_matrix, rank_mask):
    rows, features = weight.shape
    half = features // (2 * ring.chips)
    ids = ring.row()
    pick = selector(rank_mask, RANK).T
    sketch, carry = ring_sum(ring, ids, test_matrix.T, weight, half, None)
    sketch = sketch.astype(jnp.bfloat16)
    again = ring.first(weight, "keep", ring.far)
    mixed, _, carry = ring_apply(ring, ids, sketch, weight, half, False, carry, again)
    powered, carry = ring_sum(ring, ids, mixed, weight, half, carry)
    powered_b = powered.astype(jnp.bfloat16)
    image, grams, _ = ring_apply(ring, ids, powered_b, weight, half, True, carry, None)
    image_b = image.astype(jnp.bfloat16)
    square = lax.dot_general(
        image_b, image_b, (((1,), (1,)), ((), ())), preferred_element_type=jnp.float32
    )
    square, strips = sum_beside_inverse(square, ring, ids, grams)
    own = powered[:, :half]
    count = rows * 2 * ring.chips * RANK
    left_factor, right_factor, spread = finish(
        strips, pick, square, own, image, count, math.sqrt(features)
    )
    return (left_factor.T, right_factor.T, spread.reshape(1))


def body(weight, test_matrix, rank_mask):
    members = lax.axis_size("row")
    chips = members // 2
    paired = members % 2 == 0 and chips > 2 and chips & (chips - 1) == 0
    if not paired or weight.shape[1] % (members * 128):
        return plain_body(weight, test_matrix, rank_mask)
    return ring_body(Ring(members), weight, test_matrix, rank_mask)


def solution(mesh):
    in_specs = (P(("groups", "row"), None), P("row", None), P("groups"))
    out_specs = (P(("groups", "row"), None), P(("groups", "row"), None), P("groups"))
    return jax.shard_map(body, mesh=mesh, in_specs=in_specs, out_specs=out_specs, check_vma=False)
```

```python
import functools
import math

import jax
import jax.numpy as jnp
import numpy as np
from jax import lax
from jax.experimental import pallas as pl
from jax.experimental.pallas import tpu as pltpu
from jax.sharding import PartitionSpec as P

RANK = 224
PANEL = 16
SPARE = 4 * 1024 * 1024


def selector(rank_mask, kept):
    at = lax.iota(jnp.int32, rank_mask.shape[0])
    positions = jnp.sum(jnp.where(at[:, None] <= at[None, :], rank_mask[:, None], 0), axis=0) - 1
    targets = lax.iota(jnp.int32, kept)
    matches = (rank_mask[:, None] == 1) & (positions[:, None] == targets[None, :])
    return matches.astype(jnp.float32)


def plain_body(weight, test_matrix, rank_mask):
    across = (((0,), (0,)), ((), ()))
    members = lax.axis_size("row")
    picker = selector(rank_mask, RANK)
    sketch_part = lax.psum_scatter(
        lax.dot_general(weight, test_matrix, across, preferred_element_type=jnp.float32),
        "row",
        scatter_dimension=0,
        tiled=True,
    ).astype(jnp.bfloat16)

    def add_rows(piece_rows):
        return jnp.dot(weight, piece_rows, preferred_element_type=jnp.float32)

    mixed = add_rows(lax.all_gather(sketch_part, "row", axis=0, tiled=True)).astype(jnp.bfloat16)
    powered = lax.psum_scatter(
        lax.dot_general(weight, mixed, across, preferred_element_type=jnp.float32),
        "row",
        scatter_dimension=0,
        tiled=True,
    )
    local_gram = lax.dot_general(powered, powered, across, precision=lax.Precision.HIGHEST)
    gram_matrix = lax.psum(local_gram, "row")
    cholesky_factor = jnp.linalg.cholesky(gram_matrix)
    ortho_basis = lax.linalg.triangular_solve(
        cholesky_factor, powered, left_side=False, lower=True, transpose_a=True
    )
    own_chosen = jnp.dot(ortho_basis, picker, precision=lax.Precision.HIGHEST)
    projected = add_rows(lax.all_gather(own_chosen.astype(jnp.bfloat16), "row", axis=0, tiled=True))
    left_factor = own_chosen * math.sqrt(weight.shape[1])
    energy = lax.psum(jnp.sum(projected * projected), "row")
    spread = jnp.sqrt(energy / (weight.shape[0] * members * RANK) + 1e-06)
    right_factor = (projected / spread).astype(jnp.bfloat16)
    return (left_factor, right_factor, spread.reshape(1))


class Ring:
    def __init__(self, members):
        chips = members // 2
        order = list(range(0, chips, 2)) + list(range(chips - 1, 0, -2))
        place = {chip: at for at, chip in enumerate(order)}
        self.chips, self.far = chips, chips // 2
        self.pair = [(device, device ^ 1) for device in range(members)]
        self.ahead = []
        for at, chip in enumerate(order):
            self.ahead.append((2 * chip, 2 * order[(at + 1) % chips]))
            self.ahead.append((2 * chip + 1, 2 * order[at - 1] + 1))

        def halves(device, steps, core):
            at = place[device // 2] + (steps if device % 2 == 0 else -steps)
            chip = order[at % chips]
            return [2 * chip + core, 2 * chip + 1 - core]

        self.width, self.table = {}, []
        for device in range(members):
            core, row = device % 2, []

            def put(name, values):
                self.width[name] = (len(row), len(values))
                row.extend(values)

            for k in range(self.far + 1):
                one = k == self.far
                mine, other = halves(device, k, core), halves(device, -k, 1 - core)
                put(("keep", k), mine[:1] if one else mine)
                put(("give", k), [] if k == 0 else other[:1] if one else other)
                mine, other = halves(device, -k, core), halves(device, k, 1 - core)
                put(("use", k), mine if k == 0 else (mine[:1] + other[:1] if one else mine + other))
            put("core", [core])
            self.table.append(row)

    def first(self, weight, name, k):
        half = weight.shape[1] // (2 * self.chips)
        base, turns = self.width[name, k]
        return First(weight.shape[0], half, base, turns, name == "use")

    def calls(self):
        far = self.far
        calls = [[("keep", far), ("give", far), ("give", far - 1)]]
        for k in range(far - 1, 0, -1):
            calls.append([("keep", k), ("give", k - 1) if k > 1 else ("keep", 0)])
        return calls

    def row(self):
        table = jnp.asarray(np.array(self.table, np.int32))
        return lax.dynamic_index_in_dim(table, lax.axis_index("row"), 0, keepdims=False)


class First:
    def __init__(self, rows, half, base, turns, by_rows):
        self.half, self.base, self.turns, self.by_rows = half, base, turns, by_rows
        self.rows = rows
        cuts = 2 if turns == 2 else 4
        self.tall = -(-rows // (128 * cuts)) * 128 if by_rows and rows % 128 == 0 else rows
        self.shape = (self.tall, turns * half) if by_rows else (rows, half)

    def copies(self, ids_ref, weight_ref, target_ref, sems):
        if not self.by_rows:
            start = pl.multiple_of(ids_ref[self.base] * self.half, 128)
            source = weight_ref.at[:, pl.ds(start, self.half)]
            return [pltpu.make_async_copy(source, target_ref, sems.at[0])]
        return self.strips(ids_ref, weight_ref, 0, target_ref, sems)

    def strips(self, ids_ref, weight_ref, low, target_ref, sems):
        copies = []
        for turn in range(self.turns):
            start = pl.multiple_of(ids_ref[self.base + turn] * self.half, 128)
            source = weight_ref.at[pl.ds(low, min(self.tall, self.rows - low)), pl.ds(start, self.half)]
            target = target_ref.at[:, pl.ds(turn * self.half, self.half)]
            copies.append(pltpu.make_async_copy(source, target, sems.at[turn]))
        return copies


def in_turn(blocks, ahead, work, prepare=None):
    for block in blocks[: ahead + 1]:
        for copy in block:
            copy.start()
    if prepare is not None:
        prepare()
    for at, block in enumerate(blocks):
        for copy in block:
            copy.wait()
        if at > 0 and at + ahead < len(blocks):
            for copy in blocks[at + ahead]:
                copy.start()
        work(at)


def columns_kernel(half, entries, following, outs, carried, ids_ref, left_ref, weight_ref, *refs):
    refs = list(refs)
    sems, held_ref = refs.pop(), refs.pop()
    turns = len(entries)
    ready_ref = refs.pop(0) if carried else held_ref.at[turns - 1]
    next_ref = refs.pop()
    blocks = [[]] if carried else []
    for turn in range(len(blocks), turns):
        start = pl.multiple_of(ids_ref[entries[turn]] * half, 128)
        source = weight_ref.at[:, pl.ds(start, half)]
        target_ref = held_ref.at[turn - 1] if turn else ready_ref
        blocks.append([pltpu.make_async_copy(source, target_ref, sems.at[turn, 0])])
    blocks.append(following.copies(ids_ref, weight_ref, next_ref, sems.at[turns]))
    places = [(out, at) for out, count in enumerate(outs) for at in range(count)]

    def work(turn):
        if turn == turns:
            return
        block = held_ref[turn - 1] if turn else ready_ref[...]
        part = jnp.dot(left_ref[...], block, preferred_element_type=jnp.float32)
        out, at = places[turn]
        refs[out][:, at * half : (at + 1) * half] = part.astype(refs[out].dtype)

    in_turn(blocks, 2, work)


def column_sums(left, weight, ids, ring, groups, carry, following):
    rows, wide = left.shape[1], left.shape[0]
    half = weight.shape[1] // (2 * ring.chips)
    entries, outs, out_shape = [], [], []
    for name, k in groups:
        base, count = ring.width[name, k]
        entries += range(base, base + count)
        outs.append(count)
        kind = jnp.float32 if name == "keep" else jnp.bfloat16
        out_shape.append(jax.ShapeDtypeStruct((wide, count * half), kind))
    turns = len(entries)
    out_shape.append(jax.ShapeDtypeStruct(following.shape, jnp.bfloat16))
    whole = pl.BlockSpec(memory_space=pltpu.VMEM)
    carried = carry is not None
    return pl.pallas_call(
        functools.partial(columns_kernel, half, entries, following, outs, carried),
        out_shape=out_shape,
        in_specs=[
            pl.BlockSpec(memory_space=pltpu.SMEM),
            whole,
            pl.BlockSpec(memory_space=pl.ANY),
        ]
        + [whole] * carried,
        out_specs=[whole] * len(out_shape),
        scratch_shapes=[
            pltpu.VMEM((turns - carried, rows, half), jnp.bfloat16),
            pltpu.SemaphoreType.DMA((turns + 1, 4)),
        ],
        compiler_params=pltpu.CompilerParams(
            vmem_limit_bytes=2 * (turns - carried) * rows * half + SPARE
        ),
        cost_estimate=pl.CostEstimate(
            flops=2 * wide * rows * turns * half,
            bytes_accessed=2 * rows * turns * half + 2 * rows * wide,
            transcendentals=0,
        ),
    )(ids, left, weight, *([carry] if carried else []))


def invert_kernel(starts, first, *refs):
    refs = list(refs)
    lanes = lax.broadcasted_iota(jnp.int32, (8, 128), 1)
    if starts:
        gram_ref, work_ref, out_ref = refs
        size = work_ref.shape[0]
        total = gram_ref[0]
        for chip in range(1, gram_ref.shape[0]):
            total = total + gram_ref[chip]
        work_ref[...] = jnp.zeros_like(work_ref)
        work_ref[:, :size] = total
    else:
        before_ref, work_ref, out_ref = refs
        size = work_ref.shape[0]
        work_ref[...] = before_ref[...]
    side = first * PANEL // 128
    start = first * PANEL
    tall = size - start
    rows_at = start + lax.broadcasted_iota(jnp.int32, (tall, 128), 0)
    inside = lax.broadcasted_iota(jnp.int32, (PANEL, 128), 0)

    def packed(values):
        total = jnp.broadcast_to(values[0][:1], (PANEL, 128))
        for s in range(1, PANEL):
            total = jnp.where(inside == s, jnp.broadcast_to(values[s][:1], (PANEL, 128)), total)
        return total

    def panel(p, _):
        here = pl.ds(pl.multiple_of(PANEL * p, PANEL), PANEL)
        raw = [work_ref[here, :128], work_ref[here, 128:]]
        low = PANEL * p - 128 * side
        entry, ratio, inverse = {}, {}, []
        for s in range(PANEL):
            at = jnp.full((PANEL, 128), low + s, jnp.int32)
            column = jnp.take_along_axis(raw[side], at, axis=1)
            for r in range(s + 1):
                entry[r, s] = jnp.broadcast_to(column[r : r + 1], (8, 128))
        for s in range(PANEL):
            inverse.append(1.0 / entry[s, s])
            for t in range(s + 1, PANEL):
                ratio[t, s] = entry[s, t] * inverse[s]
            for t in range(s + 1, PANEL):
                for u in range(t, PANEL):
                    entry[t, u] = entry[t, u] - ratio[t, s] * entry[s, u]
        own = (lanes >= low) & (lanes < low + PANEL)
        row = []
        for t in range(PANEL):
            halves = [jnp.broadcast_to(part[t : t + 1], (8, 128)) for part in raw]
            unit = jnp.where(lanes == low + t, 1.0, 0.0)
            halves[side] = jnp.where(own, unit, halves[side])
            for s in range(t):
                halves = [half - ratio[t, s] * done for half, done in zip(halves, row[s])]
            row.append(halves)
        scale = lax.rsqrt(packed([entry[s, s] for s in range(PANEL)]))
        inverses = packed(inverse)
        factors = []
        for half in range(2):
            whole = packed([row[s][half] for s in range(PANEL)])
            beyond = lanes[:1] + 128 * half >= PANEL * p + PANEL
            strip = jnp.where(beyond, 0.0, whole * scale)
            place = pl.ds(pl.multiple_of(PANEL * (p - first), PANEL), PANEL)
            out_ref[place, 128 * half : min(128 * half + 128, size)] = strip[
                :, : min(128, size - 128 * half)
            ]
            factors.append(jnp.where(beyond, whole * inverses, 0.0).T)
        factor = jnp.concatenate(factors, 0)[start:size]
        spread = lambda x: jnp.tile(x, (tall // 8, 1))
        after = rows_at >= PANEL * p + PANEL
        for half in range(2):
            place = (slice(start, size), slice(128 * half, 128 * half + 128))
            rest = work_ref[place]
            if half == side:
                rest = jnp.where(spread(own) & after, 0.0, rest)
            for s in range(PANEL):
                rest = rest - jnp.broadcast_to(factor[:, s : s + 1], (tall, 128)) * spread(row[s][half])
            work_ref[place] = rest
        return 0

    lax.fori_loop(first, first + out_ref.shape[0] // PANEL, panel, 0)


def invert_panels(first, size, source):
    tall = min(4 * PANEL, size - PANEL * first)
    whole = pl.BlockSpec(memory_space=pltpu.VMEM)
    return pl.pallas_call(
        functools.partial(invert_kernel, first == 0, first),
        out_shape=[
            jax.ShapeDtypeStruct((size, 256), jnp.float32),
            jax.ShapeDtypeStruct((tall, size), jnp.float32),
        ],
        in_specs=[whole],
        out_specs=[whole] * 2,
        input_output_aliases={0: 0} if first else {},
        compiler_params=pltpu.CompilerParams(vmem_limit_bytes=SPARE),
        cost_estimate=pl.CostEstimate(flops=10**9, bytes_accessed=2 * 10**7, transcendentals=0),
    )(source)


def rows_kernel(first, following, pieces, spans, chained, turned, grams, ids_ref, weight_ref, *refs):
    refs = list(refs)
    ready_ref = refs.pop(0)
    piece_refs = [refs.pop(0) for _ in range(pieces)]
    before_ref = refs.pop(0) if chained else None
    if grams and chained:
        refs.pop(0)
    out_ref = refs.pop(0)
    gram_ref = refs.pop(0) if grams else None
    next_ref = refs.pop(0) if following is not None else None
    held_ref, joined_ref, sems = refs
    half, turns = first.half, first.turns
    halves = turns // pieces
    blocks = [[]]
    for number, (low, tall) in enumerate(spans[1:], 1):
        target_ref = held_ref.at[pl.ds(low - first.tall, tall)]
        blocks.append(first.strips(ids_ref, weight_ref, low, target_ref, sems.at[number]))
    if following is not None:
        blocks.append(following.copies(ids_ref, weight_ref, next_ref, sems.at[0]))

    def piece(turn):
        at = turn % halves * half
        return piece_refs[turn // halves][:, at : at + half]

    def prepare():
        for turn in range(turns):
            upright = piece(turn).astype(jnp.float32).T.astype(jnp.bfloat16)
            joined_ref[turn * half : (turn + 1) * half, :] = upright

    def work(number):
        if number == len(spans):
            return
        low, tall = spans[number]
        block_ref, at = (held_ref, low - first.tall) if number else (ready_ref, 0)
        parts = [
            jnp.dot(
                block_ref[at + side * tall // 2 : at + (side + 1) * tall // 2, :],
                joined_ref[...],
                preferred_element_type=jnp.float32,
            )
            for side in range(2)
        ]
        for side, part in enumerate(parts):
            place = (slice(low + side * tall // 2, low + (side + 1) * tall // 2), slice(None))
            parts[side] = before_ref[place] + part if chained else part
            if not turned:
                out_ref[place] = parts[side]
        if turned:
            out_ref[:, low : low + tall] = jnp.concatenate(parts, 0).T.astype(out_ref.dtype)
        if grams and 0 < number <= turns // 2:
            squares = [
                jnp.dot(
                    piece(turn),
                    joined_ref[turn * half : (turn + 1) * half, :],
                    preferred_element_type=jnp.float32,
                )
                for turn in range(2 * number - 2, 2 * number)
            ]
            gram_ref[ids_ref[first.base + 2 * number - 2] // 2] = squares[0] + squares[1]

    in_turn(blocks, 2, work, prepare)


def row_products(weight, pieces, ids, first, before, turned, grams, carry, following):
    rows, wide = weight.shape[0], pieces[0].shape[0]
    turns, half = first.turns, first.half
    chips = weight.shape[1] // (2 * half)
    spans = [(low, min(first.tall, rows - low)) for low in range(0, rows, first.tall)]
    whole = pl.BlockSpec(memory_space=pltpu.VMEM)
    operands = [ids, weight, carry, *pieces]
    in_specs = [pl.BlockSpec(memory_space=pltpu.SMEM), pl.BlockSpec(memory_space=pl.ANY), whole]
    in_specs += [whole] * len(pieces)
    kind = jnp.bfloat16 if turned and grams is None else jnp.float32
    out_shape = [jax.ShapeDtypeStruct((wide, rows) if turned else (rows, wide), kind)]
    aliases = {}
    if before is not None:
        if not turned:
            aliases[len(operands)] = 0
        operands.append(before)
        in_specs.append(whole)
    if grams is not None:
        if before is not None:
            aliases[len(operands)] = 1
            operands.append(grams)
            in_specs.append(whole)
        out_shape.append(jax.ShapeDtypeStruct((chips, wide, wide), jnp.float32))
    if following is not None:
        out_shape.append(jax.ShapeDtypeStruct(following.shape, jnp.bfloat16))
    depth = turns * half
    return pl.pallas_call(
        functools.partial(
            rows_kernel,
            first,
            following,
            len(pieces),
            spans,
            before is not None,
            turned,
            grams is not None,
        ),
        out_shape=out_shape,
        in_specs=in_specs,
        out_specs=[whole] * len(out_shape),
        scratch_shapes=[
            pltpu.VMEM((max(rows - first.tall, 16), depth), jnp.bfloat16),
            pltpu.VMEM((depth, wide), jnp.bfloat16),
            pltpu.SemaphoreType.DMA((len(spans) + 1, 4)),
        ],
        input_output_aliases=aliases,
        compiler_params=pltpu.CompilerParams(
            vmem_limit_bytes=2 * depth * (rows - first.tall + 256) + SPARE
        ),
        cost_estimate=pl.CostEstimate(
            flops=2 * rows * wide * turns * half,
            bytes_accessed=2 * rows * turns * half + 8 * rows * wide,
            transcendentals=0,
        ),
    )(*operands)


def ring_sum(ring, ids, left, weight, half, carry):
    calls = ring.calls()
    got, parts = None, {}
    for number, groups in enumerate(calls):
        k = ring.far - number
        if number:
            left, parts["give", k] = lax.optimization_barrier((left, parts["give", k]))
        if number + 1 < len(calls):
            following = ring.first(weight, *calls[number + 1][0])
        else:
            following = ring.first(weight, "use", 0)
        *outs, carry = column_sums(left, weight, ids, ring, groups, carry, following)
        for (name, at), out in zip(groups, outs):
            parts[name, at] = lax.ppermute(out, "row", ring.pair) if name == "give" else out
        keep, given = parts["keep", k], parts["give", k]
        if got is not None:
            got = got.astype(jnp.float32)
            size = got.shape[1]
            if size < keep.shape[1]:
                keep = jnp.concatenate([keep[:, :size] + got, keep[:, size:]], 1)
            else:
                keep = keep + got
            keep, given = lax.optimization_barrier((keep, given))
        total = (keep + given.astype(jnp.float32)).astype(jnp.bfloat16)
        total, left = lax.optimization_barrier((total, left))
        got = lax.ppermute(total, "row", ring.ahead)
    keep = parts["keep", 0]
    swap = lambda x: jnp.concatenate([x[:, half:], x[:, :half]], 1)
    own = keep + swap(lax.ppermute(keep, "row", ring.pair))
    own, got = lax.optimization_barrier((own, got))
    other = swap(lax.ppermute(got, "row", ring.pair))
    return own + (got.astype(jnp.float32) + other.astype(jnp.float32)), carry


def ring_apply(ring, ids, chunk, weight, half, with_grams, carry, following):
    before, grams = None, () if with_grams else None
    moving = chunk
    for k in range(ring.far + 1):
        if k == 0:
            pieces = [chunk]
        else:
            moving = lax.ppermute(moving if k < ring.far else moving[:, :half], "row", ring.ahead)
            moving, before = lax.optimization_barrier((moving, before))
            pieces = [moving, lax.ppermute(moving, "row", ring.pair)]
        last = k == ring.far
        then = following if last else ring.first(weight, "use", k + 1)
        first = ring.first(weight, "use", k)
        outs = list(
            row_products(
                weight, pieces, ids, first, before, last, grams, carry, then
            )
        )
        carry = outs.pop() if then is not None else None
        before = outs.pop(0)
        grams = outs.pop() if outs else None
    return before, grams, carry


def sum_beside_inverse(value, ring, ids, grams):
    size = value.shape[0]
    rows = size // 2
    core = ring.width["core"][0]
    first = ids[core : core + 1, None] == 0
    at, to = (lax.broadcasted_iota(jnp.int32, (rows, rows), axis) for axis in range(2))
    top, corner, bottom = value[:rows, :rows], value[:rows, rows:], value[rows:, rows:]
    diagonal = jnp.sum(jnp.where(at == to, bottom, 0.0), axis=0, keepdims=True)
    low = jnp.concatenate([corner, jnp.zeros_like(diagonal)], 0)
    high = jnp.concatenate([jnp.where(at <= to, top, bottom), diagonal], 0)
    part = jnp.where(first, low, high)
    part = part + lax.ppermute(jnp.where(first, high, low), "row", ring.pair)
    hops = [
        [(device, device ^ (2 << bit)) for device in range(2 * ring.chips)]
        for bit in reversed(range(ring.chips.bit_length() - 1))
    ]
    panels = list(range(0, size // PANEL, 4))
    work, strips = grams, []
    for turn in range(max(len(hops), len(panels))):
        if turn < len(hops):
            got = lax.ppermute(part, "row", hops[turn])
        if turn < len(panels):
            work, strip = invert_panels(panels[turn], size, work)
            strips.append(strip)
        if turn < len(hops):
            got, work = lax.optimization_barrier((got, work))
            part = part + got
    other = lax.ppermute(part, "row", ring.pair)
    low, high = jnp.where(first, part, other), jnp.where(first, other, part)
    mixed, diagonal = high[:rows], high[rows:]
    top = jnp.where(at < to, 2.0 * mixed, jnp.where(at == to, mixed, 0.0))
    bottom = jnp.where(at > to, 2.0 * mixed, jnp.where(at == to, diagonal, 0.0))
    top = jnp.concatenate([top, 2.0 * low[:rows]], 1)
    bottom = jnp.concatenate([jnp.zeros_like(bottom), bottom], 1)
    return jnp.concatenate([top, bottom], 0), strips


def finish_kernel(strips, count, scale, *refs):
    strip_refs = refs[:strips]
    pick_ref, square_ref, own_ref, image_ref = refs[strips : strips + 4]
    left_ref, right_ref, spread_ref, inverse_ref = refs[strips + 4 :]

    def exact(a, b):
        return jnp.dot(a, b, precision=lax.Precision.HIGHEST, preferred_element_type=jnp.float32)

    def halves(value):
        high = value.astype(jnp.bfloat16)
        return high, (value - high.astype(jnp.float32)).astype(jnp.bfloat16)

    low = 0
    for strip_ref in strip_refs:
        inverse_ref[low : low + strip_ref.shape[0], :] = strip_ref[...]
        low += strip_ref.shape[0]
    change = exact(pick_ref[...], inverse_ref[...])
    energy = jnp.sum(change * exact(change, square_ref[...]), axis=1, keepdims=True)
    spread = jnp.sqrt(jnp.sum(energy, axis=0, keepdims=True) / count + 1e-06)
    spread_ref[...] = spread
    left_ref[...] = exact(change, own_ref[...]) * scale
    high, low = halves(change / spread)
    rows = image_ref.shape[1]
    for at in range(0, rows, 512):
        place = (slice(None), slice(at, min(at + 512, rows)))
        image_high, image_low = halves(image_ref[place])
        total = jnp.dot(high, image_high, preferred_element_type=jnp.float32)
        total += jnp.dot(high, image_low, preferred_element_type=jnp.float32)
        total += jnp.dot(low, image_high, preferred_element_type=jnp.float32)
        right_ref[place] = total.astype(jnp.bfloat16)


def finish(strips, pick, square, own, image, count, scale):
    kept, size = pick.shape
    whole = pl.BlockSpec(memory_space=pltpu.VMEM)
    operands = [*strips, pick, square, own, image]
    return pl.pallas_call(
        functools.partial(finish_kernel, len(strips), count, scale),
        out_shape=[
            jax.ShapeDtypeStruct((kept, own.shape[1]), jnp.float32),
            jax.ShapeDtypeStruct((kept, image.shape[1]), jnp.bfloat16),
            jax.ShapeDtypeStruct((1, 1), jnp.float32),
        ],
        in_specs=[whole] * len(operands),
        out_specs=[whole] * 3,
        scratch_shapes=[pltpu.VMEM((size, size), jnp.float32)],
        compiler_params=pltpu.CompilerParams(vmem_limit_bytes=2 * SPARE),
    )(*operands)


def ring_body(ring, weight, test_matrix, rank_mask):
    rows, features = weight.shape
    half = features // (2 * ring.chips)
    ids = ring.row()
    pick = selector(rank_mask, RANK).T
    sketch, carry = ring_sum(ring, ids, test_matrix.T, weight, half, None)
    sketch = sketch.astype(jnp.bfloat16)
    again = ring.first(weight, "keep", ring.far)
    mixed, _, carry = ring_apply(ring, ids, sketch, weight, half, False, carry, again)
    powered, carry = ring_sum(ring, ids, mixed, weight, half, carry)
    powered_b = powered.astype(jnp.bfloat16)
    image, grams, _ = ring_apply(ring, ids, powered_b, weight, half, True, carry, None)
    image_b = image.astype(jnp.bfloat16)
    square = lax.dot_general(
        image_b, image_b, (((1,), (1,)), ((), ())), preferred_element_type=jnp.float32
    )
    square, strips = sum_beside_inverse(square, ring, ids, grams)
    own = powered[:, :half]
    count = rows * 2 * ring.chips * RANK
    left_factor, right_factor, spread = finish(
        strips, pick, square, own, image, count, math.sqrt(features)
    )
    return (left_factor.T, right_factor.T, spread.reshape(1))


def body(weight, test_matrix, rank_mask):
    members = lax.axis_size("row")
    chips = members // 2
    paired = members % 2 == 0 and chips > 2 and chips & (chips - 1) == 0
    if not paired or weight.shape[1] % (members * 128):
        return plain_body(weight, test_matrix, rank_mask)
    return ring_body(Ring(members), weight, test_matrix, rank_mask)


def solution(mesh):
    in_specs = (P(("groups", "row"), None), P("row", None), P("groups"))
    out_specs = (P(("groups", "row"), None), P(("groups", "row"), None), P("groups"))
    return jax.shard_map(body, mesh=mesh, in_specs=in_specs, out_specs=out_specs, check_vma=False)
```

```python
import functools
import math

import jax
import jax.numpy as jnp
import numpy as np
from jax import lax
from jax.experimental import pallas as pl
from jax.experimental.pallas import tpu as pltpu
from jax.sharding import PartitionSpec as P

RANK = 224
PANEL = 16
SPARE = 4 * 1024 * 1024


def selector(rank_mask, kept):
    at = lax.iota(jnp.int32, rank_mask.shape[0])
    positions = jnp.sum(jnp.where(at[:, None] <= at[None, :], rank_mask[:, None], 0), axis=0) - 1
    targets = lax.iota(jnp.int32, kept)
    matches = (rank_mask[:, None] == 1) & (positions[:, None] == targets[None, :])
    return matches.astype(jnp.float32)


def plain_body(weight, test_matrix, rank_mask):
    across = (((0,), (0,)), ((), ()))
    members = lax.axis_size("row")
    picker = selector(rank_mask, RANK)
    sketch_part = lax.psum_scatter(
        lax.dot_general(weight, test_matrix, across, preferred_element_type=jnp.float32),
        "row",
        scatter_dimension=0,
        tiled=True,
    ).astype(jnp.bfloat16)

    def add_rows(piece_rows):
        return jnp.dot(weight, piece_rows, preferred_element_type=jnp.float32)

    mixed = add_rows(lax.all_gather(sketch_part, "row", axis=0, tiled=True)).astype(jnp.bfloat16)
    powered = lax.psum_scatter(
        lax.dot_general(weight, mixed, across, preferred_element_type=jnp.float32),
        "row",
        scatter_dimension=0,
        tiled=True,
    )
    local_gram = lax.dot_general(powered, powered, across, precision=lax.Precision.HIGHEST)
    gram_matrix = lax.psum(local_gram, "row")
    cholesky_factor = jnp.linalg.cholesky(gram_matrix)
    ortho_basis = lax.linalg.triangular_solve(
        cholesky_factor, powered, left_side=False, lower=True, transpose_a=True
    )
    own_chosen = jnp.dot(ortho_basis, picker, precision=lax.Precision.HIGHEST)
    projected = add_rows(lax.all_gather(own_chosen.astype(jnp.bfloat16), "row", axis=0, tiled=True))
    left_factor = own_chosen * math.sqrt(weight.shape[1])
    energy = lax.psum(jnp.sum(projected * projected), "row")
    spread = jnp.sqrt(energy / (weight.shape[0] * members * RANK) + 1e-06)
    right_factor = (projected / spread).astype(jnp.bfloat16)
    return (left_factor, right_factor, spread.reshape(1))


class Ring:
    def __init__(self, members):
        chips = members // 2
        order = list(range(0, chips, 2)) + list(range(chips - 1, 0, -2))
        place = {chip: at for at, chip in enumerate(order)}
        self.chips, self.far = chips, chips // 2
        self.pair = [(device, device ^ 1) for device in range(members)]
        self.ahead = []
        for at, chip in enumerate(order):
            self.ahead.append((2 * chip, 2 * order[(at + 1) % chips]))
            self.ahead.append((2 * chip + 1, 2 * order[at - 1] + 1))

        def halves(device, steps, core):
            at = place[device // 2] + (steps if device % 2 == 0 else -steps)
            chip = order[at % chips]
            return [2 * chip + core, 2 * chip + 1 - core]

        self.width, self.table = {}, []
        for device in range(members):
            core, row = device % 2, []

            def put(name, values):
                self.width[name] = (len(row), len(values))
                row.extend(values)

            for k in range(self.far + 1):
                one = k == self.far
                mine, other = halves(device, k, core), halves(device, -k, 1 - core)
                put(("keep", k), mine[:1] if one else mine)
                put(("give", k), [] if k == 0 else other[:1] if one else other)
                mine, other = halves(device, -k, core), halves(device, k, 1 - core)
                put(("use", k), mine if k == 0 else (mine[:1] + other[:1] if one else mine + other))
            put("core", [core])
            self.table.append(row)

    def first(self, weight, name, k):
        half = weight.shape[1] // (2 * self.chips)
        base, turns = self.width[name, k]
        return First(weight.shape[0], half, base, turns, name == "use")

    def calls(self):
        far = self.far
        calls = [[("keep", far), ("give", far), ("give", far - 1)]]
        for k in range(far - 1, 0, -1):
            calls.append([("keep", k), ("give", k - 1) if k > 1 else ("keep", 0)])
        return calls

    def row(self):
        table = jnp.asarray(np.array(self.table, np.int32))
        return lax.dynamic_index_in_dim(table, lax.axis_index("row"), 0, keepdims=False)


class First:
    def __init__(self, rows, half, base, turns, by_rows):
        self.half, self.base, self.turns, self.by_rows = half, base, turns, by_rows
        self.rows = rows
        cuts = 2 if turns == 2 else 4
        self.tall = -(-rows // (128 * cuts)) * 128 if by_rows and rows % 128 == 0 else rows
        self.shape = (self.tall, turns * half) if by_rows else (rows, half)

    def copies(self, ids_ref, weight_ref, target_ref, sems):
        if not self.by_rows:
            start = pl.multiple_of(ids_ref[self.base] * self.half, 128)
            source = weight_ref.at[:, pl.ds(start, self.half)]
            return [pltpu.make_async_copy(source, target_ref, sems.at[0])]
        return self.strips(ids_ref, weight_ref, 0, target_ref, sems)

    def strips(self, ids_ref, weight_ref, low, target_ref, sems):
        copies = []
        for turn in range(self.turns):
            start = pl.multiple_of(ids_ref[self.base + turn] * self.half, 128)
            source = weight_ref.at[pl.ds(low, min(self.tall, self.rows - low)), pl.ds(start, self.half)]
            target = target_ref.at[:, pl.ds(turn * self.half, self.half)]
            copies.append(pltpu.make_async_copy(source, target, sems.at[turn]))
        return copies


def in_turn(blocks, ahead, work, prepare=None):
    for block in blocks[: ahead + 1]:
        for copy in block:
            copy.start()
    if prepare is not None:
        prepare()
    for at, block in enumerate(blocks):
        for copy in block:
            copy.wait()
        if at > 0 and at + ahead < len(blocks):
            for copy in blocks[at + ahead]:
                copy.start()
        work(at)


def columns_kernel(half, entries, following, outs, carried, ids_ref, left_ref, weight_ref, *refs):
    refs = list(refs)
    sems, held_ref = refs.pop(), refs.pop()
    turns = len(entries)
    ready_ref = refs.pop(0) if carried else held_ref.at[turns - 1]
    next_ref = refs.pop()
    blocks = [[]] if carried else []
    for turn in range(len(blocks), turns):
        start = pl.multiple_of(ids_ref[entries[turn]] * half, 128)
        source = weight_ref.at[:, pl.ds(start, half)]
        target_ref = held_ref.at[turn - 1] if turn else ready_ref
        blocks.append([pltpu.make_async_copy(source, target_ref, sems.at[turn, 0])])
    blocks.append(following.copies(ids_ref, weight_ref, next_ref, sems.at[turns]))
    places = [(out, at) for out, count in enumerate(outs) for at in range(count)]

    def work(turn):
        if turn == turns:
            return
        block = held_ref[turn - 1] if turn else ready_ref[...]
        part = jnp.dot(left_ref[...], block, preferred_element_type=jnp.float32)
        out, at = places[turn]
        refs[out][:, at * half : (at + 1) * half] = part.astype(refs[out].dtype)

    in_turn(blocks, 2, work)


def column_sums(left, weight, ids, ring, groups, carry, following):
    rows, wide = left.shape[1], left.shape[0]
    half = weight.shape[1] // (2 * ring.chips)
    entries, outs, out_shape = [], [], []
    for name, k in groups:
        base, count = ring.width[name, k]
        entries += range(base, base + count)
        outs.append(count)
        kind = jnp.float32 if name == "keep" else jnp.bfloat16
        out_shape.append(jax.ShapeDtypeStruct((wide, count * half), kind))
    turns = len(entries)
    out_shape.append(jax.ShapeDtypeStruct(following.shape, jnp.bfloat16))
    whole = pl.BlockSpec(memory_space=pltpu.VMEM)
    carried = carry is not None
    return pl.pallas_call(
        functools.partial(columns_kernel, half, entries, following, outs, carried),
        out_shape=out_shape,
        in_specs=[
            pl.BlockSpec(memory_space=pltpu.SMEM),
            whole,
            pl.BlockSpec(memory_space=pl.ANY),
        ]
        + [whole] * carried,
        out_specs=[whole] * len(out_shape),
        scratch_shapes=[
            pltpu.VMEM((turns - carried, rows, half), jnp.bfloat16),
            pltpu.SemaphoreType.DMA((turns + 1, 4)),
        ],
        compiler_params=pltpu.CompilerParams(
            vmem_limit_bytes=2 * (turns - carried) * rows * half + SPARE
        ),
        cost_estimate=pl.CostEstimate(
            flops=2 * wide * rows * turns * half,
            bytes_accessed=2 * rows * turns * half + 2 * rows * wide,
            transcendentals=0,
        ),
    )(ids, left, weight, *([carry] if carried else []))


def invert_kernel(starts, first, *refs):
    refs = list(refs)
    lanes = lax.broadcasted_iota(jnp.int32, (8, 128), 1)
    if starts:
        gram_ref, work_ref, out_ref = refs
        size = work_ref.shape[0]
        total = gram_ref[0]
        for chip in range(1, gram_ref.shape[0]):
            total = total + gram_ref[chip]
        work_ref[...] = jnp.zeros_like(work_ref)
        work_ref[:, :size] = total
    else:
        before_ref, work_ref, out_ref = refs
        size = work_ref.shape[0]
        work_ref[...] = before_ref[...]
    side = first * PANEL // 128
    start = first * PANEL
    tall = size - start
    rows_at = start + lax.broadcasted_iota(jnp.int32, (tall, 128), 0)
    inside = lax.broadcasted_iota(jnp.int32, (PANEL, 128), 0)

    def packed(values):
        total = jnp.broadcast_to(values[0][:1], (PANEL, 128))
        for s in range(1, PANEL):
            total = jnp.where(inside == s, jnp.broadcast_to(values[s][:1], (PANEL, 128)), total)
        return total

    def panel(p, _):
        here = pl.ds(pl.multiple_of(PANEL * p, PANEL), PANEL)
        raw = [work_ref[here, :128], work_ref[here, 128:]]
        low = PANEL * p - 128 * side
        entry, ratio, inverse = {}, {}, []
        for s in range(PANEL):
            at = jnp.full((PANEL, 128), low + s, jnp.int32)
            column = jnp.take_along_axis(raw[side], at, axis=1)
            for r in range(s + 1):
                entry[r, s] = jnp.broadcast_to(column[r : r + 1], (8, 128))
        for s in range(PANEL):
            inverse.append(pl.reciprocal(entry[s, s]))
            for t in range(s + 1, PANEL):
                ratio[t, s] = entry[s, t] * inverse[s]
            for t in range(s + 1, PANEL):
                for u in range(t, PANEL):
                    entry[t, u] = entry[t, u] - ratio[t, s] * entry[s, u]
        own = (lanes >= low) & (lanes < low + PANEL)
        row = []
        for t in range(PANEL):
            halves = [jnp.broadcast_to(part[t : t + 1], (8, 128)) for part in raw]
            unit = jnp.where(lanes == low + t, 1.0, 0.0)
            halves[side] = jnp.where(own, unit, halves[side])
            for s in range(t):
                halves = [half - ratio[t, s] * done for half, done in zip(halves, row[s])]
            row.append(halves)
        scale = lax.rsqrt(packed([entry[s, s] for s in range(PANEL)]))
        inverses = packed(inverse)
        factors = []
        for half in range(2):
            whole = packed([row[s][half] for s in range(PANEL)])
            beyond = lanes[:1] + 128 * half >= PANEL * p + PANEL
            strip = jnp.where(beyond, 0.0, whole * scale)
            place = pl.ds(pl.multiple_of(PANEL * (p - first), PANEL), PANEL)
            out_ref[place, 128 * half : min(128 * half + 128, size)] = strip[
                :, : min(128, size - 128 * half)
            ]
            factors.append(jnp.where(beyond, whole * inverses, 0.0).T)
        factor = jnp.concatenate(factors, 0)[start:size]
        spread = lambda x: jnp.tile(x, (tall // 8, 1))
        after = rows_at >= PANEL * p + PANEL
        for half in range(2):
            place = (slice(start, size), slice(128 * half, 128 * half + 128))
            rest = work_ref[place]
            if half == side:
                rest = jnp.where(spread(own) & after, 0.0, rest)
            for s in range(PANEL):
                rest = rest - jnp.broadcast_to(factor[:, s : s + 1], (tall, 128)) * spread(row[s][half])
            work_ref[place] = rest
        return 0

    lax.fori_loop(first, first + out_ref.shape[0] // PANEL, panel, 0)


def invert_panels(first, size, source):
    tall = min(4 * PANEL, size - PANEL * first)
    whole = pl.BlockSpec(memory_space=pltpu.VMEM)
    return pl.pallas_call(
        functools.partial(invert_kernel, first == 0, first),
        out_shape=[
            jax.ShapeDtypeStruct((size, 256), jnp.float32),
            jax.ShapeDtypeStruct((tall, size), jnp.float32),
        ],
        in_specs=[whole],
        out_specs=[whole] * 2,
        input_output_aliases={0: 0} if first else {},
        compiler_params=pltpu.CompilerParams(vmem_limit_bytes=SPARE),
        cost_estimate=pl.CostEstimate(flops=10**9, bytes_accessed=2 * 10**7, transcendentals=0),
    )(source)


def rows_kernel(first, following, pieces, spans, chained, turned, grams, ids_ref, weight_ref, *refs):
    refs = list(refs)
    ready_ref = refs.pop(0)
    piece_refs = [refs.pop(0) for _ in range(pieces)]
    before_ref = refs.pop(0) if chained else None
    if grams and chained:
        refs.pop(0)
    out_ref = refs.pop(0)
    gram_ref = refs.pop(0) if grams else None
    next_ref = refs.pop(0) if following is not None else None
    held_ref, joined_ref, sems = refs
    half, turns = first.half, first.turns
    halves = turns // pieces
    blocks = [[]]
    for number, (low, tall) in enumerate(spans[1:], 1):
        target_ref = held_ref.at[pl.ds(low - first.tall, tall)]
        blocks.append(first.strips(ids_ref, weight_ref, low, target_ref, sems.at[number]))
    if following is not None:
        blocks.append(following.copies(ids_ref, weight_ref, next_ref, sems.at[0]))

    def piece(turn):
        at = turn % halves * half
        return piece_refs[turn // halves][:, at : at + half]

    def prepare():
        for turn in range(turns):
            upright = piece(turn).astype(jnp.float32).T.astype(jnp.bfloat16)
            joined_ref[turn * half : (turn + 1) * half, :] = upright

    def work(number):
        if number == len(spans):
            return
        low, tall = spans[number]
        block_ref, at = (held_ref, low - first.tall) if number else (ready_ref, 0)
        parts = [
            jnp.dot(
                block_ref[at + side * tall // 2 : at + (side + 1) * tall // 2, :],
                joined_ref[...],
                preferred_element_type=jnp.float32,
            )
            for side in range(2)
        ]
        for side, part in enumerate(parts):
            place = (slice(low + side * tall // 2, low + (side + 1) * tall // 2), slice(None))
            parts[side] = before_ref[place] + part if chained else part
            if not turned:
                out_ref[place] = parts[side]
        if turned:
            out_ref[:, low : low + tall] = jnp.concatenate(parts, 0).T.astype(out_ref.dtype)
        number += turns == 2
        if grams and 0 < number <= turns // 2:
            squares = [
                jnp.dot(
                    piece(turn),
                    joined_ref[turn * half : (turn + 1) * half, :],
                    preferred_element_type=jnp.float32,
                )
                for turn in range(2 * number - 2, 2 * number)
            ]
            gram_ref[ids_ref[first.base + 2 * number - 2] // 2] = squares[0] + squares[1]

    in_turn(blocks, 2, work, prepare)


def row_products(weight, pieces, ids, first, before, turned, grams, carry, following):
    rows, wide = weight.shape[0], pieces[0].shape[0]
    turns, half = first.turns, first.half
    chips = weight.shape[1] // (2 * half)
    spans = [(low, min(first.tall, rows - low)) for low in range(0, rows, first.tall)]
    whole = pl.BlockSpec(memory_space=pltpu.VMEM)
    operands = [ids, weight, carry, *pieces]
    in_specs = [pl.BlockSpec(memory_space=pltpu.SMEM), pl.BlockSpec(memory_space=pl.ANY), whole]
    in_specs += [whole] * len(pieces)
    kind = jnp.bfloat16 if turned and grams is None else jnp.float32
    out_shape = [jax.ShapeDtypeStruct((wide, rows) if turned else (rows, wide), kind)]
    aliases = {}
    if before is not None:
        if not turned:
            aliases[len(operands)] = 0
        operands.append(before)
        in_specs.append(whole)
    if grams is not None:
        if before is not None:
            aliases[len(operands)] = 1
            operands.append(grams)
            in_specs.append(whole)
        out_shape.append(jax.ShapeDtypeStruct((chips, wide, wide), jnp.float32))
    if following is not None:
        out_shape.append(jax.ShapeDtypeStruct(following.shape, jnp.bfloat16))
    depth = turns * half
    return pl.pallas_call(
        functools.partial(
            rows_kernel,
            first,
            following,
            len(pieces),
            spans,
            before is not None,
            turned,
            grams is not None,
        ),
        out_shape=out_shape,
        in_specs=in_specs,
        out_specs=[whole] * len(out_shape),
        scratch_shapes=[
            pltpu.VMEM((max(rows - first.tall, 16), depth), jnp.bfloat16),
            pltpu.VMEM((depth, wide), jnp.bfloat16),
            pltpu.SemaphoreType.DMA((len(spans) + 1, 4)),
        ],
        input_output_aliases=aliases,
        compiler_params=pltpu.CompilerParams(
            vmem_limit_bytes=2 * depth * (rows - first.tall + 256) + SPARE
        ),
        cost_estimate=pl.CostEstimate(
            flops=2 * rows * wide * turns * half,
            bytes_accessed=2 * rows * turns * half + 8 * rows * wide,
            transcendentals=0,
        ),
    )(*operands)


def ring_sum(ring, ids, left, weight, half, carry):
    calls = ring.calls()
    got, parts = None, {}
    for number, groups in enumerate(calls):
        k = ring.far - number
        if number:
            left, parts["give", k] = lax.optimization_barrier((left, parts["give", k]))
        if number + 1 < len(calls):
            following = ring.first(weight, *calls[number + 1][0])
        else:
            following = ring.first(weight, "use", 0)
        *outs, carry = column_sums(left, weight, ids, ring, groups, carry, following)
        for (name, at), out in zip(groups, outs):
            parts[name, at] = lax.ppermute(out, "row", ring.pair) if name == "give" else out
        keep, given = parts["keep", k], parts["give", k]
        if got is not None:
            got = got.astype(jnp.float32)
            size = got.shape[1]
            if size < keep.shape[1]:
                keep = jnp.concatenate([keep[:, :size] + got, keep[:, size:]], 1)
            else:
                keep = keep + got
            keep, given = lax.optimization_barrier((keep, given))
        total = (keep + given.astype(jnp.float32)).astype(jnp.bfloat16)
        total, left = lax.optimization_barrier((total, left))
        got = lax.ppermute(total, "row", ring.ahead)
    keep = parts["keep", 0]
    swap = lambda x: jnp.concatenate([x[:, half:], x[:, :half]], 1)
    own = keep + swap(lax.ppermute(keep, "row", ring.pair))
    own, got = lax.optimization_barrier((own, got))
    other = swap(lax.ppermute(got, "row", ring.pair))
    return own + (got.astype(jnp.float32) + other.astype(jnp.float32)), carry


def ring_apply(ring, ids, chunk, weight, half, with_grams, carry, following):
    before, grams = None, () if with_grams else None
    moving = chunk
    for k in range(ring.far + 1):
        if k == 0:
            pieces = [chunk]
        else:
            moving = lax.ppermute(moving if k < ring.far else moving[:, :half], "row", ring.ahead)
            moving, before = lax.optimization_barrier((moving, before))
            pieces = [moving, lax.ppermute(moving, "row", ring.pair)]
        last = k == ring.far
        then = following if last else ring.first(weight, "use", k + 1)
        first = ring.first(weight, "use", k)
        outs = list(
            row_products(
                weight, pieces, ids, first, before, last, grams, carry, then
            )
        )
        carry = outs.pop() if then is not None else None
        before = outs.pop(0)
        grams = outs.pop() if outs else None
    return before, grams, carry


def sum_beside_inverse(value, ring, ids, grams):
    size = value.shape[0]
    rows = size // 2
    core = ring.width["core"][0]
    first = ids[core : core + 1, None] == 0
    at, to = (lax.broadcasted_iota(jnp.int32, (rows, rows), axis) for axis in range(2))
    top, corner, bottom = value[:rows, :rows], value[:rows, rows:], value[rows:, rows:]
    diagonal = jnp.sum(jnp.where(at == to, bottom, 0.0), axis=0, keepdims=True)
    low = jnp.concatenate([corner, jnp.zeros_like(diagonal)], 0)
    high = jnp.concatenate([jnp.where(at <= to, top, bottom), diagonal], 0)
    part = jnp.where(first, low, high)
    part = part + lax.ppermute(jnp.where(first, high, low), "row", ring.pair)
    hops = [
        [(device, device ^ (2 << bit)) for device in range(2 * ring.chips)]
        for bit in reversed(range(ring.chips.bit_length() - 1))
    ]
    panels = list(range(0, size // PANEL, 4))
    work, strips = grams, []
    for turn in range(max(len(hops), len(panels))):
        if turn < len(hops):
            got = lax.ppermute(part, "row", hops[turn])
        if turn < len(panels):
            work, strip = invert_panels(panels[turn], size, work)
            strips.append(strip)
        if turn < len(hops):
            got, work = lax.optimization_barrier((got, work))
            part = part + got
    other = lax.ppermute(part, "row", ring.pair)
    low, high = jnp.where(first, part, other), jnp.where(first, other, part)
    mixed, diagonal = high[:rows], high[rows:]
    top = jnp.where(at < to, 2.0 * mixed, jnp.where(at == to, mixed, 0.0))
    bottom = jnp.where(at > to, 2.0 * mixed, jnp.where(at == to, diagonal, 0.0))
    top = jnp.concatenate([top, 2.0 * low[:rows]], 1)
    bottom = jnp.concatenate([jnp.zeros_like(bottom), bottom], 1)
    return jnp.concatenate([top, bottom], 0), strips


def finish_kernel(strips, count, scale, *refs):
    strip_refs = refs[:strips]
    pick_ref, square_ref, own_ref, image_ref = refs[strips : strips + 4]
    left_ref, right_ref, spread_ref, inverse_ref = refs[strips + 4 :]

    def halves(value):
        high = value.astype(jnp.bfloat16)
        return high, (value - high.astype(jnp.float32)).astype(jnp.bfloat16)

    def product(a, b):
        return jnp.dot(a, b, preferred_element_type=jnp.float32)

    def close(a, b):
        return product(a[0], b[0]) + (product(a[0], b[1]) + product(a[1], b[0]))

    low = 0
    for strip_ref in strip_refs:
        inverse_ref[low : low + strip_ref.shape[0], :] = strip_ref[...]
        low += strip_ref.shape[0]
    pick = pick_ref[...].astype(jnp.bfloat16)
    inverse = inverse_ref[...]
    high, rest = halves(inverse)
    low = (inverse - high.astype(jnp.float32) - rest.astype(jnp.float32)).astype(jnp.bfloat16)
    change = product(pick, high) + (product(pick, rest) + product(pick, low))
    parts = halves(change)
    energy = jnp.sum(change * close(parts, halves(square_ref[...])), axis=1, keepdims=True)
    spread = jnp.sqrt(jnp.sum(energy, axis=0, keepdims=True) / count + 1e-06)
    spread_ref[...] = spread
    left_ref[...] = close(parts, halves(own_ref[...])) * scale
    parts = halves(change / spread)
    rows = image_ref.shape[1]
    for at in range(0, rows, 512):
        place = (slice(None), slice(at, min(at + 512, rows)))
        right_ref[place] = close(parts, halves(image_ref[place])).astype(jnp.bfloat16)


def finish(strips, pick, square, own, image, count, scale):
    kept, size = pick.shape
    whole = pl.BlockSpec(memory_space=pltpu.VMEM)
    operands = [*strips, pick, square, own, image]
    return pl.pallas_call(
        functools.partial(finish_kernel, len(strips), count, scale),
        out_shape=[
            jax.ShapeDtypeStruct((kept, own.shape[1]), jnp.float32),
            jax.ShapeDtypeStruct((kept, image.shape[1]), jnp.bfloat16),
            jax.ShapeDtypeStruct((1, 1), jnp.float32),
        ],
        in_specs=[whole] * len(operands),
        out_specs=[whole] * 3,
        scratch_shapes=[pltpu.VMEM((size, size), jnp.float32)],
        compiler_params=pltpu.CompilerParams(vmem_limit_bytes=2 * SPARE),
    )(*operands)


def ring_body(ring, weight, test_matrix, rank_mask):
    rows, features = weight.shape
    half = features // (2 * ring.chips)
    ids = ring.row()
    pick = selector(rank_mask, RANK).T
    sketch, carry = ring_sum(ring, ids, test_matrix.T, weight, half, None)
    sketch = sketch.astype(jnp.bfloat16)
    again = ring.first(weight, "keep", ring.far)
    mixed, _, carry = ring_apply(ring, ids, sketch, weight, half, False, carry, again)
    powered, carry = ring_sum(ring, ids, mixed, weight, half, carry)
    powered_b = powered.astype(jnp.bfloat16)
    image, grams, _ = ring_apply(ring, ids, powered_b, weight, half, True, carry, None)
    image_b = image.astype(jnp.bfloat16)
    square = lax.dot_general(
        image_b, image_b, (((1,), (1,)), ((), ())), preferred_element_type=jnp.float32
    )
    square, strips = sum_beside_inverse(square, ring, ids, grams)
    own = powered[:, :half]
    count = rows * 2 * ring.chips * RANK
    left_factor, right_factor, spread = finish(
        strips, pick, square, own, image, count, math.sqrt(features)
    )
    return (left_factor.T, right_factor.T, spread.reshape(1))


def body(weight, test_matrix, rank_mask):
    members = lax.axis_size("row")
    chips = members // 2
    paired = members % 2 == 0 and chips > 2 and chips & (chips - 1) == 0
    if not paired or weight.shape[1] % (members * 128):
        return plain_body(weight, test_matrix, rank_mask)
    return ring_body(Ring(members), weight, test_matrix, rank_mask)


def solution(mesh):
    in_specs = (P(("groups", "row"), None), P("row", None), P("groups"))
    out_specs = (P(("groups", "row"), None), P(("groups", "row"), None), P("groups"))
    return jax.shard_map(body, mesh=mesh, in_specs=in_specs, out_specs=out_specs, check_vma=False)
```

```python
import functools
import math

import jax
import jax.numpy as jnp
import numpy as np
from jax import lax
from jax.experimental import pallas as pl
from jax.experimental.pallas import tpu as pltpu
from jax.sharding import PartitionSpec as P

RANK = 224
PANEL = 16
SPARE = 4 * 1024 * 1024


def selector(rank_mask, kept):
    at = lax.iota(jnp.int32, rank_mask.shape[0])
    positions = jnp.sum(jnp.where(at[:, None] <= at[None, :], rank_mask[:, None], 0), axis=0) - 1
    targets = lax.iota(jnp.int32, kept)
    matches = (rank_mask[:, None] == 1) & (positions[:, None] == targets[None, :])
    return matches.astype(jnp.float32)


def plain_body(weight, test_matrix, rank_mask):
    across = (((0,), (0,)), ((), ()))
    members = lax.axis_size("row")
    picker = selector(rank_mask, RANK)
    sketch_part = lax.psum_scatter(
        lax.dot_general(weight, test_matrix, across, preferred_element_type=jnp.float32),
        "row",
        scatter_dimension=0,
        tiled=True,
    ).astype(jnp.bfloat16)

    def add_rows(piece_rows):
        return jnp.dot(weight, piece_rows, preferred_element_type=jnp.float32)

    mixed = add_rows(lax.all_gather(sketch_part, "row", axis=0, tiled=True)).astype(jnp.bfloat16)
    powered = lax.psum_scatter(
        lax.dot_general(weight, mixed, across, preferred_element_type=jnp.float32),
        "row",
        scatter_dimension=0,
        tiled=True,
    )
    local_gram = lax.dot_general(powered, powered, across, precision=lax.Precision.HIGHEST)
    gram_matrix = lax.psum(local_gram, "row")
    cholesky_factor = jnp.linalg.cholesky(gram_matrix)
    ortho_basis = lax.linalg.triangular_solve(
        cholesky_factor, powered, left_side=False, lower=True, transpose_a=True
    )
    own_chosen = jnp.dot(ortho_basis, picker, precision=lax.Precision.HIGHEST)
    projected = add_rows(lax.all_gather(own_chosen.astype(jnp.bfloat16), "row", axis=0, tiled=True))
    left_factor = own_chosen * math.sqrt(weight.shape[1])
    energy = lax.psum(jnp.sum(projected * projected), "row")
    spread = jnp.sqrt(energy / (weight.shape[0] * members * RANK) + 1e-06)
    right_factor = (projected / spread).astype(jnp.bfloat16)
    return (left_factor, right_factor, spread.reshape(1))


class Ring:
    def __init__(self, members):
        chips = members // 2
        order = list(range(0, chips, 2)) + list(range(chips - 1, 0, -2))
        place = {chip: at for at, chip in enumerate(order)}
        self.chips, self.far = chips, chips // 2
        self.pair = [(device, device ^ 1) for device in range(members)]
        self.ahead = []
        for at, chip in enumerate(order):
            self.ahead.append((2 * chip, 2 * order[(at + 1) % chips]))
            self.ahead.append((2 * chip + 1, 2 * order[at - 1] + 1))

        def halves(device, steps, core):
            at = place[device // 2] + (steps if device % 2 == 0 else -steps)
            chip = order[at % chips]
            return [2 * chip + core, 2 * chip + 1 - core]

        self.width, self.table = {}, []
        for device in range(members):
            core, row = device % 2, []

            def put(name, values):
                self.width[name] = (len(row), len(values))
                row.extend(values)

            for k in range(self.far + 1):
                one = k == self.far
                mine, other = halves(device, k, core), halves(device, -k, 1 - core)
                put(("keep", k), mine[:1] if one else mine)
                put(("give", k), [] if k == 0 else other[:1] if one else other)
                mine, other = halves(device, -k, core), halves(device, k, 1 - core)
                put(("use", k), mine if k == 0 else (mine[:1] + other[:1] if one else mine + other))
            put("core", [core])
            self.table.append(row)

    def first(self, weight, name, k):
        half = weight.shape[1] // (2 * self.chips)
        base, turns = self.width[name, k]
        return First(weight.shape[0], half, base, turns, name == "use")

    def calls(self):
        far = self.far
        calls = [[("keep", far), ("give", far)], [("give", far - 1)]]
        for k in range(far - 1, 0, -1):
            calls.append([("keep", k), ("give", k - 1) if k > 1 else ("keep", 0)])
        return calls

    def row(self):
        table = jnp.asarray(np.array(self.table, np.int32))
        return lax.dynamic_index_in_dim(table, lax.axis_index("row"), 0, keepdims=False)


class First:
    def __init__(self, rows, half, base, turns, by_rows):
        self.half, self.base, self.turns, self.by_rows = half, base, turns, by_rows
        self.rows = rows
        cuts = 2 if turns == 2 else 4
        self.tall = -(-rows // (128 * cuts)) * 128 if by_rows and rows % 128 == 0 else rows
        self.shape = (self.tall, turns * half) if by_rows else (rows, half)

    def copies(self, ids_ref, weight_ref, target_ref, sems):
        if not self.by_rows:
            start = pl.multiple_of(ids_ref[self.base] * self.half, 128)
            source = weight_ref.at[:, pl.ds(start, self.half)]
            return [pltpu.make_async_copy(source, target_ref, sems.at[0])]
        return self.strips(ids_ref, weight_ref, 0, target_ref, sems)

    def strips(self, ids_ref, weight_ref, low, target_ref, sems):
        copies = []
        for turn in range(self.turns):
            start = pl.multiple_of(ids_ref[self.base + turn] * self.half, 128)
            source = weight_ref.at[pl.ds(low, min(self.tall, self.rows - low)), pl.ds(start, self.half)]
            target = target_ref.at[:, pl.ds(turn * self.half, self.half)]
            copies.append(pltpu.make_async_copy(source, target, sems.at[turn]))
        return copies


def in_turn(blocks, ahead, work, prepare=None):
    for block in blocks[: ahead + 1]:
        for copy in block:
            copy.start()
    if prepare is not None:
        prepare()
    for at, block in enumerate(blocks):
        for copy in block:
            copy.wait()
        if at > 0 and at + ahead < len(blocks):
            for copy in blocks[at + ahead]:
                copy.start()
        work(at)


def columns_kernel(half, entries, following, outs, carried, ids_ref, left_ref, weight_ref, *refs):
    refs = list(refs)
    sems, held_ref = refs.pop(), refs.pop()
    turns = len(entries)
    ready_ref = refs.pop(0) if carried else held_ref.at[turns - 1]
    next_ref = refs.pop()
    blocks = [[]] if carried else []
    for turn in range(len(blocks), turns):
        start = pl.multiple_of(ids_ref[entries[turn]] * half, 128)
        source = weight_ref.at[:, pl.ds(start, half)]
        target_ref = held_ref.at[turn - 1] if turn else ready_ref
        blocks.append([pltpu.make_async_copy(source, target_ref, sems.at[turn, 0])])
    blocks.append(following.copies(ids_ref, weight_ref, next_ref, sems.at[turns]))
    places = [(out, at) for out, count in enumerate(outs) for at in range(count)]

    def work(turn):
        if turn == turns:
            return
        block = held_ref[turn - 1] if turn else ready_ref[...]
        part = jnp.dot(left_ref[...], block, preferred_element_type=jnp.float32)
        out, at = places[turn]
        refs[out][:, at * half : (at + 1) * half] = part.astype(refs[out].dtype)

    in_turn(blocks, 2, work)


def column_sums(left, weight, ids, ring, groups, carry, following):
    rows, wide = left.shape[1], left.shape[0]
    half = weight.shape[1] // (2 * ring.chips)
    entries, outs, out_shape = [], [], []
    for name, k in groups:
        base, count = ring.width[name, k]
        entries += range(base, base + count)
        outs.append(count)
        kind = jnp.float32 if name == "keep" else jnp.bfloat16
        out_shape.append(jax.ShapeDtypeStruct((wide, count * half), kind))
    turns = len(entries)
    out_shape.append(jax.ShapeDtypeStruct(following.shape, jnp.bfloat16))
    whole = pl.BlockSpec(memory_space=pltpu.VMEM)
    carried = carry is not None
    return pl.pallas_call(
        functools.partial(columns_kernel, half, entries, following, outs, carried),
        out_shape=out_shape,
        in_specs=[
            pl.BlockSpec(memory_space=pltpu.SMEM),
            whole,
            pl.BlockSpec(memory_space=pl.ANY),
        ]
        + [whole] * carried,
        out_specs=[whole] * len(out_shape),
        scratch_shapes=[
            pltpu.VMEM((turns - carried, rows, half), jnp.bfloat16),
            pltpu.SemaphoreType.DMA((turns + 1, 4)),
        ],
        compiler_params=pltpu.CompilerParams(
            vmem_limit_bytes=2 * (turns - carried) * rows * half + SPARE
        ),
        cost_estimate=pl.CostEstimate(
            flops=2 * wide * rows * turns * half,
            bytes_accessed=2 * rows * turns * half + 2 * rows * wide,
            transcendentals=0,
        ),
    )(ids, left, weight, *([carry] if carried else []))


def invert_kernel(starts, first, *refs):
    refs = list(refs)
    lanes = lax.broadcasted_iota(jnp.int32, (8, 128), 1)
    if starts:
        gram_ref, work_ref, out_ref = refs
        size = work_ref.shape[0]
        total = gram_ref[0]
        for chip in range(1, gram_ref.shape[0]):
            total = total + gram_ref[chip]
        work_ref[...] = jnp.zeros_like(work_ref)
        work_ref[:, :size] = total
    else:
        before_ref, work_ref, out_ref = refs
        size = work_ref.shape[0]
        work_ref[...] = before_ref[...]
    side = first * PANEL // 128
    start = first * PANEL
    tall = size - start
    rows_at = start + lax.broadcasted_iota(jnp.int32, (tall, 128), 0)
    inside = lax.broadcasted_iota(jnp.int32, (PANEL, 128), 0)

    def packed(values):
        total = jnp.broadcast_to(values[0][:1], (PANEL, 128))
        for s in range(1, PANEL):
            total = jnp.where(inside == s, jnp.broadcast_to(values[s][:1], (PANEL, 128)), total)
        return total

    def panel(p, _):
        here = pl.ds(pl.multiple_of(PANEL * p, PANEL), PANEL)
        raw = [work_ref[here, :128], work_ref[here, 128:]]
        low = PANEL * p - 128 * side
        entry, ratio, inverse = {}, {}, []
        for s in range(PANEL):
            at = jnp.full((PANEL, 128), low + s, jnp.int32)
            column = jnp.take_along_axis(raw[side], at, axis=1)
            for r in range(s + 1):
                entry[r, s] = jnp.broadcast_to(column[r : r + 1], (8, 128))
        for s in range(PANEL):
            inverse.append(pl.reciprocal(entry[s, s]))
            for t in range(s + 1, PANEL):
                ratio[t, s] = entry[s, t] * inverse[s]
            for t in range(s + 1, PANEL):
                for u in range(t, PANEL):
                    entry[t, u] = entry[t, u] - ratio[t, s] * entry[s, u]
        own = (lanes >= low) & (lanes < low + PANEL)
        row = []
        for t in range(PANEL):
            halves = [jnp.broadcast_to(part[t : t + 1], (8, 128)) for part in raw]
            unit = jnp.where(lanes == low + t, 1.0, 0.0)
            halves[side] = jnp.where(own, unit, halves[side])
            for s in range(t):
                halves = [half - ratio[t, s] * done for half, done in zip(halves, row[s])]
            row.append(halves)
        scale = lax.rsqrt(packed([entry[s, s] for s in range(PANEL)]))
        inverses = packed(inverse)
        factors = []
        for half in range(2):
            whole = packed([row[s][half] for s in range(PANEL)])
            beyond = lanes[:1] + 128 * half >= PANEL * p + PANEL
            strip = jnp.where(beyond, 0.0, whole * scale)
            place = pl.ds(pl.multiple_of(PANEL * (p - first), PANEL), PANEL)
            out_ref[place, 128 * half : min(128 * half + 128, size)] = strip[
                :, : min(128, size - 128 * half)
            ]
            factors.append(jnp.where(beyond, whole * inverses, 0.0).T)
        factor = jnp.concatenate(factors, 0)[start:size]
        spread = lambda x: jnp.tile(x, (tall // 8, 1))
        after = rows_at >= PANEL * p + PANEL
        for half in range(2):
            place = (slice(start, size), slice(128 * half, 128 * half + 128))
            rest = work_ref[place]
            if half == side:
                rest = jnp.where(spread(own) & after, 0.0, rest)
            for s in range(PANEL):
                rest = rest - jnp.broadcast_to(factor[:, s : s + 1], (tall, 128)) * spread(row[s][half])
            work_ref[place] = rest
        return 0

    lax.fori_loop(first, first + out_ref.shape[0] // PANEL, panel, 0)


def invert_panels(first, size, source):
    tall = min(4 * PANEL, size - PANEL * first)
    whole = pl.BlockSpec(memory_space=pltpu.VMEM)
    return pl.pallas_call(
        functools.partial(invert_kernel, first == 0, first),
        out_shape=[
            jax.ShapeDtypeStruct((size, 256), jnp.float32),
            jax.ShapeDtypeStruct((tall, size), jnp.float32),
        ],
        in_specs=[whole],
        out_specs=[whole] * 2,
        input_output_aliases={0: 0} if first else {},
        compiler_params=pltpu.CompilerParams(vmem_limit_bytes=SPARE),
        cost_estimate=pl.CostEstimate(flops=10**9, bytes_accessed=2 * 10**7, transcendentals=0),
    )(source)


def rows_kernel(first, following, pieces, spans, chained, turned, grams, ids_ref, weight_ref, *refs):
    refs = list(refs)
    ready_ref = refs.pop(0)
    piece_refs = [refs.pop(0) for _ in range(pieces)]
    before_ref = refs.pop(0) if chained else None
    if grams and chained:
        refs.pop(0)
    out_ref = refs.pop(0)
    gram_ref = refs.pop(0) if grams else None
    next_ref = refs.pop(0) if following is not None else None
    held_ref, joined_ref, sems = refs
    half, turns = first.half, first.turns
    halves = turns // pieces
    blocks = [[]]
    for number, (low, tall) in enumerate(spans[1:], 1):
        target_ref = held_ref.at[pl.ds(low - first.tall, tall)]
        blocks.append(first.strips(ids_ref, weight_ref, low, target_ref, sems.at[number]))
    if following is not None:
        blocks.append(following.copies(ids_ref, weight_ref, next_ref, sems.at[0]))

    def piece(turn):
        at = turn % halves * half
        return piece_refs[turn // halves][:, at : at + half]

    def prepare():
        for turn in range(turns):
            upright = piece(turn).astype(jnp.float32).T.astype(jnp.bfloat16)
            joined_ref[turn * half : (turn + 1) * half, :] = upright

    def work(number):
        if number == len(spans):
            return
        low, tall = spans[number]
        block_ref, at = (held_ref, low - first.tall) if number else (ready_ref, 0)
        parts = [
            jnp.dot(
                block_ref[at + side * tall // 2 : at + (side + 1) * tall // 2, :],
                joined_ref[...],
                preferred_element_type=jnp.float32,
            )
            for side in range(2)
        ]
        for side, part in enumerate(parts):
            place = (slice(low + side * tall // 2, low + (side + 1) * tall // 2), slice(None))
            parts[side] = before_ref[place] + part if chained else part
            if not turned:
                out_ref[place] = parts[side]
        if turned:
            out_ref[:, low : low + tall] = jnp.concatenate(parts, 0).T.astype(out_ref.dtype)
        number += turns == 2
        if grams and 0 < number <= turns // 2:
            squares = [
                jnp.dot(
                    piece(turn),
                    joined_ref[turn * half : (turn + 1) * half, :],
                    preferred_element_type=jnp.float32,
                )
                for turn in range(2 * number - 2, 2 * number)
            ]
            gram_ref[ids_ref[first.base + 2 * number - 2] // 2] = squares[0] + squares[1]

    in_turn(blocks, 2, work, prepare)


def row_products(weight, pieces, ids, first, before, turned, grams, carry, following):
    rows, wide = weight.shape[0], pieces[0].shape[0]
    turns, half = first.turns, first.half
    chips = weight.shape[1] // (2 * half)
    spans = [(low, min(first.tall, rows - low)) for low in range(0, rows, first.tall)]
    whole = pl.BlockSpec(memory_space=pltpu.VMEM)
    operands = [ids, weight, carry, *pieces]
    in_specs = [pl.BlockSpec(memory_space=pltpu.SMEM), pl.BlockSpec(memory_space=pl.ANY), whole]
    in_specs += [whole] * len(pieces)
    kind = jnp.bfloat16 if turned and grams is None else jnp.float32
    out_shape = [jax.ShapeDtypeStruct((wide, rows) if turned else (rows, wide), kind)]
    aliases = {}
    if before is not None:
        if not turned:
            aliases[len(operands)] = 0
        operands.append(before)
        in_specs.append(whole)
    if grams is not None:
        if before is not None:
            aliases[len(operands)] = 1
            operands.append(grams)
            in_specs.append(whole)
        out_shape.append(jax.ShapeDtypeStruct((chips, wide, wide), jnp.float32))
    if following is not None:
        out_shape.append(jax.ShapeDtypeStruct(following.shape, jnp.bfloat16))
    depth = turns * half
    return pl.pallas_call(
        functools.partial(
            rows_kernel,
            first,
            following,
            len(pieces),
            spans,
            before is not None,
            turned,
            grams is not None,
        ),
        out_shape=out_shape,
        in_specs=in_specs,
        out_specs=[whole] * len(out_shape),
        scratch_shapes=[
            pltpu.VMEM((max(rows - first.tall, 16), depth), jnp.bfloat16),
            pltpu.VMEM((depth, wide), jnp.bfloat16),
            pltpu.SemaphoreType.DMA((len(spans) + 1, 4)),
        ],
        input_output_aliases=aliases,
        compiler_params=pltpu.CompilerParams(
            vmem_limit_bytes=2 * depth * (rows - first.tall + 256) + SPARE
        ),
        cost_estimate=pl.CostEstimate(
            flops=2 * rows * wide * turns * half,
            bytes_accessed=2 * rows * turns * half + 8 * rows * wide,
            transcendentals=0,
        ),
    )(*operands)


def ring_sum(ring, ids, left, weight, half, carry):
    calls = ring.calls()
    got, parts, free = None, {}, left
    for number, groups in enumerate(calls):
        k = ring.far - max(number - 1, 0)
        if number > 1:
            left, parts["give", k] = lax.optimization_barrier((left, parts["give", k]))
        if number + 1 < len(calls):
            following = ring.first(weight, *calls[number + 1][0])
        else:
            following = ring.first(weight, "use", 0)
        side = free if number == 1 else left
        *outs, carry = column_sums(side, weight, ids, ring, groups, carry, following)
        for (name, at), out in zip(groups, outs):
            parts[name, at] = lax.ppermute(out, "row", ring.pair) if name == "give" else out
        if number == 1:
            continue
        keep, given = parts["keep", k], parts["give", k]
        if got is not None:
            got = got.astype(jnp.float32)
            size = got.shape[1]
            if size < keep.shape[1]:
                keep = jnp.concatenate([keep[:, :size] + got, keep[:, size:]], 1)
            else:
                keep = keep + got
            keep, given = lax.optimization_barrier((keep, given))
        total = (keep + given.astype(jnp.float32)).astype(jnp.bfloat16)
        total, left = lax.optimization_barrier((total, left))
        got = lax.ppermute(total, "row", ring.ahead)
    keep = parts["keep", 0]
    swap = lambda x: jnp.concatenate([x[:, half:], x[:, :half]], 1)
    own = keep + swap(lax.ppermute(keep, "row", ring.pair))
    own, got = lax.optimization_barrier((own, got))
    other = swap(lax.ppermute(got, "row", ring.pair))
    return own + (got.astype(jnp.float32) + other.astype(jnp.float32)), carry


def ring_apply(ring, ids, chunk, weight, half, with_grams, carry, following):
    before, grams = None, () if with_grams else None
    moving = chunk
    for k in range(ring.far + 1):
        if k == 0:
            pieces = [chunk]
        else:
            moving = lax.ppermute(moving if k < ring.far else moving[:, :half], "row", ring.ahead)
            moving, before = lax.optimization_barrier((moving, before))
            pieces = [moving, lax.ppermute(moving, "row", ring.pair)]
        last = k == ring.far
        then = following if last else ring.first(weight, "use", k + 1)
        first = ring.first(weight, "use", k)
        outs = list(
            row_products(
                weight, pieces, ids, first, before, last, grams, carry, then
            )
        )
        carry = outs.pop() if then is not None else None
        before = outs.pop(0)
        grams = outs.pop() if outs else None
    return before, grams, carry


def sum_beside_inverse(value, ring, ids, grams):
    size = value.shape[0]
    rows = size // 2
    core = ring.width["core"][0]
    first = lax.broadcast_in_dim(ids[core : core + 1] == 0, (rows + 1, rows), (1,))
    at, to = (lax.broadcasted_iota(jnp.int32, (rows, rows), axis) for axis in range(2))
    top, corner, bottom = value[:rows, :rows], value[:rows, rows:], value[rows:, rows:]
    diagonal = jnp.sum(jnp.where(at == to, bottom, 0.0), axis=0, keepdims=True)
    low = jnp.concatenate([corner, jnp.zeros_like(diagonal)], 0)
    high = jnp.concatenate([jnp.where(at <= to, top, bottom), diagonal], 0)
    part = jnp.where(first, low, high)
    part = part + lax.ppermute(jnp.where(first, high, low), "row", ring.pair)
    hops = [
        [(device, device ^ (2 << bit)) for device in range(2 * ring.chips)]
        for bit in reversed(range(ring.chips.bit_length() - 1))
    ]
    panels = list(range(0, size // PANEL, 4))
    work, strips = grams, []
    for turn in range(max(len(hops), len(panels))):
        if turn < len(hops):
            got = lax.ppermute(part, "row", hops[turn])
        if turn < len(panels):
            work, strip = invert_panels(panels[turn], size, work)
            strips.append(strip)
        if turn < len(hops):
            got, work = lax.optimization_barrier((got, work))
            part = part + got
    other = lax.ppermute(part, "row", ring.pair)
    low, high = jnp.where(first, part, other), jnp.where(first, other, part)
    mixed, diagonal = high[:rows], high[rows:]
    top = jnp.where(at < to, 2.0 * mixed, jnp.where(at == to, mixed, 0.0))
    bottom = jnp.where(at > to, 2.0 * mixed, jnp.where(at == to, diagonal, 0.0))
    top = jnp.concatenate([top, 2.0 * low[:rows]], 1)
    bottom = jnp.concatenate([jnp.zeros_like(bottom), bottom], 1)
    return jnp.concatenate([top, bottom], 0), strips


def finish_kernel(strips, count, scale, *refs):
    strip_refs = refs[:strips]
    pick_ref, square_ref, own_ref, image_ref = refs[strips : strips + 4]
    left_ref, right_ref, spread_ref, inverse_ref = refs[strips + 4 :]

    def halves(value):
        high = value.astype(jnp.bfloat16)
        return high, (value - high.astype(jnp.float32)).astype(jnp.bfloat16)

    def product(a, b):
        return jnp.dot(a, b, preferred_element_type=jnp.float32)

    def close(a, b):
        return product(a[0], b[0]) + (product(a[0], b[1]) + product(a[1], b[0]))

    low = 0
    for strip_ref in strip_refs:
        inverse_ref[low : low + strip_ref.shape[0], :] = strip_ref[...]
        low += strip_ref.shape[0]
    pick = pick_ref[...].astype(jnp.bfloat16)
    inverse = inverse_ref[...]
    high, rest = halves(inverse)
    low = (inverse - high.astype(jnp.float32) - rest.astype(jnp.float32)).astype(jnp.bfloat16)
    change = product(pick, high) + (product(pick, rest) + product(pick, low))
    parts = halves(change)
    energy = jnp.sum(change * close(parts, halves(square_ref[...])), axis=1, keepdims=True)
    spread = jnp.sqrt(jnp.sum(energy, axis=0, keepdims=True) / count + 1e-06)
    spread_ref[...] = spread
    left_ref[...] = close(parts, halves(own_ref[...])) * scale
    parts = halves(change / spread)
    rows = image_ref.shape[1]
    for at in range(0, rows, 512):
        place = (slice(None), slice(at, min(at + 512, rows)))
        right_ref[place] = close(parts, halves(image_ref[place])).astype(jnp.bfloat16)


def finish(strips, pick, square, own, image, count, scale):
    kept, size = pick.shape
    whole = pl.BlockSpec(memory_space=pltpu.VMEM)
    operands = [*strips, pick, square, own, image]
    return pl.pallas_call(
        functools.partial(finish_kernel, len(strips), count, scale),
        out_shape=[
            jax.ShapeDtypeStruct((kept, own.shape[1]), jnp.float32),
            jax.ShapeDtypeStruct((kept, image.shape[1]), jnp.bfloat16),
            jax.ShapeDtypeStruct((1, 1), jnp.float32),
        ],
        in_specs=[whole] * len(operands),
        out_specs=[whole] * 3,
        scratch_shapes=[pltpu.VMEM((size, size), jnp.float32)],
        compiler_params=pltpu.CompilerParams(vmem_limit_bytes=2 * SPARE),
    )(*operands)


def ring_body(ring, weight, test_matrix, rank_mask):
    rows, features = weight.shape
    half = features // (2 * ring.chips)
    ids = ring.row()
    pick = selector(rank_mask, RANK).T
    sketch, carry = ring_sum(ring, ids, test_matrix.T, weight, half, None)
    sketch = sketch.astype(jnp.bfloat16)
    again = ring.first(weight, "keep", ring.far)
    mixed, _, carry = ring_apply(ring, ids, sketch, weight, half, False, carry, again)
    powered, carry = ring_sum(ring, ids, mixed, weight, half, carry)
    powered_b = powered.astype(jnp.bfloat16)
    image, grams, _ = ring_apply(ring, ids, powered_b, weight, half, True, carry, None)
    image_b = image.astype(jnp.bfloat16)
    square = lax.dot_general(
        image_b, image_b, (((1,), (1,)), ((), ())), preferred_element_type=jnp.float32
    )
    square, strips = sum_beside_inverse(square, ring, ids, grams)
    own = powered[:, :half]
    count = rows * 2 * ring.chips * RANK
    left_factor, right_factor, spread = finish(
        strips, pick, square, own, image, count, math.sqrt(features)
    )
    return (left_factor.T, right_factor.T, spread.reshape(1))


def body(weight, test_matrix, rank_mask):
    members = lax.axis_size("row")
    chips = members // 2
    paired = members % 2 == 0 and chips > 2 and chips & (chips - 1) == 0
    if not paired or weight.shape[1] % (members * 128):
        return plain_body(weight, test_matrix, rank_mask)
    return ring_body(Ring(members), weight, test_matrix, rank_mask)


def solution(mesh):
    in_specs = (P(("groups", "row"), None), P("row", None), P("groups"))
    out_specs = (P(("groups", "row"), None), P(("groups", "row"), None), P("groups"))
    return jax.shard_map(body, mesh=mesh, in_specs=in_specs, out_specs=out_specs, check_vma=False)
```
